32 devices in a mesh: section: 2 (over core), seq: 4 (over z), head: 4 (over y, x).
Axes of the slice: x: 2, y: 2, z: 4, core: 2. Of those that a mesh axis runs over, the one named last changes fastest.
Arguments:
- tokens: bfloat16 [2, 1024, 768], P(None, 'seq'), may hold values from -12 to 12
- cotangent: bfloat16 [2, 1024, 768], P(None, 'seq'), may hold values from -6 to 6
- lengths: int32 [2], replicated, may hold values from 256 to 1024, as said below
- clusters: int32 [2, 12, 1024], P(None, 'head', 'seq'), may hold values from 0 to 99, as said below
- top_index: int32 [2, 12, 100, 32], P(None, 'head'), may hold values from 0 to 1023, as said below
- w_qkv: bfloat16 [2, 3, 768, 768], P('section', None, None, 'head'), may hold values from -1 to 1
- w_out: bfloat16 [2, 768, 768], P('section', 'head'), may hold values from -0.21875 to 0.21875
- w_in: bfloat16 [2, 768, 3072], P('section', None, 'head'), may hold values from -0.21875 to 0.21875
- w_back: bfloat16 [2, 3072, 768], P('section', 'head'), may hold values from -0.109375 to 0.109375
- gains: bfloat16 [2, 2, 768], P('section'), may hold values from 0.099609375 to 1.8984375
Outputs:
- acts: float32 [2, 2, 1024, 768], P('section', None, 'seq')
- in_grads: float32 [2, 2, 1024, 768], P('section', None, 'seq')
- grad_qkv: float32 [2, 3, 768, 768], P('section', None, 'seq', 'head')
- grad_out: float32 [2, 768, 768], P('section', 'head', 'seq')
- grad_in: float32 [2, 768, 3072], P('section', 'seq', 'head')
- grad_back: float32 [2, 3072, 768], P('section', 'head', 'seq')
- grad_gains: float32 [2, 2, 768], P('section', None, 'seq')
The draws below stay inside these ranges and needn't reach their ends.
Inputs may be any that keep to these rules, and one draw needn't show every extreme that they name: `lengths`: one micro-batch, drawn from the seed, has length 1024. `clusters`: every cluster of every head has at least one member below its micro-batch's length. `top_index`: the 32 positions of a cluster are distinct and below its micro-batch's length. All clusters of all heads of one micro-batch name together exactly 64 distinct positions.
All inputs are finite; a program needn't handle non-finite values.
Results may differ from the reference program's by a relative error of at most 0.019.
Values may be sent and summed in bfloat16 or wider, within the bound.
No kernel may reach another device: no remote copies, remote signals or barrier semaphores. Data moves between devices by JAX's collectives and lax.ppermute only.
A program may use at most 192 MiB of HBM per device.

```python
import jax
import jax.numpy as jnp
from jax import lax

D = 768
H = 12
DH = 64
FF = 3072
C = 100
TOPK = 32
HUBS = 64
MB = 2
TOKENS = 1024
N_SECTION = 2


def shared_lengths(key):
    pick_key, len_key = jax.random.split(key)
    full_pick = jax.random.randint(pick_key, (), 0, MB)
    drawn_len = jax.random.randint(len_key, (MB,), TOKENS // 4, TOKENS + 1)
    return jnp.where(jnp.arange(MB) == full_pick, TOKENS, drawn_len).astype(jnp.int32)


def shared_hubs(key):
    seq_lengths = shared_lengths(key)
    hub_key = jax.random.fold_in(key, 23)
    key_list = jax.random.split(hub_key, MB)

    def one_batch(one_key, one_len):
        shuffled = jax.random.permutation(one_key, TOKENS).astype(jnp.int32)
        ranking = (shuffled >= one_len).astype(jnp.int32) * TOKENS + jnp.arange(TOKENS, dtype=jnp.int32)
        picked = jnp.argsort(ranking)[:HUBS]
        return shuffled[picked]
    return jax.vmap(one_batch)(key_list, seq_lengths).astype(jnp.int32)


def draw_lengths(key, part):
    return shared_lengths(key)


def draw_top_index(key, part):
    hub_rows = shared_hubs(key)
    key = jax.random.fold_in(key, 7)
    key_list = jax.random.split(key, MB * H * C)
    orders = jax.vmap(lambda one_key: jax.random.permutation(one_key, HUBS))(key_list).reshape(MB, H, C, HUBS).astype(jnp.int32)
    selected = orders[..., :TOPK]
    selected = selected.at[:, 0, 1].set(orders[:, 0, 0, TOPK:])
    spread_rows = jnp.broadcast_to(hub_rows[:, None, None, :], (MB, H, C, HUBS))
    return jnp.take_along_axis(spread_rows, selected, axis=3).astype(jnp.int32)


def draw_clusters(key, part):
    key = jax.random.fold_in(key, 11)
    base_key, perm_key = jax.random.split(key)
    assigned = jax.random.randint(base_key, (MB, H, TOKENS), 0, C)
    key_list = jax.random.split(perm_key, MB * H)
    firsts = jax.vmap(lambda one_key: jax.random.permutation(one_key, C))(key_list).reshape(MB, H, C)
    return assigned.at[:, :, :C].set(firsts).astype(jnp.int32)


def draw_tokens(key, part):
    hub_rows = shared_hubs(key)
    hub_flag = jnp.zeros((MB, TOKENS), jnp.float32).at[jnp.arange(MB, dtype=jnp.int32)[:, None], hub_rows].set(1.0)
    key = jax.random.fold_in(key, 5)
    mean_key, jitter_key = jax.random.split(key)
    common = jnp.clip(jax.random.normal(mean_key, (D,), jnp.float32), -2.5, 2.5)
    partner = jnp.roll(common, D // 2)
    drawn_scale = 1.5
    lifted = 3.0
    jitter_vals = jnp.clip(jax.random.normal(jitter_key, (MB, TOKENS, D), jnp.float32), -4.0, 4.0)
    flag_cols = hub_flag[..., None]
    blended = flag_cols * (lifted * partner)[None, None, :] + (1.0 - flag_cols) * (drawn_scale * common)[None, None, :]
    return (blended + jitter_vals).astype(jnp.bfloat16)


def draw_w_qkv(key, part):
    key = jax.random.fold_in(key, 13)
    query_key, own_key, value_key = jax.random.split(key, 3)
    shape_all = (N_SECTION, D, H * DH)
    query_part = jnp.clip(jax.random.normal(query_key, shape_all, jnp.float32), -4.0, 4.0)
    own_part = jnp.clip(jax.random.normal(own_key, shape_all, jnp.float32), -4.0, 4.0)
    value_part = jnp.clip(jax.random.normal(value_key, shape_all, jnp.float32), -4.0, 4.0)
    key_part = 0.8 * jnp.roll(query_part, D // 2, axis=1) + 0.6 * own_part
    stacked = jnp.stack([query_part, key_part, value_part], axis=1)
    return (stacked * D ** (-0.5)).astype(jnp.bfloat16)


def steps_of(key, extent, cuts, smallest, top_value):
    level = 1.0
    for axis_at, shards_of in cuts:
        steps = jax.random.uniform(jax.random.fold_in(jax.random.fold_in(key, 6), axis_at), (shards_of,), jnp.float32, smallest / len(cuts), top_value / len(cuts))
        level = level * jnp.repeat(jnp.exp(steps), extent[axis_at] // shards_of).reshape((-1,) + (1,) * (len(extent) - 1 - axis_at))
    return level


def noise(stream_key, dims, spread, reach, cuts=(), held_as=jnp.bfloat16):
    result = jax.random.normal(stream_key, dims, jnp.float32) * spread
    if len(cuts) > 0:
        result = steps_of(stream_key, dims, cuts, -0.22, 0.18) * result
    return jnp.clip(result, min=-reach, max=reach).astype(held_as)


def setup_inputs(seed: int = 0) -> dict:
    seeds = jax.random.split(jax.random.key(seed), 11)
    return {
        "tokens": draw_tokens(jax.random.fold_in(seeds[10], 71), 0),
        "cotangent": noise(seeds[1], (MB, TOKENS, D), 1.0, 6.0, ((1, 4),)),
        "lengths": draw_lengths(jax.random.fold_in(seeds[10], 71), 0),
        "clusters": draw_clusters(jax.random.fold_in(seeds[10], 71), 0),
        "top_index": draw_top_index(jax.random.fold_in(seeds[10], 71), 0),
        "w_qkv": draw_w_qkv(jax.random.fold_in(seeds[10], 71), 0),
        "w_out": noise(seeds[6], (N_SECTION, H * DH, D), (H * DH) ** -0.5, 0.21875, ((0, 2), (1, 4))),
        "w_in": noise(seeds[7], (N_SECTION, D, FF), D ** -0.5, 0.21875, ((0, 2), (2, 4))),
        "w_back": noise(seeds[8], (N_SECTION, FF, D), FF ** -0.5, 0.109375, ((0, 2), (1, 4))),
        "gains": jnp.clip(1.0 + 0.18 * jax.random.normal(seeds[9], (N_SECTION, 2, D), jnp.float32), 0.099609375, 1.8984375).astype(jnp.bfloat16),
    }


epsilon = 1e-05
negative = -1e+30
highest = lax.Precision.HIGHEST

@jax.custom_vjp
def low(v):
    return lax.optimization_barrier(v.astype(jnp.bfloat16)).astype(jnp.float32)

@jax.custom_vjp
def low_back(v):
    return v

def low_keep(v):
    return (low(v), None)

def low_pass(kept, grad):
    return (grad,)

def back_keep(v):
    return (v, None)

def back_low(kept, grad):
    return (low(grad),)
low.defvjp(low_keep, low_pass)
low_back.defvjp(back_keep, back_low)

def both_round(values):
    return low(low_back(values))

def norm_stats(values):
    centred = values - lax.optimization_barrier(jnp.mean(values, axis=-1, keepdims=True))
    return centred * lax.rsqrt(lax.optimization_barrier(jnp.mean(centred * centred, axis=-1, keepdims=True)) + epsilon)

def head_attention(queries, key_rows, value_rows, cluster_ids, top_slots, live_mask):
    cluster_count = top_slots.shape[0]
    total_rows = queries.shape[0]
    inv_root = queries.shape[1] ** (-0.5)
    member_table = (cluster_ids[:, None] == jnp.arange(cluster_count, dtype=jnp.int32)[None, :]).astype(jnp.float32) * live_mask[:, None]
    cluster_sums = jnp.dot(member_table.T, queries, precision=highest)
    counts = lax.optimization_barrier(jnp.sum(member_table, axis=0))
    centre = low(cluster_sums / counts[:, None])
    scores = low_back(jnp.dot(centre, key_rows.T, precision=highest) * inv_root)
    in_top = jnp.zeros((cluster_count, total_rows), jnp.float32).at[jnp.arange(cluster_count, dtype=jnp.int32)[:, None], top_slots].set(1.0)
    peak_score = lax.optimization_barrier(jnp.max(jnp.where(live_mask[None, :] > 0, scores, negative), axis=1, keepdims=True))
    weighted = jnp.exp(scores - peak_score) * live_mask[None, :]
    total_mass = lax.optimization_barrier(jnp.sum(weighted, axis=1))
    top_share = lax.optimization_barrier(jnp.sum(weighted * in_top, axis=1)) / total_mass
    carried = low_back(jnp.dot(low(weighted * (1.0 - in_top)), value_rows, precision=highest))
    remote = carried / total_mass[:, None]
    key_top = key_rows[top_slots][cluster_ids]
    value_top = value_rows[top_slots][cluster_ids]
    logits = low_back(jnp.einsum('td,tjd->tj', queries, key_top, precision=highest) * inv_root)
    member_prob = jax.nn.softmax(logits, axis=-1)
    top_out = jnp.einsum('tj,tjd->td', low(member_prob), value_top, precision=highest)
    return live_mask[:, None] * (top_share[cluster_ids][:, None] * top_out + remote[cluster_ids])

def block_layer(source, w_qkv, w_out, w_in, w_back, gains, cluster_ids, top_slots, length):
    total_rows = source.shape[0]
    head_count = cluster_ids.shape[0]
    hd_size = w_qkv.shape[2] // head_count
    live_mask = (jnp.arange(total_rows, dtype=jnp.int32) < length).astype(jnp.float32)
    normed_one = low(norm_stats(source) * gains[0])
    projected = [both_round(jnp.dot(normed_one, w_qkv[part_at], precision=highest)).reshape(total_rows, head_count, hd_size).transpose(1, 0, 2) for part_at in range(3)]
    one_head = jax.checkpoint(lambda pieces: head_attention(pieces[0], pieces[1], pieces[2], pieces[3], pieces[4], live_mask))
    attention = lax.map(one_head, (projected[0], projected[1], projected[2], cluster_ids, top_slots))
    attention = both_round(attention.transpose(1, 0, 2).reshape(total_rows, head_count * hd_size))
    middle = source + low_back(jnp.dot(attention, w_out, precision=highest))
    normed_two = low(norm_stats(middle) * gains[1])
    hidden = low_back(jnp.dot(normed_two, w_in, precision=highest))
    active = low(jax.nn.gelu(hidden))
    return middle + low_back(jnp.dot(active, w_back, precision=highest))

def reference(tokens, cotangent, lengths, clusters, top_index, w_qkv, w_out, w_in, w_back, gains):
    micro_count = tokens.shape[0]
    layer_count = w_qkv.shape[0]
    inputs = tokens.astype(jnp.float32)
    extras = jnp.zeros((layer_count,) + tokens.shape, jnp.float32)

    def forward(extra_in, wq_all, wo_all, wi_all, wb_all, gain_all):
        stacked = []
        for micro_at in range(micro_count):
            current = inputs[micro_at]
            per_layer = []
            for layer_at in range(layer_count):
                current = block_layer(current + extra_in[layer_at, micro_at], wq_all[layer_at], wo_all[layer_at], wi_all[layer_at], wb_all[layer_at], gain_all[layer_at], clusters[micro_at], top_index[micro_at], lengths[micro_at])
                per_layer.append(current)
            stacked.append(jnp.stack(per_layer))
        return jnp.stack(stacked, axis=1)
    acts, pullback = jax.vjp(forward, extras, w_qkv.astype(jnp.float32), w_out.astype(jnp.float32), w_in.astype(jnp.float32), w_back.astype(jnp.float32), gains.astype(jnp.float32))
    seed_grad = jnp.zeros_like(acts).at[layer_count - 1].set(cotangent.astype(jnp.float32))
    grads = pullback(seed_grad)
    return (acts, grads[0], grads[1], grads[2], grads[3], grads[4], grads[5])
```

```python
import functools

import jax
import jax.numpy as jnp
from jax import lax
from jax.experimental import pallas as pl
from jax.experimental.pallas import tpu as pltpu
from jax.sharding import PartitionSpec as P

epsilon = 1e-05
negative = -1e30
f32 = jnp.float32
bf16 = jnp.bfloat16
LANES = 128
HUBS = 64
DIRECT = 4


def round_up(value, step):
    return -(-value // step) * step


def iota(shape, dim):
    return lax.broadcasted_iota(jnp.int32, shape, dim)


def mm(a, b):
    return lax.dot_general(a, b, (((1,), (0,)), ((), ())), preferred_element_type=f32)


def mt(a, b):
    return lax.dot_general(a, b, (((1,), (1,)), ((), ())), preferred_element_type=f32)


def tm(a, b):
    return lax.dot_general(a, b, (((0,), (0,)), ((), ())), preferred_element_type=f32)


def parts2(v):
    high = v.astype(bf16)
    return high, (v - high.astype(f32)).astype(bf16)


def parts3(v):
    high = v.astype(bf16)
    rest = v - high.astype(f32)
    mid = rest.astype(bf16)
    return high.astype(f32), mid.astype(f32), rest - mid.astype(f32)


def pick_rows(one_hot, table):
    high, low = parts2(table)
    return mm(one_hot, high) + mm(one_hot, low)


def layer_stats(values):
    centred = values - jnp.mean(values, axis=-1, keepdims=True)
    inverse = lax.rsqrt(jnp.mean(centred * centred, axis=-1, keepdims=True) + epsilon)
    return centred * inverse, inverse


def norm_back(grad_hat, normed, inverse):
    return inverse * (
        grad_hat
        - jnp.mean(grad_hat, axis=-1, keepdims=True)
        - normed * jnp.mean(grad_hat * normed, axis=-1, keepdims=True)
    )


def columns(base_width, cols, rows):
    lane = iota((rows, base_width), 1)
    out = jnp.zeros((rows, base_width), f32)
    for at, col in enumerate(cols):
        out = jnp.where(lane == at, col, out)
    return out


def live_row(scal, rows):
    return (scal[1] + iota((1, rows), 1)) < scal[0]


def live_col(scal, rows):
    return (scal[1] + iota((rows, 1), 0)) < scal[0]


def table_t(cl_row, head, scal, clusters_pad):
    rows = cl_row.shape[1]
    same = iota((clusters_pad, rows), 0) == cl_row[head : head + 1, :]
    return (same & live_row(scal, rows)).astype(f32).astype(bf16)


def table(cl_col, head, clusters_pad):
    rows = cl_col.shape[0]
    same = iota((rows, clusters_pad), 1) == cl_col[:, head : head + 1]
    return same.astype(f32).astype(bf16)


def rolled(values, scal):
    return pltpu.roll(values.astype(f32), scal[2], 1).astype(bf16)


def summed(four):
    top_a, top_b, low_a, low_b = four
    return jnp.concatenate(
        [
            top_a[...].astype(f32) + top_b[...].astype(f32),
            low_a[...].astype(f32) + low_b[...].astype(f32),
        ],
        axis=0,
    )


def halves(values, top, low):
    half = values.shape[0] // 2
    top[...] = values[:half].astype(bf16)
    low[...] = values[half:].astype(bf16)


def call(kernel, outs, scal, args, flops=0):
    vmem = pl.BlockSpec(memory_space=pltpu.VMEM)
    moved = sum(a.size * a.dtype.itemsize for a in args) + sum(
        o.size * o.dtype.itemsize for o in outs
    )
    return pl.pallas_call(
        kernel,
        out_shape=outs,
        in_specs=[pl.BlockSpec(memory_space=pltpu.SMEM)] + [vmem] * len(args),
        out_specs=[vmem] * len(outs),
        compiler_params=pltpu.CompilerParams(vmem_limit_bytes=48 * 1024 * 1024),
        cost_estimate=pl.CostEstimate(flops=flops, bytes_accessed=moved, transcendentals=0),
    )(scal, *args)


def shaped(shape, dtype=f32):
    return jax.ShapeDtypeStruct(tuple(shape), dtype)


def prep_kernel(heads, slots, clusters_pad, total_rows, scal, flat, own_pick, in_list):
    entries = flat.shape[1]
    rows = own_pick.shape[1]
    per_head = entries // heads
    high_rows = round_up(max(total_rows // LANES, 1), 16)
    position = flat[...]
    high_hot = (iota((high_rows, entries), 0) == position // LANES).astype(f32).astype(bf16)
    low_hot = (iota((LANES, entries), 0) == position % LANES).astype(f32).astype(bf16)
    named = mt(high_hot, low_hot) > 0.5
    mask = named.astype(f32).astype(bf16)
    upper = (iota((LANES, LANES), 0) <= iota((LANES, LANES), 1)).astype(f32).astype(bf16)
    before = (iota((high_rows, high_rows), 1) < iota((high_rows, high_rows), 0)).astype(f32)
    rank = mm(mask, upper) + jnp.sum(mm(before.astype(bf16), mask), axis=1, keepdims=True)
    rank = jnp.where(named, rank, 0.0)
    first = scal[1] // LANES
    at_row = iota((high_rows, LANES), 0)
    own = jnp.concatenate(
        [
            jnp.sum(jnp.where(at_row == first + r, rank, 0.0), axis=0, keepdims=True)
            for r in range(rows // LANES)
        ],
        axis=1,
    )
    hub_row = iota((HUBS, rows), 0).astype(f32) + 1.0
    own_pick[...] = (hub_row == own).astype(f32).astype(bf16)
    by_low = tm(rank.astype(bf16), high_hot)
    hub_of = jnp.sum(by_low * low_hot.astype(f32), axis=0, keepdims=True)
    hub_hot = (iota((HUBS, entries), 0).astype(f32) + 1.0 == hub_of).astype(f32).astype(bf16)
    owner = iota((clusters_pad, per_head), 1) // slots
    owner_hot = (owner == iota((clusters_pad, per_head), 0)).astype(f32).astype(bf16)
    for h in range(heads):
        in_list[h] = mt(owner_hot, hub_hot[:, h * per_head : (h + 1) * per_head]).astype(bf16)


def project_kernel(first, heads, size, cl_pad, cl_rows, scal, *refs):
    if first:
        source, gains, w_qkv, cl_row, own_pick = refs[:5]
        n1r, q, k, v, pay = refs[5:]
        x = source[...].astype(f32)
    else:
        source, *four = refs[:5]
        gains, w_qkv, cl_row, own_pick = refs[5:9]
        y, n1r, q, k, v, pay = refs[9:]
        x = source[...] + summed(four)
        y[...] = x
    hat, _ = layer_stats(x)
    n1 = (hat * gains[0:1, :]).astype(bf16)
    qv = mm(n1, w_qkv[0]).astype(bf16)
    kv = mm(n1, w_qkv[1]).astype(bf16)
    vv = mm(n1, w_qkv[2]).astype(bf16)
    q[...] = qv
    k[...] = kv
    v[...] = vv
    sums, counts = [], []
    for h in range(heads):
        members = table_t(cl_row, h, scal, cl_pad)
        sums.append(mm(members, qv[:, h * size : (h + 1) * size]))
        counts.append(jnp.sum(members.astype(f32), axis=1, keepdims=True))
    width = heads * size
    spare = round_up(width + 1, LANES) - width
    block = jnp.concatenate(sums + [columns(spare, counts, cl_pad)], axis=1).astype(bf16)
    put_blocks(pay, 0, block, cl_rows)
    both = jnp.concatenate([mm(own_pick[...], kv), mm(own_pick[...], vv)], axis=1).astype(bf16)
    put_blocks(pay, cl_rows * (block.shape[1] // LANES), both, HUBS)
    n1r[...] = rolled(n1, scal)


def put_blocks(ref, start, block, rows):
    for at in range(block.shape[1] // LANES):
        ref[start + at * rows : start + (at + 1) * rows, :] = block[
            :rows, at * LANES : (at + 1) * LANES
        ]


def get_blocks(values, start, rows, count):
    return jnp.concatenate(
        [values[start + at * rows : start + (at + 1) * rows] for at in range(count)], axis=1
    )


def total_of(refs, start, rows, count):
    total = None
    for ref in refs:
        piece = ref[start : start + rows * count, :].astype(f32)
        total = piece if total is None else total + piece
    return get_blocks(total, 0, rows, count)


def pad_rows(values, rows):
    extra = rows - values.shape[0]
    if extra == 0:
        return values
    return jnp.concatenate([values, jnp.zeros((extra, values.shape[1]), values.dtype)], axis=0)


def centroid_kernel(count, heads, size, cl_pad, cl_rows, scal, *refs):
    pays = refs[:count]
    k, v, in_list, own_pick, centre_ref, cnt_ref, pay = refs[count:]
    width = heads * size
    blocks = round_up(width + 1, LANES) // LANES
    total = pad_rows(total_of(pays, 0, cl_rows, blocks), cl_pad)
    cnt_ref[...] = total[:, (blocks - 1) * LANES :]
    rows = k.shape[0]
    live = live_row(scal, rows)
    inv_root = size ** (-0.5)
    carried, extras = [], []
    for h in range(heads):
        cnt = total[:, width + h : width + h + 1]
        centre = jnp.where(
            cnt > 0, total[:, h * size : (h + 1) * size] / jnp.maximum(cnt, 1.0), 0.0
        ).astype(bf16)
        centre_ref[h] = centre
        scores = mt(centre, k[:, h * size : (h + 1) * size]) * inv_root
        peak = jnp.max(jnp.where(live, scores, negative), axis=1, keepdims=True)
        weighted = jnp.where(live, jnp.exp(jnp.where(live, scores - peak, 0.0)), 0.0)
        in_top = mm(in_list[h], own_pick[...])
        mass = jnp.sum(weighted, axis=1, keepdims=True)
        top_mass = jnp.sum(weighted * in_top, axis=1, keepdims=True)
        rest = (weighted * (1.0 - in_top)).astype(bf16)
        carried.append(mm(rest, v[:, h * size : (h + 1) * size]))
        for value in (peak, mass, top_mass):
            extras.extend(parts3(value))
    spare = blocks * LANES - width
    block = jnp.concatenate(carried + [columns(spare, extras, cl_pad)], axis=1).astype(bf16)
    put_blocks(pay, 0, block, cl_rows)


def member_kernel(count, heads, size, cl_pad, cl_rows, scal, *refs):
    pays = refs[:count]
    q, cl_col, in_list, hub_ref, prob_ref, top_ref = refs[count:]
    width = heads * size
    blocks = round_up(width + 1, LANES) // LANES
    hub = total_of(pays, blocks * cl_rows, HUBS, 2 * width // LANES).astype(bf16)
    hub_ref[...] = hub
    inv_root = size ** (-0.5)
    probs, outs = [], []
    for h in range(heads):
        keys = hub[:, h * size : (h + 1) * size]
        values = hub[:, width + h * size : width + (h + 1) * size]
        logits = mt(q[:, h * size : (h + 1) * size], keys) * inv_root
        chosen = mm(table(cl_col, h, cl_pad), in_list[h]) > 0.5
        logits = jnp.where(chosen, logits, negative)
        exponent = jnp.where(
            chosen, jnp.exp(logits - jnp.max(logits, axis=1, keepdims=True)), 0.0
        )
        prob = exponent / jnp.sum(exponent, axis=1, keepdims=True)
        probs.append(prob)
        outs.append(mm(prob.astype(bf16), values))
    prob_ref[...] = jnp.concatenate(probs, axis=1)
    top_ref[...] = jnp.concatenate(outs, axis=1)


def combine_kernel(count, heads, size, cl_pad, cl_rows, scal, *refs):
    pays = refs[:count]
    top_out, cl_col, att_ref, stat_ref = refs[count:]
    width = heads * size
    blocks = round_up(width + 1, LANES) // LANES
    tables = [
        pad_rows(get_blocks(ref[...].astype(f32), 0, cl_rows, blocks), cl_pad) for ref in pays
    ]
    rows = top_out.shape[0]
    live = live_col(scal, rows)
    pieces = []
    for h in range(heads):

        def value(one, which):
            at = width + 9 * h + 3 * which
            return one[:, at : at + 1] + one[:, at + 1 : at + 2] + one[:, at + 2 : at + 3]

        peaks = [value(one, 0) for one in tables]
        peak = functools.reduce(jnp.maximum, peaks)
        mass = top_mass = carried = 0.0
        for one, mine in zip(tables, peaks):
            scale = jnp.exp(mine - peak)
            mass = mass + value(one, 1) * scale
            top_mass = top_mass + value(one, 2) * scale
            carried = carried + one[:, h * size : (h + 1) * size] * scale
        safe = jnp.where(mass > 0, mass, 1.0)
        remote = carried / safe
        share = top_mass / safe
        lanes = LANES - size
        stat_ref[h] = jnp.concatenate(
            [carried, columns(lanes, (peak, safe, top_mass, share), cl_pad)], axis=1
        )
        looked = pick_rows(
            table(cl_col, h, cl_pad),
            jnp.concatenate([remote, columns(lanes, (share,), cl_pad)], axis=1),
        )
        att = looked[:, size : size + 1] * top_out[:, h * size : (h + 1) * size] + looked[:, :size]
        pieces.append(jnp.where(live, att, 0.0))
    joined = jnp.concatenate(pieces, axis=1).astype(bf16)
    att_ref[...] = joined


def feed_kernel(count, scal, *refs):
    source = refs[0]
    atts = refs[1 : 1 + count]
    w_out, gains, w_in, w_back = refs[1 + count : 5 + count]
    x1_ref, n2r, active_ref, slope_ref, top, low = refs[5 + count :]
    x1 = source[...].astype(f32)
    for at, ref in enumerate(atts):
        x1 = x1 + mm(ref[...], w_out[at])
    x1_ref[...] = x1
    hat, _ = layer_stats(x1)
    n2 = (hat * gains[1:2, :]).astype(bf16)
    hidden = mm(n2, w_in[...])
    root = (2.0 / 3.141592653589793) ** 0.5
    square = hidden * hidden
    bent = jnp.tanh(root * hidden * (1.0 + 0.044715 * square))
    active = (0.5 * hidden * (1.0 + bent)).astype(bf16)
    active_ref[...] = active
    slope_ref[...] = 0.5 * (1.0 + bent) + 0.5 * hidden * (1.0 - bent * bent) * root * (
        1.0 + 3 * 0.044715 * square
    )
    halves(mm(active, w_back[...]), top, low)
    n2r[...] = rolled(n2, scal)


def feed_back_kernel(last, scal, *refs):
    if last:
        cot, slope, w_in, w_back = refs[:4]
        dybr, dz_ref, top, low = refs[4:]
        dyb = cot[...]
    else:
        grad_middle, source, *four = refs[:6]
        gains, slope, w_in, w_back = refs[6:10]
        dy_ref, gain_ref, dybr, dz_ref, top, low = refs[10:]
        dy = input_grad(grad_middle, source, four, gains, gain_ref)
        dy_ref[...] = dy
        dyb = dy.astype(bf16)
    dz = (mt(dyb, w_back[...]) * slope[...]).astype(bf16)
    dz_ref[...] = dz
    halves(mt(dz, w_in[...]), top, low)
    dybr[...] = rolled(dyb, scal)


def input_grad(grad_middle, source, four, gains, gain_ref):
    grad_normed = summed(four)
    hat, inverse = layer_stats(source[...].astype(f32))
    gain_ref[...] = jnp.sum(grad_normed * hat, axis=0, keepdims=True)
    return grad_middle[...] + norm_back(grad_normed * gains[0:1, :], hat, inverse)


def input_grad_kernel(scal, *refs):
    grad_middle, source, *four = refs[:6]
    gains, dy_ref, gain_ref = refs[6:]
    dy_ref[...] = input_grad(grad_middle, source, four, gains, gain_ref)


def middle_back_kernel(heads, size, cl_pad, cl_rows, scal, *refs):
    four = refs[:4]
    middle, grad_out, gains, w_out, top_out, cl_row = refs[4:10]
    dx1_ref, dx1r, dtop_ref, gain_ref, pay = refs[10:]
    grad_normed = summed(four)
    hat, inverse = layer_stats(middle[...])
    gain_ref[...] = jnp.sum(grad_normed * hat, axis=0, keepdims=True)
    dx1 = grad_out[...].astype(f32) + norm_back(grad_normed * gains[1:2, :], hat, inverse)
    dx1_ref[...] = dx1
    dx1b = dx1.astype(bf16)
    rows = dx1.shape[0]
    datt = mt(dx1b, w_out[...])
    dtop = jnp.where(live_col(scal, rows), datt, 0.0).astype(bf16)
    dtop_ref[...] = dtop
    sums, shares = [], []
    for h in range(heads):
        members = table_t(cl_row, h, scal, cl_pad)
        own = dtop[:, h * size : (h + 1) * size]
        sums.append(mm(members, own))
        product = own.astype(f32) * top_out[:, h * size : (h + 1) * size]
        both = mm(members, jnp.concatenate(parts2(product), axis=1))
        shares.extend(parts3(jnp.sum(both, axis=1, keepdims=True)))
    width = heads * size
    spare = round_up(width + 1, LANES) - width
    block = jnp.concatenate(sums + [columns(spare, shares, cl_pad)], axis=1).astype(bf16)
    put_blocks(pay, 0, block, cl_rows)
    dx1r[...] = rolled(dx1b, scal)


def member_back_kernel(heads, size, cl_pad, scal, *refs):
    q, hub_ref, prob_ref, dtop, stat, cl_col, dq_ref, pay = refs
    width = heads * size
    inv_root = size ** (-0.5)
    hub = hub_ref[...]
    dqs, dks, dvs = [], [], []
    for h in range(heads):
        keys = hub[:, h * size : (h + 1) * size]
        values = hub[:, width + h * size : width + (h + 1) * size]
        prob = prob_ref[:, h * HUBS : (h + 1) * HUBS]
        own = dtop[:, h * size : (h + 1) * size]
        share = pick_rows(table(cl_col, h, cl_pad), stat[h])[:, size + 3 : size + 4]
        da = mt(own, values) * share
        dg = (prob * (da - jnp.sum(prob * da, axis=1, keepdims=True))).astype(bf16)
        dqs.append(mm(dg, keys) * inv_root)
        dks.append(tm(dg, q[:, h * size : (h + 1) * size]) * inv_root)
        scaled = own.astype(f32) * share
        dvs.append(tm(prob.astype(bf16), scaled.astype(bf16)))
    dq_ref[...] = jnp.concatenate(dqs, axis=1)
    put_blocks(pay, 0, jnp.concatenate(dks + dvs, axis=1).astype(bf16), HUBS)


def centroid_back_kernel(count, heads, size, cl_pad, cl_rows, scal, *refs):
    pays = refs[:count]
    centre_ref, stat, k, v, in_list, own_pick, pay, dk_ref, dv_ref = refs[count:]
    width = heads * size
    blocks = round_up(width + 1, LANES) // LANES
    total = pad_rows(total_of(pays, 0, cl_rows, blocks), cl_pad)
    rows = k.shape[0]
    live = live_row(scal, rows)
    inv_root = size ** (-0.5)
    dcs, dks, dvs = [], [], []
    for h in range(heads):
        keys = k[:, h * size : (h + 1) * size]
        values = v[:, h * size : (h + 1) * size]
        centre = centre_ref[h]
        grad_remote = total[:, h * size : (h + 1) * size]
        at = width + 3 * h
        grad_share = total[:, at : at + 1] + total[:, at + 1 : at + 2] + total[:, at + 2 : at + 3]
        carried = stat[h][:, :size]
        peak = stat[h][:, size : size + 1]
        mass = stat[h][:, size + 1 : size + 2]
        top_mass = stat[h][:, size + 2 : size + 3]
        grad_carried = (grad_remote / mass).astype(bf16)
        grad_top = grad_share / mass
        grad_mass = -(
            jnp.sum(grad_remote * carried, axis=1, keepdims=True) + grad_share * top_mass
        ) / (mass * mass)
        scores = mt(centre, keys) * inv_root
        weighted = jnp.where(live, jnp.exp(jnp.where(live, scores - peak, 0.0)), 0.0)
        in_top = mm(in_list[h], own_pick[...])
        rest = (weighted * (1.0 - in_top)).astype(bf16)
        grad_weighted = (
            (1.0 - in_top) * mt(grad_carried, values) + in_top * grad_top + grad_mass
        )
        grad_scores = (grad_weighted * weighted).astype(bf16)
        dcs.append(mm(grad_scores, keys) * inv_root)
        dks.append(tm(grad_scores, centre) * inv_root)
        dvs.append(tm(rest, grad_carried))
    spare = blocks * LANES - width
    block = jnp.concatenate(dcs + [jnp.zeros((cl_pad, spare), f32)], axis=1).astype(bf16)
    put_blocks(pay, 0, block, cl_rows)
    dk_ref[...] = jnp.concatenate(dks, axis=1)
    dv_ref[...] = jnp.concatenate(dvs, axis=1)


def project_back_kernel(count, heads, size, cl_pad, cl_rows, scal, *refs):
    centre_pays = refs[:count]
    hub_pays = refs[count : 2 * count]
    dq_top, dk_c, dv_c, cnt_ref, cl_col, own_pick, w_qkv = refs[2 * count : 2 * count + 7]
    dqkv_ref, top, low = refs[2 * count + 7 :]
    width = heads * size
    blocks = round_up(width + 1, LANES) // LANES
    total = pad_rows(total_of(centre_pays, 0, cl_rows, blocks), cl_pad)
    hub = total_of(hub_pays, 0, HUBS, 2 * width // LANES)
    high, low_part = parts2(hub)
    spread = tm(own_pick[...], high) + tm(own_pick[...], low_part)
    rows = dq_top.shape[0]
    live = live_col(scal, rows)
    base = round_up(width + 1, LANES) - LANES
    dqs = []
    for h in range(heads):
        at = width - base + h
        cnt = jnp.maximum(cnt_ref[:, at : at + 1], 1.0)
        from_centre = pick_rows(
            table(cl_col, h, cl_pad), total[:, h * size : (h + 1) * size] / cnt
        )
        dqs.append(jnp.where(live, from_centre, 0.0))
    dq = (dq_top[...] + jnp.concatenate(dqs, axis=1)).astype(bf16)
    dk = (dk_c[...] + spread[:, :width]).astype(bf16)
    dv = (dv_c[...] + spread[:, width:]).astype(bf16)
    dqkv_ref[...] = jnp.concatenate([dq, dk, dv], axis=1)
    halves(mt(dq, w_qkv[0]) + mt(dk, w_qkv[1]) + mt(dv, w_qkv[2]), top, low)


def moved(block, axis, target):
    devices = range(lax.axis_size(axis))
    return lax.ppermute(block, axis, [(i, target(i)) for i in devices])


def swap(block):
    return moved(block, "section", lambda i: i ^ 1)


def every_seq(block):
    count = lax.axis_size("seq")
    if count > DIRECT:
        gathered = lax.all_gather(block, "seq")
        return [gathered[at] for at in range(count)]
    return [block] + [
        moved(block, "seq", lambda i, k=k: (i + k) % count) for k in range(1, count)
    ]


def every_head(block):
    return [block] + [
        moved(block, "head", lambda i, k=k: i ^ k) for k in range(1, lax.axis_size("head"))
    ]


def head_sum(top, low):
    distances = [1 << at for at in range(lax.axis_size("head").bit_length() - 1)]
    for step in range(len(distances)):
        one = distances[step]
        other = distances[len(distances) - 1 - step]
        far_top = moved(top, "head", lambda i: i ^ one)
        far_low = moved(low, "head", lambda i: i ^ other)
        if step < len(distances) - 1:
            top = (top.astype(f32) + far_top.astype(f32)).astype(bf16)
            low = (low.astype(f32) + far_low.astype(f32)).astype(bf16)
    return (top, far_top, low, far_low)


def to_owner(block, layer):
    far = lax.ppermute(block, "section", [(1 - layer, layer)])
    return block.astype(f32) + far.astype(f32)


def over_seq(block, layer):
    count = lax.axis_size("seq")
    part = block.shape[0] // count
    if count > DIRECT:
        return lax.psum_scatter(block.astype(bf16), "seq", scatter_dimension=0, tiled=True).astype(
            f32
        )
    total = block[:part]
    for k in range(1, count):
        route = [
            (layer * count + i, layer * count + (i + k) % count) for i in range(count)
        ]
        piece = block[k * part : (k + 1) * part].astype(bf16)
        total = total + lax.ppermute(piece, ("section", "seq"), route).astype(f32)
    return total


def shards(tokens, cotangent, lengths, clusters, top_index, w_qkv, w_out, w_in, w_back, gains):
    section = lax.axis_index("section")
    me = lax.axis_index("seq")
    count = lax.axis_size("seq")
    pick = lambda array: lax.dynamic_index_in_dim(array, section, 0, keepdims=False)
    tok, cot, length = pick(tokens), pick(cotangent), pick(lengths)
    cl_row, tops = pick(clusters), pick(top_index)
    rows, dim = tok.shape
    heads, cluster_count, slots = tops.shape
    size = w_qkv.shape[3] // heads
    width = heads * size
    hidden = w_in.shape[2]
    total_rows = rows * count
    cl_pad = round_up(cluster_count, LANES)
    cl_rows = round_up(cluster_count, 16)
    shift = lax.rem(dim - me * (dim // count), dim) if count <= DIRECT else 0
    scal = jnp.stack([length, me * rows, jnp.asarray(shift, jnp.int32)]).astype(jnp.int32)
    cl_col = cl_row.T
    blocks = round_up(width + 1, LANES) // LANES
    hub_blocks = 2 * width // LANES
    sizes = (heads, size, cl_pad, cl_rows)
    fours = [shaped((rows // 2, dim), bf16)] * 2

    def both_layers(mine):
        other = swap(mine)
        return [jnp.where(section == layer, mine, other) for layer in range(2)]

    w_qkv = both_layers(w_qkv[0])
    out_all = both_layers(jnp.stack(every_head(w_out[0])))
    w_in = both_layers(w_in[0])
    w_back = both_layers(w_back[0])
    gains = [g.astype(f32) for g in both_layers(gains[0])]

    own_pick, in_list = call(
        functools.partial(prep_kernel, heads, slots, cl_pad, total_rows),
        [shaped((HUBS, rows), bf16), shaped((heads, cl_pad, HUBS), bf16)],
        scal,
        [tops.reshape(1, -1)],
    )

    source, four = tok, None
    kept, acts = [], []
    for layer in range(2):
        outs = [
            shaped((rows, dim), bf16),
            shaped((rows, width), bf16),
            shaped((rows, width), bf16),
            shaped((rows, width), bf16),
            shaped((blocks * cl_rows + hub_blocks * HUBS, LANES), bf16),
        ]
        tail = [gains[layer], w_qkv[layer], cl_row, own_pick]
        if layer == 0:
            n1r, q, k, v, pay = call(
                functools.partial(project_kernel, True, *sizes), outs, scal, [tok] + tail
            )
        else:
            source, n1r, q, k, v, pay = call(
                functools.partial(project_kernel, False, *sizes),
                [shaped((rows, dim))] + outs,
                scal,
                [x1, *four] + tail,
            )
            acts.append(source)
        pays = every_seq(pay)
        centre, cnt, pay = call(
            functools.partial(centroid_kernel, len(pays), *sizes),
            [
                shaped((heads, cl_pad, size), bf16),
                shaped((cl_pad, LANES)),
                shaped((blocks * cl_rows, LANES), bf16),
            ],
            scal,
            [*pays, k, v, in_list, own_pick],
        )
        stats = every_seq(pay)
        hub, prob, top_out = call(
            functools.partial(member_kernel, len(pays), *sizes),
            [
                shaped((HUBS, 2 * width), bf16),
                shaped((rows, heads * HUBS)),
                shaped((rows, width)),
            ],
            scal,
            [*pays, q, cl_col, in_list],
        )
        att, stat = call(
            functools.partial(combine_kernel, len(stats), *sizes),
            [shaped((rows, width), bf16), shaped((heads, cl_pad, LANES))],
            scal,
            [*stats, top_out, cl_col],
        )
        atts = every_head(att)
        x1, n2r, active, slope, top, low = call(
            functools.partial(feed_kernel, len(atts)),
            [
                shaped((rows, dim)),
                shaped((rows, dim), bf16),
                shaped((rows, hidden), bf16),
                shaped((rows, hidden)),
            ]
            + fours,
            scal,
            [source, *atts, out_all[layer], gains[layer], w_in[layer], w_back[layer]],
        )
        four = head_sum(top, low)
        kept.append(
            (source, n1r, q, k, v, centre, cnt, hub, prob, top_out, att, stat, x1, n2r, active, slope)
        )
    top_a, top_b, low_a, low_b = (piece.astype(f32) for piece in four)
    acts.append(x1 + jnp.concatenate([top_a + top_b, low_a + low_b], axis=0))

    in_grads, grads, gain_grads = [None, None], [None, None], [None, None]
    for layer in (1, 0):
        (source, n1r, q, k, v, centre, cnt, hub, prob, top_out, att, stat, x1, n2r, active, slope) = kept[layer]
        outs = [shaped((rows, dim), bf16), shaped((rows, hidden), bf16)] + fours
        tail = [slope, w_in[layer], w_back[layer]]
        if layer == 1:
            dy = cot
            dybr, dz, top, low = call(
                functools.partial(feed_back_kernel, True), outs, scal, [cot] + tail
            )
        else:
            dy, gain_one, dybr, dz, top, low = call(
                functools.partial(feed_back_kernel, False),
                [shaped((rows, dim)), shaped((1, dim))] + outs,
                scal,
                [dx1, kept[1][0], *four, gains[1]] + tail,
            )
            in_grads[1] = dy
            gain_grads[1] = jnp.concatenate([gain_one, gain_two], axis=0)
        four = head_sum(top, low)
        first = to_owner(tm(dybr, active).astype(bf16), layer)
        second = to_owner(tm(n2r, dz).astype(bf16), layer)
        dx1, dx1r, dtop, gain_two, pay = call(
            functools.partial(middle_back_kernel, *sizes),
            [
                shaped((rows, dim)),
                shaped((rows, dim), bf16),
                shaped((rows, width), bf16),
                shaped((1, dim)),
                shaped((blocks * cl_rows, LANES), bf16),
            ],
            scal,
            [*four, x1, dy, gains[layer], out_all[layer][0], top_out, cl_row],
        )
        pays = every_seq(pay)
        dq_top, hub_pay = call(
            functools.partial(member_back_kernel, heads, size, cl_pad),
            [shaped((rows, width)), shaped((hub_blocks * HUBS, LANES), bf16)],
            scal,
            [q, hub, prob, dtop, stat, cl_col],
        )
        hub_pays = every_seq(hub_pay)
        pay, dk, dv = call(
            functools.partial(centroid_back_kernel, len(pays), *sizes),
            [
                shaped((blocks * cl_rows, LANES), bf16),
                shaped((rows, width)),
                shaped((rows, width)),
            ],
            scal,
            [*pays, centre, stat, k, v, in_list, own_pick],
        )
        pays = every_seq(pay)
        dqkv, top, low = call(
            functools.partial(project_back_kernel, len(pays), *sizes),
            [shaped((rows, 3 * width), bf16)] + fours,
            scal,
            [*pays, *hub_pays, dq_top, dk, dv, cnt, cl_col, own_pick, w_qkv[layer]],
        )
        four = head_sum(top, low)
        third = jnp.concatenate([tm(n1r, dqkv), tm(dx1r, att)], axis=1)
        third = to_owner(third.astype(bf16), layer)
        grads[layer] = [over_seq(one, layer) for one in (first, second, third)]
    dy, gain_one = call(
        input_grad_kernel,
        [shaped((rows, dim)), shaped((1, dim))],
        scal,
        [dx1, tok, *four, gains[0]],
    )
    in_grads[0] = dy
    gain_grads[0] = jnp.concatenate([gain_one, gain_two], axis=0)

    def owned(pair):
        mine = jnp.where(section == 0, pair[0], pair[1])
        far = swap(jnp.where(section == 0, pair[1], pair[0]))
        return mine, far

    def stacked(pair):
        mine, far = owned(pair)
        return jnp.stack([jnp.where(section == 0, mine, far), jnp.where(section == 0, far, mine)])

    mine, far = owned(gain_grads)
    gain_sum = lax.psum_scatter(
        (mine + far), "seq", scatter_dimension=1, tiled=True
    ) if count > DIRECT else gain_over_seq(mine + far, me, count)
    back, into, rest = (jnp.where(section == 0, a, b) for a, b in zip(*grads))
    grad_qkv = rest[:, : 3 * width].reshape(-1, 3, width).transpose(1, 0, 2)
    grad_out = rest[:, 3 * width :].T
    return (
        stacked(acts)[None],
        stacked(in_grads)[None],
        grad_qkv[None],
        grad_out[None],
        into[None],
        back.T[None],
        gain_sum[None],
    )


def gain_over_seq(values, me, count):
    everyone = sum(every_seq(values))
    part = values.shape[1] // count
    return lax.dynamic_slice_in_dim(everyone, me * part, part, 1)


def solution(mesh):
    placed = (
        P(None, "seq", None),
        P(None, "seq", None),
        P(),
        P(None, "head", "seq"),
        P(None, "head", None, None),
        P("section", None, None, "head"),
        P("section", "head", None),
        P("section", None, "head"),
        P("section", "head", None),
        P("section", None, None),
    )
    return jax.shard_map(
        shards,
        mesh=mesh,
        in_specs=placed,
        out_specs=(
            P("section", None, "seq", None),
            P("section", None, "seq", None),
            P("section", None, "seq", "head"),
            P("section", "head", "seq"),
            P("section", "seq", "head"),
            P("section", "head", "seq"),
            P("section", None, "seq"),
        ),
        check_vma=False,
    )
```

```python
import functools

import jax
import jax.numpy as jnp
from jax import lax
from jax.experimental import pallas as pl
from jax.experimental.pallas import tpu as pltpu
from jax.sharding import PartitionSpec as P

SECTION, SEQ, HEAD = "section", "seq", "head"
epsilon = 1e-05
negative = -1e30
f32 = jnp.float32
bf16 = jnp.bfloat16
LANES = 128
HUBS = 64
VMEM_LIMIT = 32 * 1024 * 1024
DIRECT = 4


def round_up(value, step):
    return -(-value // step) * step


def iota(shape, dim):
    return lax.broadcasted_iota(jnp.int32, shape, dim)


def mm(a, b):
    return lax.dot_general(a, b, (((1,), (0,)), ((), ())), preferred_element_type=f32)


def mt(a, b):
    return lax.dot_general(a, b, (((1,), (1,)), ((), ())), preferred_element_type=f32)


def tm(a, b):
    return lax.dot_general(a, b, (((0,), (0,)), ((), ())), preferred_element_type=f32)


def parts2(v):
    high = v.astype(bf16)
    return high, (v - high.astype(f32)).astype(bf16)


def parts3(v):
    high = v.astype(bf16)
    rest = v - high.astype(f32)
    mid = rest.astype(bf16)
    return high.astype(f32), mid.astype(f32), rest - mid.astype(f32)


def pick_rows(one_hot, table):
    high, low = parts2(table)
    return mm(one_hot, high) + mm(one_hot, low)


def layer_stats(values):
    centred = values - jnp.mean(values, axis=-1, keepdims=True)
    inverse = lax.rsqrt(jnp.mean(centred * centred, axis=-1, keepdims=True) + epsilon)
    return centred * inverse, inverse


def norm_back(grad_hat, normed, inverse):
    return inverse * (
        grad_hat
        - jnp.mean(grad_hat, axis=-1, keepdims=True)
        - normed * jnp.mean(grad_hat * normed, axis=-1, keepdims=True)
    )


def columns(base_width, cols, rows):
    lane = iota((rows, base_width), 1)
    out = jnp.zeros((rows, base_width), f32)
    for at, col in enumerate(cols):
        out = jnp.where(lane == at, col, out)
    return out


def here(name):
    return lax.axis_index(name)


def live_row(lengths, rows):
    return (here(SEQ) * rows + iota((1, rows), 1)) < lengths[here(SECTION)]


def live_col(lengths, rows):
    return (here(SEQ) * rows + iota((rows, 1), 0)) < lengths[here(SECTION)]


def gain_row(mine, other, layer, row):
    return jnp.where(
        here(SECTION) == layer,
        mine[row : row + 1, :].astype(f32),
        other[row : row + 1, :].astype(f32),
    )


class Choice:
    def __init__(self, layer, pairs, bufs, sems):
        self.copies = [
            (pltpu.make_async_copy(mine, buf, sem), pltpu.make_async_copy(other, buf, sem))
            for (mine, other), buf, sem in zip(pairs, bufs, sems)
        ]
        mine_here = here(SECTION) == layer

        @pl.when(mine_here)
        def _():
            for mine, _other in self.copies:
                mine.start()

        @pl.when(jnp.logical_not(mine_here))
        def _():
            for _mine, other in self.copies:
                other.start()

    def wait(self, at):
        self.copies[at][0].wait()


def summed(four):
    top_a, top_b, low_a, low_b = four
    return jnp.concatenate(
        [
            top_a[...].astype(f32) + top_b[...].astype(f32),
            low_a[...].astype(f32) + low_b[...].astype(f32),
        ],
        axis=0,
    )


def halves(values, top, low):
    half = values.shape[0] // 2
    top[...] = values[:half].astype(bf16)
    low[...] = values[half:].astype(bf16)


def call(kernel, outs, lengths, args, anys=(), bufs=(), ties=(), sems=None, outs_any=False):
    vmem = pl.BlockSpec(memory_space=pltpu.VMEM)
    anywhere = pl.BlockSpec(memory_space=pl.ANY)
    args, anys, ties = list(args), list(anys), list(ties)
    moved_bytes = sum(a.size * a.dtype.itemsize for a in args + list(outs) + list(bufs))
    first, last = 1 + len(args) + len(anys), 1 + len(args) + len(anys) + len(ties)

    def body(*refs):
        kernel(*refs[:first], *refs[last:])

    scratch = [pltpu.VMEM(b.shape, b.dtype) for b in bufs]
    if bufs or sems:
        scratch.append(pltpu.SemaphoreType.DMA((sems or len(bufs),)))
    whole = kernel.func if isinstance(kernel, functools.partial) else kernel
    with jax.named_scope(whole.__name__):
        return pl.pallas_call(
            body,
            out_shape=outs,
            in_specs=[pl.BlockSpec(memory_space=pltpu.SMEM)]
            + [vmem] * len(args)
            + [anywhere] * (len(anys) + len(ties)),
            out_specs=[anywhere if outs_any else vmem] * len(outs),
            scratch_shapes=scratch,
            compiler_params=pltpu.CompilerParams(vmem_limit_bytes=VMEM_LIMIT),
            cost_estimate=pl.CostEstimate(
                flops=0, bytes_accessed=moved_bytes, transcendentals=0
            ),
        )(lengths, *args, *anys, *ties)


def shaped(shape, dtype=f32):
    return jax.ShapeDtypeStruct(tuple(shape), dtype)


def named_rows(tops, head, clusters_pad):
    section = here(SECTION)
    slots, clusters = tops.shape[2:]
    rows = tops[section, head]
    if clusters < clusters_pad:
        rows = jnp.concatenate(
            [rows, jnp.full((slots, clusters_pad - clusters), -1, jnp.int32)], axis=1
        )
    return jnp.concatenate([rows[at : at + 1, :] for at in range(slots)], axis=1)


def cluster_row(clusters, head):
    return clusters[head, pl.ds(here(SECTION), 1), :]


def rank_kernel(heads, cl_pad, lengths, tops, clusters, own_pick, hubs, members_t):
    rows = own_pick.shape[1]
    high_rows = hubs.shape[0]
    named = None
    for h in range(heads):
        position = named_rows(tops, h, cl_pad)
        entries = position.shape[1]
        high_hot = (iota((high_rows, entries), 0) == position // LANES).astype(f32).astype(bf16)
        low_hot = (iota((LANES, entries), 0) == position % LANES).astype(f32).astype(bf16)
        found = mt(high_hot, low_hot)
        named = found if named is None else named + found
    named = named > 0.5
    mask = named.astype(f32).astype(bf16)
    upper = (iota((LANES, LANES), 0) <= iota((LANES, LANES), 1)).astype(f32).astype(bf16)
    before = (iota((high_rows, high_rows), 1) < iota((high_rows, high_rows), 0)).astype(f32)
    rank = mm(mask, upper) + jnp.sum(mm(before.astype(bf16), mask), axis=1, keepdims=True)
    rank = jnp.where(named, rank, 0.0)
    hubs[...] = rank
    first = here(SEQ) * (rows // LANES)
    at_row = iota((high_rows, LANES), 0)
    own = jnp.concatenate(
        [
            jnp.sum(jnp.where(at_row == first + r, rank, 0.0), axis=0, keepdims=True)
            for r in range(rows // LANES)
        ],
        axis=1,
    )
    hub_row = iota((HUBS, rows), 0).astype(f32) + 1.0
    own_pick[...] = (hub_row == own).astype(f32).astype(bf16)
    live = live_row(lengths, rows)
    for h in range(heads):
        same = iota((cl_pad, rows), 0) == cluster_row(clusters, h)
        members_t[h] = (same & live).astype(f32).astype(bf16)


def list_kernel(heads, cl_pad, lengths, tops, clusters, hubs, own_pick, in_top, chosen, members):
    slots = tops.shape[2]
    rows = own_pick.shape[1]
    high_rows = hubs.shape[0]
    rank = hubs[...].astype(bf16)
    for h in range(heads):
        position = named_rows(tops, h, cl_pad)
        entries = position.shape[1]
        high_hot = (iota((high_rows, entries), 0) == position // LANES).astype(f32).astype(bf16)
        by_low = tm(rank, high_hot)
        hub_of = jnp.sum(
            jnp.where(iota((LANES, entries), 0) == position % LANES, by_low, 0.0),
            axis=0,
            keepdims=True,
        )
        hub_row = iota((HUBS, cl_pad), 0).astype(f32) + 1.0
        in_list = jnp.zeros((HUBS, cl_pad), f32)
        for at in range(slots):
            row = hub_of[:, at * cl_pad : (at + 1) * cl_pad]
            in_list = jnp.where(hub_row == row, 1.0, in_list)
        in_list = in_list.astype(bf16)
        in_top[h] = tm(in_list, own_pick[...]).astype(bf16)
        same = (iota((cl_pad, rows), 0) == cluster_row(clusters, h)).astype(f32)
        table = same.T.astype(bf16)
        members[h] = table
        chosen[:, h * HUBS : (h + 1) * HUBS] = mt(table, in_list).astype(bf16)


def project_kernel(layer, heads, size, cl_rows, lengths, *refs):
    if layer == 0:
        source, gain_mine, gain_other, members_t, own_pick, w_mine, w_other = refs[:7]
        n1r, q, k, v, pay = refs[7:]
    else:
        source, *four = refs[:5]
        gain_mine, gain_other, members_t, own_pick, w_mine, w_other = refs[5:11]
        y, n1r, q, k, v, pay, w_qkv, sems = refs[11:]
        weights = Choice(layer, [(w_mine, w_other)], [w_qkv], [sems.at[0]])
    if layer == 0:
        x = source[here(SECTION)].astype(f32)
    else:
        x = source[...] + summed(four)
        y[...] = x
    hat, _ = layer_stats(x)
    n1 = (hat * gain_row(gain_mine, gain_other, layer, 0)).astype(bf16)
    if layer == 0:
        w_qkv = [jnp.where(here(SECTION) == 0, w_mine[at], w_other[at]) for at in range(3)]
    else:
        weights.wait(0)
    qv = mt(n1, w_qkv[0]).astype(bf16)
    kv = mt(n1, w_qkv[1]).astype(bf16)
    vv = mt(n1, w_qkv[2]).astype(bf16)
    q[...] = qv
    k[...] = kv
    v[...] = vv
    sums, counts = [], []
    for h in range(heads):
        members = members_t[h]
        sums.append(mm(members, qv[:, h * size : (h + 1) * size]))
        counts.append(jnp.sum(members.astype(f32), axis=1, keepdims=True))
    width = heads * size
    spare = round_up(width + 1, LANES) - width
    cl_pad = members_t.shape[1]
    block = jnp.concatenate(sums + [columns(spare, counts, cl_pad)], axis=1).astype(bf16)
    put_blocks(pay, 0, block, cl_rows)
    both = jnp.concatenate([mm(own_pick[...], kv), mm(own_pick[...], vv)], axis=1).astype(bf16)
    put_blocks(pay, cl_rows * (block.shape[1] // LANES), both, HUBS)
    n1r[...] = n1


def put_blocks(ref, start, block, rows):
    for at in range(block.shape[1] // LANES):
        ref[start + at * rows : start + (at + 1) * rows, :] = block[
            :rows, at * LANES : (at + 1) * LANES
        ]


def get_blocks(values, start, rows, count):
    return jnp.concatenate(
        [values[start + at * rows : start + (at + 1) * rows] for at in range(count)], axis=1
    )


def total_of(refs, start, rows, count):
    total = None
    for ref in refs:
        piece = ref[start : start + rows * count, :].astype(f32)
        total = piece if total is None else total + piece
    return get_blocks(total, 0, rows, count)


def pad_rows(values, rows):
    extra = rows - values.shape[0]
    if extra == 0:
        return values
    return jnp.concatenate([values, jnp.zeros((extra, values.shape[1]), values.dtype)], axis=0)


def centroid_kernel(count, heads, size, cl_rows, lengths, *refs):
    pays = refs[:count]
    k, v, in_tops, centre_ref, cnt_ref, pay = refs[count:]
    width = heads * size
    cl_pad = in_tops.shape[1]
    blocks = round_up(width + 1, LANES) // LANES
    total = pad_rows(total_of(pays, 0, cl_rows, blocks), cl_pad)
    cnt_ref[...] = total[:, (blocks - 1) * LANES :]
    rows = k.shape[0]
    live = live_row(lengths, rows)
    inv_root = size ** (-0.5)
    carried, extras = [], []
    for h in range(heads):
        cnt = total[:, width + h : width + h + 1]
        centre = jnp.where(
            cnt > 0, total[:, h * size : (h + 1) * size] / jnp.maximum(cnt, 1.0), 0.0
        ).astype(bf16)
        centre_ref[h] = centre
        scores = mt(centre, k[:, h * size : (h + 1) * size]) * inv_root
        peak = jnp.max(jnp.where(live, scores, negative), axis=1, keepdims=True)
        weighted = jnp.where(live, jnp.exp(jnp.where(live, scores - peak, 0.0)), 0.0)
        in_top = in_tops[h].astype(f32)
        mass = jnp.sum(weighted, axis=1, keepdims=True)
        top_mass = jnp.sum(weighted * in_top, axis=1, keepdims=True)
        rest = (weighted * (1.0 - in_top)).astype(bf16)
        carried.append(mm(rest, v[:, h * size : (h + 1) * size]))
        for value in (peak, mass, top_mass):
            extras.extend(parts3(value))
    spare = blocks * LANES - width
    block = jnp.concatenate(carried + [columns(spare, extras, cl_pad)], axis=1).astype(bf16)
    put_blocks(pay, 0, block, cl_rows)


def member_kernel(count, heads, size, cl_rows, lengths, *refs):
    pays = refs[:count]
    q, chosen_ref, hub_ref, prob_ref, top_ref = refs[count:]
    width = heads * size
    blocks = round_up(width + 1, LANES) // LANES
    hub = total_of(pays, blocks * cl_rows, HUBS, 2 * width // LANES).astype(bf16)
    hub_ref[...] = hub
    inv_root = size ** (-0.5)
    probs, outs = [], []
    for h in range(heads):
        keys = hub[:, h * size : (h + 1) * size]
        values = hub[:, width + h * size : width + (h + 1) * size]
        logits = mt(q[:, h * size : (h + 1) * size], keys) * inv_root
        chosen = chosen_ref[:, h * HUBS : (h + 1) * HUBS].astype(f32) > 0.5
        logits = jnp.where(chosen, logits, negative)
        exponent = jnp.where(
            chosen, jnp.exp(logits - jnp.max(logits, axis=1, keepdims=True)), 0.0
        )
        prob = exponent / jnp.sum(exponent, axis=1, keepdims=True)
        probs.append(prob)
        outs.append(mm(prob.astype(bf16), values))
    prob_ref[...] = jnp.concatenate(probs, axis=1)
    top_ref[...] = jnp.concatenate(outs, axis=1)


def combine_kernel(layer, count, heads, size, cl_rows, lengths, *refs):
    pays = refs[:count]
    top_out, members, mine, other, att_ref, top, low, stat_ref, w_out, sems = refs[count:]
    weights = Choice(layer, [(mine, other)], [w_out], [sems.at[0]])
    width = heads * size
    cl_pad = members.shape[2]
    blocks = round_up(width + 1, LANES) // LANES
    tables = [
        pad_rows(get_blocks(ref[...].astype(f32), 0, cl_rows, blocks), cl_pad) for ref in pays
    ]
    rows = top_out.shape[0]
    live = live_col(lengths, rows)
    pieces = []
    for h in range(heads):

        def value(one, which):
            at = width + 9 * h + 3 * which
            return one[:, at : at + 1] + one[:, at + 1 : at + 2] + one[:, at + 2 : at + 3]

        peaks = [value(one, 0) for one in tables]
        peak = functools.reduce(jnp.maximum, peaks)
        mass = top_mass = carried = 0.0
        for one, mine in zip(tables, peaks):
            scale = jnp.exp(mine - peak)
            mass = mass + value(one, 1) * scale
            top_mass = top_mass + value(one, 2) * scale
            carried = carried + one[:, h * size : (h + 1) * size] * scale
        safe = jnp.where(mass > 0, mass, 1.0)
        remote = carried / safe
        share = top_mass / safe
        lanes = LANES - size
        stat_ref[h] = jnp.concatenate(
            [carried, columns(lanes, (peak, safe, top_mass, share), cl_pad)], axis=1
        )
        looked = pick_rows(
            members[h], jnp.concatenate([remote, columns(lanes, (share,), cl_pad)], axis=1)
        )
        att = looked[:, size : size + 1] * top_out[:, h * size : (h + 1) * size] + looked[:, :size]
        pieces.append(jnp.where(live, att, 0.0))
    joined = jnp.concatenate(pieces, axis=1).astype(bf16)
    att_ref[...] = joined
    weights.wait(0)
    halves(mm(joined, w_out[...]), top, low)


def feed_kernel(layer, with_back, lengths, *refs):
    source, *four = refs[:5]
    gain_mine, gain_other, in_mine, in_other, back_mine, back_other = refs[5:11]
    if with_back:
        x1_ref, n2r, active_ref, slope_ref, top, low, w_in, w_back, sems = refs[11:]
        pairs = [(in_mine, in_other), (back_mine, back_other)]
        weights = Choice(layer, pairs, [w_in, w_back], [sems.at[0], sems.at[1]])
    else:
        x1_ref, n2r, active_ref, slope_ref, w_in, sems = refs[11:]
        weights = Choice(layer, [(in_mine, in_other)], [w_in], [sems.at[0]])
    x1 = source[here(SECTION)].astype(f32) if layer == 0 else source[...]
    x1 = x1 + summed(four)
    x1_ref[...] = x1
    hat, _ = layer_stats(x1)
    n2 = (hat * gain_row(gain_mine, gain_other, layer, 1)).astype(bf16)
    weights.wait(0)
    hidden = mm(n2, w_in[...])
    root = (2.0 / 3.141592653589793) ** 0.5
    square = hidden * hidden
    bent = jnp.tanh(root * hidden * (1.0 + 0.044715 * square))
    active = (0.5 * hidden * (1.0 + bent)).astype(bf16)
    active_ref[...] = active
    slope_ref[...] = 0.5 * (1.0 + bent) + 0.5 * hidden * (1.0 - bent * bent) * root * (
        1.0 + 3 * 0.044715 * square
    )
    if with_back:
        weights.wait(1)
        halves(mm(active, w_back[...]), top, low)
    n2r[...] = n2


def late_feed_kernel(layer, lengths, active, mine, other, top, low, w_back, sems):
    weights = Choice(layer, [(mine, other)], [w_back], [sems.at[0]])
    weights.wait(0)
    halves(mm(active[...], w_back[...]), top, low)


def pass_kernel(lengths, one, two, one_on, two_on):
    one_on[...] = one[...]
    two_on[...] = two[...]


def add_kernel(lengths, source, *refs):
    refs[-1][...] = source[...] + summed(refs[:4])


def feed_back_kernel(layer, lengths, *refs):
    if layer == 1:
        cot, slope = refs[:2]
        refs = refs[2:]
    else:
        grad_middle, source, *four = refs[:6]
        gain = gain_row(*refs[6:8], layer + 1, 0)
        slope = refs[8]
        refs = refs[9:]
    weights = Choice(
        layer, [refs[:2], refs[2:4]], refs[-3:-1], [refs[-1].at[0], refs[-1].at[1]]
    )
    w_back, w_in = refs[-3:-1]
    dybr, dz_ref, top, low = refs[-7:-3]
    if layer == 1:
        dyb = cot[here(SECTION)]
    else:
        dy_ref, gain_ref = refs[4:6]
        dy = input_grad(grad_middle, source[...], four, gain, gain_ref)
        dy_ref[...] = dy
        dyb = dy.astype(bf16)
    weights.wait(0)
    dz = (mt(dyb, w_back[...]) * slope[...]).astype(bf16)
    dz_ref[...] = dz
    weights.wait(1)
    halves(mt(dz, w_in[...]), top, low)
    dybr[...] = dyb


def input_grad(grad_middle, source, four, gain, gain_ref):
    grad_normed = summed(four)
    hat, inverse = layer_stats(source)
    if gain_ref is not None:
        gain_ref[...] = jnp.sum(grad_normed * hat, axis=0, keepdims=True)
    return grad_middle[...] + norm_back(grad_normed * gain, hat, inverse)


def input_grad_kernel(lengths, *refs):
    grad_middle, source, *four = refs[:6]
    *gains, gain_two, last_one, last_two, sent, keep, gain_one = refs[6:]
    source = source[here(SECTION)].astype(f32)
    rows = source.shape[0]
    sent[:rows, :] = input_grad(grad_middle, source, four, gain_row(*gains, 0, 0), gain_one)
    first = jnp.concatenate([gain_one[...], gain_two[...]], axis=0)
    last = jnp.concatenate([last_one[...], last_two[...]], axis=0)
    keep[...] = jnp.where(here(SECTION) == 0, first, last)
    give = jnp.where(here(SECTION) == 0, last, first)
    sent[rows:, :] = jnp.concatenate([give, jnp.zeros((6, give.shape[1]), f32)], axis=0)


def middle_back_kernel(layer, heads, size, cl_rows, lengths, *refs):
    four = refs[:4]
    middle, grad_out, gain_mine, gain_other, top_out, members_t = refs[4:10]
    mine, other, dx1_ref, dx1r, dtop_ref, gain_ref, pay, w_out, sems = refs[10:]
    weights = Choice(layer, [(mine, other)], [w_out], [sems.at[0]])
    grad_normed = summed(four)
    hat, inverse = layer_stats(middle[...])
    gain_ref[...] = jnp.sum(grad_normed * hat, axis=0, keepdims=True)
    grad = grad_out[here(SECTION)].astype(f32) if layer == 1 else grad_out[...]
    dx1 = grad + norm_back(
        grad_normed * gain_row(gain_mine, gain_other, layer, 1), hat, inverse
    )
    dx1_ref[...] = dx1
    dx1b = dx1.astype(bf16)
    rows = dx1.shape[0]
    weights.wait(0)
    datt = mt(dx1b, w_out[...])
    dtop = jnp.where(live_col(lengths, rows), datt, 0.0).astype(bf16)
    dtop_ref[...] = dtop
    sums, shares = [], []
    for h in range(heads):
        members = members_t[h]
        own = dtop[:, h * size : (h + 1) * size]
        sums.append(mm(members, own))
        product = own.astype(f32) * top_out[:, h * size : (h + 1) * size]
        both = mm(members, jnp.concatenate(parts2(product), axis=1))
        shares.extend(parts3(jnp.sum(both, axis=1, keepdims=True)))
    width = heads * size
    spare = round_up(width + 1, LANES) - width
    cl_pad = members_t.shape[1]
    block = jnp.concatenate(sums + [columns(spare, shares, cl_pad)], axis=1).astype(bf16)
    put_blocks(pay, 0, block, cl_rows)
    dx1r[...] = dx1b


def member_back_kernel(heads, size, lengths, *refs):
    q, hub_ref, prob_ref, dtop, stat, members, dq_ref, pay = refs
    width = heads * size
    inv_root = size ** (-0.5)
    hub = hub_ref[...]
    dqs, dks, dvs = [], [], []
    for h in range(heads):
        keys = hub[:, h * size : (h + 1) * size]
        values = hub[:, width + h * size : width + (h + 1) * size]
        prob = prob_ref[:, h * HUBS : (h + 1) * HUBS]
        own = dtop[:, h * size : (h + 1) * size]
        share = pick_rows(members[h], stat[h])[:, size + 3 : size + 4]
        da = mt(own, values) * share
        dg = (prob * (da - jnp.sum(prob * da, axis=1, keepdims=True))).astype(bf16)
        dqs.append(mm(dg, keys) * inv_root)
        dks.append(tm(dg, q[:, h * size : (h + 1) * size]) * inv_root)
        scaled = own.astype(f32) * share
        dvs.append(tm(prob.astype(bf16), scaled.astype(bf16)))
    dq_ref[...] = jnp.concatenate(dqs, axis=1)
    put_blocks(pay, 0, jnp.concatenate(dks + dvs, axis=1).astype(bf16), HUBS)


def centroid_back_kernel(count, heads, size, cl_rows, lengths, *refs):
    pays = refs[:count]
    centre_ref, stat, k, v, in_tops, hub_pay, pay, dk_ref, dv_ref = refs[count:]
    width = heads * size
    cl_pad = in_tops.shape[1]
    blocks = round_up(width + 1, LANES) // LANES
    total = pad_rows(total_of(pays, 0, cl_rows, blocks), cl_pad)
    rows = k.shape[0]
    live = live_row(lengths, rows)
    inv_root = size ** (-0.5)
    dcs, dks, dvs = [], [], []
    for h in range(heads):
        keys = k[:, h * size : (h + 1) * size]
        values = v[:, h * size : (h + 1) * size]
        centre = centre_ref[h]
        grad_remote = total[:, h * size : (h + 1) * size]
        at = width + 3 * h
        grad_share = total[:, at : at + 1] + total[:, at + 1 : at + 2] + total[:, at + 2 : at + 3]
        carried = stat[h][:, :size]
        peak = stat[h][:, size : size + 1]
        mass = stat[h][:, size + 1 : size + 2]
        top_mass = stat[h][:, size + 2 : size + 3]
        grad_carried = (grad_remote / mass).astype(bf16)
        grad_top = grad_share / mass
        grad_mass = -(
            jnp.sum(grad_remote * carried, axis=1, keepdims=True) + grad_share * top_mass
        ) / (mass * mass)
        scores = mt(centre, keys) * inv_root
        weighted = jnp.where(live, jnp.exp(jnp.where(live, scores - peak, 0.0)), 0.0)
        in_top = in_tops[h].astype(f32)
        rest = (weighted * (1.0 - in_top)).astype(bf16)
        grad_weighted = (
            (1.0 - in_top) * mt(grad_carried, values) + in_top * grad_top + grad_mass
        )
        grad_scores = (grad_weighted * weighted).astype(bf16)
        dcs.append(mm(grad_scores, keys) * inv_root)
        dks.append(tm(grad_scores, centre) * inv_root)
        dvs.append(tm(rest, grad_carried))
    spare = blocks * LANES - width
    block = jnp.concatenate(dcs + [jnp.zeros((cl_pad, spare), f32)], axis=1).astype(bf16)
    put_blocks(pay, 0, block, cl_rows)
    pay[blocks * cl_rows :, :] = hub_pay[...]
    dk_ref[...] = jnp.concatenate(dks, axis=1)
    dv_ref[...] = jnp.concatenate(dvs, axis=1)


def project_back_kernel(layer, count, heads, size, cl_rows, lengths, *refs):
    pays = refs[:count]
    dq_top, dk_c, dv_c, cnt_ref, members, own_pick, mine, other = refs[count : count + 8]
    dqkv_ref, top, low, w_qkv, sems = refs[count + 8 :]
    weights = Choice(layer, [(mine, other)], [w_qkv], [sems.at[0]])
    width = heads * size
    cl_pad = members.shape[2]
    blocks = round_up(width + 1, LANES) // LANES
    total = pad_rows(total_of(pays, 0, cl_rows, blocks), cl_pad)
    hub = total_of(pays, blocks * cl_rows, HUBS, 2 * width // LANES)
    high, low_part = parts2(hub)
    spread = tm(own_pick[...], high) + tm(own_pick[...], low_part)
    rows = dq_top.shape[0]
    live = live_col(lengths, rows)
    base = round_up(width + 1, LANES) - LANES
    dqs = []
    for h in range(heads):
        at = width - base + h
        cnt = jnp.maximum(cnt_ref[:, at : at + 1], 1.0)
        from_centre = pick_rows(members[h], total[:, h * size : (h + 1) * size] / cnt)
        dqs.append(jnp.where(live, from_centre, 0.0))
    dq = (dq_top[...] + jnp.concatenate(dqs, axis=1)).astype(bf16)
    dk = (dk_c[...] + spread[:, :width]).astype(bf16)
    dv = (dv_c[...] + spread[:, width:]).astype(bf16)
    dqkv_ref[...] = jnp.concatenate([dq, dk, dv], axis=1)
    weights.wait(0)
    halves(mm(dq, w_qkv[0]) + mm(dk, w_qkv[1]) + mm(dv, w_qkv[2]), top, low)


def feed_grads_kernel(lengths, dyb, active, n2, dz, keep, give):
    back = tm(dyb[...], active[...]).astype(bf16)
    into = tm(n2[...], dz[...]).astype(bf16)

    @pl.when(here(SECTION) == 0)
    def _():
        keep[...] = back
        give[...] = into

    @pl.when(here(SECTION) == 1)
    def _():
        keep[...] = into
        give[...] = back


def attention_grads_kernel(count, lengths, n1, dqkv, dx1b, att, keep, give):
    part = n1.shape[1] // count
    half = part // 2
    both = jnp.concatenate([tm(n1[...], dqkv[...]), tm(dx1b[...], att[...])], axis=1).astype(bf16)

    def put(ref, first):
        for at in range(count):
            ref[at] = both[at * part + first : at * part + first + half]

    @pl.when(here(SECTION) == 0)
    def _():
        put(keep, 0)
        put(give, half)

    @pl.when(here(SECTION) == 1)
    def _():
        put(keep, half)
        put(give, 0)


def chip_sum_kernel(lengths, mine, far, keep, give):
    me = here(SEQ)
    for at in range(keep.shape[0]):
        stay, go = 2 * at + me % 2, 2 * at + 1 - me % 2
        keep[at] = (mine[stay].astype(f32) + far[stay].astype(f32)).astype(bf16)
        give[at] = (mine[go].astype(f32) + far[go].astype(f32)).astype(bf16)


def two_chip_sums_kernel(lengths, first, first_far, last, last_far, keep, give):
    me = here(SEQ)
    half = first.shape[1]
    for at in range(keep.shape[0]):
        stay, go = 2 * at + me % 2, 2 * at + 1 - me % 2
        for layer, (mine, far) in enumerate(((first, first_far), (last, last_far))):
            rows = slice(layer * half, (layer + 1) * half)
            keep[at, rows, :] = (mine[stay].astype(f32) + far[stay].astype(f32)).astype(bf16)
            give[at, rows, :] = (mine[go].astype(f32) + far[go].astype(f32)).astype(bf16)


def two_seq_sums_kernel(lengths, mine, far, own, other):
    total = mine[...].astype(f32) + far[...].astype(f32)
    half = own.shape[0]
    first = here(SECTION) == 0
    own[...] = jnp.where(first, total[:half], total[half:])
    other[...] = jnp.where(first, total[half:], total[:half])


def pair_sum_kernel(lengths, mine, far, keep, give):
    stay = here(SEQ) // 2
    go = 1 - stay
    keep[...] = (mine[stay].astype(f32) + far[stay].astype(f32)).astype(bf16)
    give[...] = (mine[go].astype(f32) + far[go].astype(f32)).astype(bf16)


def sorted_sum_kernel(lengths, mine, far, *outs):
    for k, out in enumerate(outs):
        at = lax.rem(here(SEQ) + k, len(outs))
        out[...] = (mine[at].astype(f32) + far[at].astype(f32)).astype(bf16)


def seq_sum_kernel(lengths, *refs):
    total = refs[0][...].astype(f32)
    for ref in refs[1:-1]:
        total = total + ref[...].astype(f32)
    refs[-1][...] = total


def feed_owner_kernel(lengths, first, last, first_far, last_far, back, into):
    @pl.when(here(SECTION) == 0)
    def _():
        back[...] = first[...]
        into[...] = first_far[...]

    @pl.when(here(SECTION) == 1)
    def _():
        into[...] = last[...]
        back[...] = last_far[...]


def attention_owner_kernel(width, lengths, own, far, grad_qkv, grad_out):
    def put(low_half, high_half):
        both = jnp.concatenate([low_half[...], high_half[...]], axis=0)
        for at in range(3):
            grad_qkv[at] = both[:, at * width : (at + 1) * width]
        grad_out[...] = both[:, 3 * width :].T

    @pl.when(here(SECTION) == 0)
    def _():
        put(own, far)

    @pl.when(here(SECTION) == 1)
    def _():
        put(far, own)


def place_kernel(lengths, own_first, own_last, far_first, far_last, out):
    @pl.when(here(SECTION) == 0)
    def _():
        out[0] = own_first[...]
        out[1] = far_first[...]

    @pl.when(here(SECTION) == 1)
    def _():
        out[0] = far_last[...]
        out[1] = own_last[...]


def gain_kernel(lengths, keep, sent_far, out):
    rows = sent_far.shape[0] - 8
    out[...] = keep[...] + sent_far[rows : rows + 2, :]


def place_last_kernel(lengths, sent, own_last, sent_far, far_last, out):
    rows = own_last.shape[0]

    @pl.when(here(SECTION) == 0)
    def _():
        out[0] = sent[:rows, :]
        out[1] = sent_far[:rows, :]

    @pl.when(here(SECTION) == 1)
    def _():
        out[0] = far_last[...]
        out[1] = own_last[...]


def moved(block, axis, target):
    devices = range(lax.axis_size(axis))
    return lax.ppermute(block, axis, [(i, target(i)) for i in devices])


def swap(block):
    return moved(block, SECTION, lambda i: i ^ 1)


def every_seq(block):
    count = lax.axis_size(SEQ)
    if count > DIRECT:
        gathered = lax.all_gather(block, SEQ)
        return [gathered[at] for at in range(count)]
    return [block] + [
        moved(block, SEQ, lambda i, k=k: (i + k) % count) for k in range(1, count)
    ]


def every_head(block):
    return [block] + [
        moved(block, HEAD, lambda i, k=k: i ^ k) for k in range(1, lax.axis_size(HEAD))
    ]


def every_head_in_turn(block):
    pieces = [block]
    distance = 1
    while distance < lax.axis_size(HEAD):
        pieces += [moved(piece, HEAD, lambda i: i ^ distance) for piece in pieces]
        distance *= 2
    return pieces


def fold_kernel(lengths, top_a, top_b, low_a, low_b, top, low):
    top[...] = (top_a[...].astype(f32) + top_b[...].astype(f32)).astype(bf16)
    low[...] = (low_a[...].astype(f32) + low_b[...].astype(f32)).astype(bf16)


def head_sum(top, low, run, before_fold=None):
    distances = [1 << at for at in range(lax.axis_size(HEAD).bit_length() - 1)]
    for step in range(len(distances)):
        one = distances[step]
        other = distances[len(distances) - 1 - step]
        far_top = moved(top, HEAD, lambda i: i ^ one)
        far_low = moved(low, HEAD, lambda i: i ^ other)
        if step < len(distances) - 1:
            ties = before_fold() if before_fold and step == 0 else []
            shape = [shaped(top.shape, bf16)] * 2
            top, low = run(
                fold_kernel, shape, [top, far_top, low, far_low], ties=ties
            )
    return (top, far_top, low, far_low)


def to_core(block, layer):
    return lax.ppermute(block, SECTION, [(1 - layer, layer)])


def seq_xor(block, distance):
    return moved(block, SEQ, lambda i: i ^ distance)


def pair_step(keep, far, run, ties=()):
    half = shaped((keep.shape[0] // 2,) + keep.shape[1:], bf16)
    keep, give = run(chip_sum_kernel, [half] * 2, [keep, far], ties=ties)
    return keep, seq_xor(give, 1)


def far_step(keep, far, run, ties=()):
    keep, give = run(
        pair_sum_kernel, [shaped(keep.shape[1:], bf16)] * 2, [keep, far], ties=ties
    )
    return keep, seq_xor(give, 2)


def shards(tokens, cotangent, lengths, clusters, top_index, w_qkv, w_out, w_in, w_back, gains):
    section = lax.axis_index(SECTION)
    me = lax.axis_index(SEQ)
    count = lax.axis_size(SEQ)
    head_devices = lax.axis_size(HEAD)
    micro, rows, dim = tokens.shape
    _, heads, cluster_count, slots = top_index.shape
    size = w_qkv.shape[3] // heads
    width = heads * size
    hidden = w_in.shape[2]
    total_rows = rows * count
    cl_pad = round_up(cluster_count, LANES)
    cl_rows = round_up(cluster_count, 16)
    high_rows = round_up(max(total_rows // LANES, 1), 16)
    blocks = round_up(width + 1, LANES) // LANES
    hub_blocks = 2 * width // LANES
    sizes = (heads, size, cl_rows)
    run = lambda kernel, outs, args, **kw: call(kernel, outs, lengths, args, **kw)
    part = functools.partial
    fours = [shaped((rows // 2, dim), bf16)] * 2
    pay_shape = shaped((blocks * cl_rows, LANES), bf16)
    table_shape = shaped((heads, cl_pad, rows), bf16)
    square = shaped((dim, hidden), bf16)
    qkv_buf = shaped((3, width, dim), bf16)

    qkv_t = w_qkv[0].transpose(0, 2, 1)
    qkv_pair = (qkv_t, swap(qkv_t))
    gain_pair = (gains[0], swap(gains[0]))
    tops = top_index.transpose(0, 1, 3, 2)
    clusters = clusters.transpose(1, 0, 2)
    out_pair = (w_out[0], swap(w_out[0]))
    in_pair = (w_in[0], swap(w_in[0]))
    back_pair = (w_back[0], swap(w_back[0]))
    own_pick, hubs, members_t = run(
        part(rank_kernel, heads, cl_pad),
        [shaped((HUBS, rows), bf16), shaped((high_rows, LANES)), table_shape],
        [tops, clusters],
    )

    source, lists = tokens, None
    kept, acts = [], []
    for layer in range(2):
        outs = [
            shaped((rows, dim), bf16),
            shaped((rows, width), bf16),
            shaped((rows, width), bf16),
            shaped((rows, width), bf16),
            shaped((blocks * cl_rows + hub_blocks * HUBS, LANES), bf16),
        ]
        if layer:
            outs = [shaped((rows, dim))] + outs
        found = run(
            part(project_kernel, layer, *sizes),
            outs,
            ([tokens] if layer == 0 else [x1, *four])
            + [*gain_pair, members_t, own_pick]
            + list(qkv_pair) * (layer == 0),
            anys=() if layer == 0 else qkv_pair,
            bufs=[] if layer == 0 else [qkv_buf],
        )
        if layer:
            source, *found = found
            acts.append(source)
            acts_far = to_core(source, 0)
        n1r, q, k, v, pay = found
        pays = every_seq(pay)
        if lists is None:
            in_tops, chosen, members = lists = run(
                part(list_kernel, heads, cl_pad),
                [
                    table_shape,
                    shaped((rows, heads * HUBS), bf16),
                    shaped((heads, rows, cl_pad), bf16),
                ],
                [tops, clusters, hubs, own_pick],
            )
        centre, cnt, pay = run(
            part(centroid_kernel, len(pays), *sizes),
            [shaped((heads, cl_pad, size), bf16), shaped((cl_pad, LANES)), pay_shape],
            [*pays, k, v, in_tops],
        )
        stats = every_seq(pay)
        hub, prob, top_out = run(
            part(member_kernel, len(pays), *sizes),
            [
                shaped((HUBS, 2 * width), bf16),
                shaped((rows, heads * HUBS)),
                shaped((rows, width)),
            ],
            [*pays, q, chosen],
            ties=[in_pair[1]] if layer == 0 else [acts_far],
        )
        att, top, low, stat = run(
            part(combine_kernel, layer, len(stats), *sizes),
            [shaped((rows, width), bf16)] + fours + [shaped((heads, cl_pad, LANES))],
            [*stats, top_out, members],
            anys=out_pair,
            bufs=[shaped((width, dim), bf16)],
        )
        four = head_sum(top, low, run)
        with_back = layer == 0
        found = run(
            part(feed_kernel, layer, with_back),
            [
                shaped((rows, dim)),
                shaped((rows, dim), bf16),
                shaped((rows, hidden), bf16),
                shaped((rows, hidden)),
            ]
            + fours * with_back,
            [source, *four, *gain_pair],
            anys=[*in_pair, *back_pair],
            bufs=[square] + [square] * with_back,
        )
        x1, n2r, active, slope = found[:4]
        if with_back:
            four = head_sum(*found[4:], run)
        kept.append(
            (source, n1r, q, k, v, centre, cnt, hub, prob, top_out, att, stat, x1, n2r, active, slope)
        )

    direct = count == DIRECT
    seq_part = dim // count
    half = seq_part // 2
    extra = 16
    if not direct:
        seq_part = half = None

    def plain_sum(grad, layer):
        total = grad.astype(f32) + to_core(grad.astype(bf16), layer).astype(f32)
        return lax.psum_scatter(
            total.astype(bf16), SEQ, scatter_dimension=0, tiled=True
        ).astype(f32)

    def feed_grads(layer, dyb, dz, ties=()):
        active, n2 = kept[layer][14], kept[layer][13]
        if not direct:
            return plain_sum(tm(dyb, active), layer), plain_sum(tm(n2, dz), layer)
        return run(
            feed_grads_kernel, [square] * 2, [dyb, active, n2, dz], ties=ties
        )

    def attention_grads(layer, dqkv, dx1b):
        n1, att = kept[layer][1], kept[layer][10]
        if not direct:
            return plain_sum(jnp.concatenate([tm(n1, dqkv), tm(dx1b, att)], axis=1), layer)
        return run(
            part(attention_grads_kernel, count),
            [shaped((count, half, 4 * width), bf16)] * 2,
            [n1, dqkv, dx1b, att],
        )

    def swapped(made):
        far = swap(made[1])
        shape = (count, -1, made[0].shape[-1])
        return made[0].reshape(shape), far.reshape(shape)

    def middle_back(layer, four, dy, ties):
        top_out, x1 = kept[layer][9], kept[layer][12]
        return run(
            part(middle_back_kernel, layer, *sizes),
            [
                shaped((rows, dim)),
                shaped((rows, dim), bf16),
                shaped((rows, width), bf16),
                shaped((1, dim)),
                pay_shape,
            ],
            [*four, x1, dy, *gain_pair, top_out, members_t],
            anys=out_pair,
            bufs=[shaped((width, dim), bf16)],
            ties=ties,
        )

    def member_back(layer, dtop, ties=()):
        _, _, q, _, _, _, _, hub, prob, _, _, stat = kept[layer][:12]
        return run(
            part(member_back_kernel, heads, size),
            [shaped((rows, width)), shaped((hub_blocks * HUBS, LANES), bf16)],
            [q, hub, prob, dtop, stat, members],
            ties=ties,
        )

    def centroid_back(layer, pays, hub_pay, ties):
        _, _, _, k, v, centre, _, _, _, _, _, stat = kept[layer][:12]
        return run(
            part(centroid_back_kernel, len(pays), *sizes),
            [
                shaped((blocks * cl_rows + hub_blocks * HUBS, LANES), bf16),
                shaped((rows, width)),
                shaped((rows, width)),
            ],
            [*pays, centre, stat, k, v, in_tops, hub_pay],
            ties=ties,
        )

    def project_back(layer, pays, dq_top, dk, dv, ties):
        cnt = kept[layer][6]
        return run(
            part(project_back_kernel, layer, len(pays), *sizes),
            [shaped((rows, 3 * width), bf16)] + fours,
            [*pays, dq_top, dk, dv, cnt, members, own_pick],
            anys=qkv_pair,
            bufs=[qkv_buf],
            ties=ties,
        )

    def shared(pay):
        return every_seq(pay)

    def step(parts, axis, one, other):
        return [parts[0], moved(parts[0], axis, lambda i: i ^ one),
                    parts[1], moved(parts[1], axis, lambda i: i ^ other)]

    def fold(four, ties):
        return run(fold_kernel, fours, four, ties=ties)

    near, away = 1, head_devices // 2
    assert head_devices == 4
    only = lambda items: list(items) if direct else []

    backs = [shaped((rows, dim), bf16), shaped((rows, hidden), bf16)] + fours
    dyb, dz, *parts = run(
        part(feed_back_kernel, 1),
        backs,
        [cotangent, kept[1][15]],
        anys=[*back_pair, *in_pair],
        bufs=[square, square],
    )
    four = step(parts, HEAD, near, away)
    parts = fold(four, [])
    four = step(parts, HEAD, away, near)
    dx1, dx1b, dtop, gain_two, pay = middle_back(1, four, cotangent, [])
    feed_last = feed_grads(1, dyb, dz, [dtop])
    pays = shared(pay)
    dq_top, hub_pay = member_back(1, dtop)
    pay, dk, dv = centroid_back(1, pays, hub_pay, only(feed_last))
    if direct:
        feed_last = swapped(feed_last)
    late_parts = run(
        part(late_feed_kernel, 1),
        fours,
        [kept[1][14]],
        anys=back_pair,
        bufs=[square],
        ties=pays[1:] + [hub_pay],
    )
    late = step(late_parts, HEAD, near, away)
    pays = shared(pay)
    dqkv, *parts = project_back(
        1, pays, dq_top, dk, dv, [late[1], late[3]] + only(feed_last[1:])
    )
    four = step(parts, HEAD, near, away)
    if direct:
        feed_last = pair_step(*feed_last, run, [dqkv])
    parts = fold(four, only(feed_last[:1]))
    four = step(parts, HEAD, away, near)
    attention_last = attention_grads(1, dqkv, dx1b)
    if direct:
        feed_last = far_step(*feed_last, run)
    dy, gain_one, dyb, dz, *parts = run(
        part(feed_back_kernel, 0),
        [shaped((rows, dim)), shaped((1, dim))] + backs,
        [dx1, kept[1][0], *four, *gain_pair, kept[0][15]],
        anys=[*back_pair, *in_pair],
        bufs=[square, square],
        ties=only([feed_last[0], *attention_last]),
    )
    last_grad, last_gains = dy, [gain_one, gain_two]
    four = step(parts, HEAD, near, away)
    if direct:
        attention_last = swapped(attention_last)
    parts = fold(four, only([attention_last[1], feed_last[1]]))
    four = step(parts, HEAD, away, near)
    feed_first = feed_grads(0, dyb, dz, parts)
    dx1, dx1b, dtop, gain_two, pay = middle_back(
        0, four, dy, only(feed_first)
    )
    pays = shared(pay)
    dq_top, hub_pay = member_back(0, dtop)
    last_grad_far = to_core(last_grad, 1)
    if direct:
        feed_first = swapped(feed_first)
    pay, dk, dv = centroid_back(0, pays, hub_pay, only(feed_first[1:]))
    late_parts = fold(late, [dk])
    late = step(late_parts, HEAD, away, near)
    pays = shared(pay)
    dqkv, *parts = project_back(
        0, pays, dq_top, dk, dv, [late[1], late[3]]
    )
    four = step(parts, HEAD, near, away)
    attention_first = attention_grads(0, dqkv, dx1b)
    if direct:
        feed_first = pair_step(*feed_first, run, [dqkv])
    parts = fold(four, only([*attention_first, feed_first[1]]) + [last_grad_far])
    if direct:
        feed_first = far_step(*feed_first, run)
    four = step(parts, HEAD, away, near)
    (last_act,) = run(
        add_kernel, [shaped((rows, dim))], [kept[1][12], *late], ties=parts
    )
    last_act_far = to_core(last_act, 1)
    keep = []
    if direct:
        attention_first = swapped(attention_first)
        both_half = [shaped((count // 2, 2 * half, 4 * width), bf16)] * 2
        keep, give = run(
            two_chip_sums_kernel, both_half, [*attention_first, *attention_last]
        )
        attention = [keep, seq_xor(give, 1)]
    sent, own_gains, _ = run(
        input_grad_kernel,
        [shaped((rows + 8, dim)), shaped((2, dim)), shaped((1, dim))],
        [dx1, tokens, *four, *gain_pair, gain_two, *last_gains],
        ties=only([keep]) + [last_act_far],
    )
    sent_far = swap(sent)
    (placed_acts,) = run(
        place_kernel,
        [shaped((2, rows, dim))],
        [acts[0], last_act, acts_far, last_act_far],
    )
    (placed_grads,) = run(
        place_last_kernel,
        [shaped((2, rows, dim))],
        [sent, last_grad, sent_far, last_grad_far],
    )
    (gain_sum,) = run(gain_kernel, [shaped((2, dim))], [own_gains, sent_far])
    if direct:
        attention = far_step(*attention, run)
        gain_all = every_seq(gain_sum)
        gain_sum = sum(gain_all)
        gain_sum = lax.dynamic_slice_in_dim(gain_sum, me * seq_part, seq_part, 1)
        ended = []
        for layer, group in enumerate((feed_first, feed_last)):
            (total,) = run(
                seq_sum_kernel, [shaped(group[0].shape)], group
            )
            ended += [total, to_core(total, layer)]
        back, into = run(
            feed_owner_kernel,
            [shaped((seq_part, hidden))] * 2,
            [ended[0], ended[2], ended[1], ended[3]],
        )
        own, other = run(
            two_seq_sums_kernel,
            [shaped((half, 4 * width))] * 2,
            attention,
            ties=[placed_acts, placed_grads, back, *gain_all],
        )
        other = swap(other)
        grad_qkv, grad_out = run(
            part(attention_owner_kernel, width),
            [shaped((3, seq_part, width)), shaped((width, seq_part))],
            [own, other],
        )
    else:
        pick = lambda one, two: jnp.where(section == 0, one, two)
        gain_sum = lax.psum_scatter(gain_sum, SEQ, scatter_dimension=1, tiled=True)
        back, into = (pick(feed_first[at], feed_last[at]) for at in range(2))
        both = pick(attention_first, attention_last)
        grad_qkv = both[:, : 3 * width].reshape(-1, 3, width).transpose(1, 0, 2)
        grad_out = both[:, 3 * width :].T
    return (
        placed_acts[None],
        placed_grads[None],
        grad_qkv[None],
        grad_out[None],
        into[None],
        back.T[None],
        gain_sum[None],
    )


def solution(mesh):
    placed = (
        P(None, SEQ, None),
        P(None, SEQ, None),
        P(),
        P(None, HEAD, SEQ),
        P(None, HEAD, None, None),
        P(SECTION, None, None, HEAD),
        P(SECTION, HEAD, None),
        P(SECTION, None, HEAD),
        P(SECTION, HEAD, None),
        P(SECTION, None, None),
    )
    return jax.shard_map(
        shards,
        mesh=mesh,
        in_specs=placed,
        out_specs=(
            P(SECTION, None, SEQ, None),
            P(SECTION, None, SEQ, None),
            P(SECTION, None, SEQ, HEAD),
            P(SECTION, HEAD, SEQ),
            P(SECTION, SEQ, HEAD),
            P(SECTION, HEAD, SEQ),
            P(SECTION, None, SEQ),
        ),
        check_vma=False,
    )
```

```python
import functools

import jax
import jax.numpy as jnp
from jax import lax
from jax.experimental import pallas as pl
from jax.experimental.pallas import tpu as pltpu
from jax.sharding import PartitionSpec as P

SECTION, SEQ, HEAD = "section", "seq", "head"
epsilon = 1e-05
negative = -1e30
f32 = jnp.float32
bf16 = jnp.bfloat16
LANES = 128
HUBS = 64
VMEM_LIMIT = 32 * 1024 * 1024
DIRECT = 4


def round_up(value, step):
    return -(-value // step) * step


def iota(shape, dim):
    return lax.broadcasted_iota(jnp.int32, shape, dim)


def mm(a, b):
    return lax.dot_general(a, b, (((1,), (0,)), ((), ())), preferred_element_type=f32)


def mt(a, b):
    return lax.dot_general(a, b, (((1,), (1,)), ((), ())), preferred_element_type=f32)


def tm(a, b):
    return lax.dot_general(a, b, (((0,), (0,)), ((), ())), preferred_element_type=f32)


def parts2(v):
    high = v.astype(bf16)
    return high, (v - high.astype(f32)).astype(bf16)


def parts3(v):
    high = v.astype(bf16)
    rest = v - high.astype(f32)
    mid = rest.astype(bf16)
    return high.astype(f32), mid.astype(f32), rest - mid.astype(f32)


def pick_rows(one_hot, table):
    high, low = parts2(table)
    return mm(one_hot, high) + mm(one_hot, low)


def layer_stats(values):
    centred = values - jnp.mean(values, axis=-1, keepdims=True)
    inverse = lax.rsqrt(jnp.mean(centred * centred, axis=-1, keepdims=True) + epsilon)
    return centred * inverse, inverse


def norm_back(grad_hat, normed, inverse):
    return inverse * (
        grad_hat
        - jnp.mean(grad_hat, axis=-1, keepdims=True)
        - normed * jnp.mean(grad_hat * normed, axis=-1, keepdims=True)
    )


def columns(base_width, cols, rows):
    lane = iota((rows, base_width), 1)
    out = jnp.zeros((rows, base_width), f32)
    for at, col in enumerate(cols):
        out = jnp.where(lane == at, col, out)
    return out


def here(name):
    return lax.axis_index(name)


def live_row(lengths, rows):
    return (here(SEQ) * rows + iota((1, rows), 1)) < lengths[here(SECTION)]


def live_col(lengths, rows):
    return (here(SEQ) * rows + iota((rows, 1), 0)) < lengths[here(SECTION)]


def gain_row(mine, other, layer, row):
    return jnp.where(
        here(SECTION) == layer,
        mine[row : row + 1, :].astype(f32),
        other[row : row + 1, :].astype(f32),
    )


class Choice:
    def __init__(self, layer, pairs, bufs, sems):
        self.copies = [
            (pltpu.make_async_copy(mine, buf, sem), pltpu.make_async_copy(other, buf, sem))
            for (mine, other), buf, sem in zip(pairs, bufs, sems)
        ]
        mine_here = here(SECTION) == layer

        @pl.when(mine_here)
        def _():
            for mine, _other in self.copies:
                mine.start()

        @pl.when(jnp.logical_not(mine_here))
        def _():
            for _mine, other in self.copies:
                other.start()

    def wait(self, at):
        self.copies[at][0].wait()


def summed(four):
    top_a, top_b, low_a, low_b = four
    return jnp.concatenate(
        [
            top_a[...].astype(f32) + top_b[...].astype(f32),
            low_a[...].astype(f32) + low_b[...].astype(f32),
        ],
        axis=0,
    )


def halves(values, top, low):
    half = values.shape[0] // 2
    top[...] = values[:half].astype(bf16)
    low[...] = values[half:].astype(bf16)


def call(kernel, outs, lengths, args, anys=(), bufs=(), ties=(), sems=None, outs_any=False):
    vmem = pl.BlockSpec(memory_space=pltpu.VMEM)
    anywhere = pl.BlockSpec(memory_space=pl.ANY)
    args, anys, ties = list(args), list(anys), list(ties)
    moved_bytes = sum(a.size * a.dtype.itemsize for a in args + list(outs) + list(bufs))
    first, last = 1 + len(args) + len(anys), 1 + len(args) + len(anys) + len(ties)

    def body(*refs):
        kernel(*refs[:first], *refs[last:])

    scratch = [pltpu.VMEM(b.shape, b.dtype) for b in bufs]
    if bufs or sems:
        scratch.append(pltpu.SemaphoreType.DMA((sems or len(bufs),)))
    whole = kernel.func if isinstance(kernel, functools.partial) else kernel
    with jax.named_scope(whole.__name__):
        return pl.pallas_call(
            body,
            out_shape=outs,
            in_specs=[pl.BlockSpec(memory_space=pltpu.SMEM)]
            + [vmem] * len(args)
            + [anywhere] * (len(anys) + len(ties)),
            out_specs=[anywhere if outs_any else vmem] * len(outs),
            scratch_shapes=scratch,
            compiler_params=pltpu.CompilerParams(vmem_limit_bytes=VMEM_LIMIT),
            cost_estimate=pl.CostEstimate(
                flops=0, bytes_accessed=moved_bytes, transcendentals=0
            ),
        )(lengths, *args, *anys, *ties)


def shaped(shape, dtype=f32):
    return jax.ShapeDtypeStruct(tuple(shape), dtype)


def named_rows(tops, head, clusters_pad):
    section = here(SECTION)
    slots, clusters = tops.shape[2:]
    rows = tops[section, head]
    if clusters < clusters_pad:
        rows = jnp.concatenate(
            [rows, jnp.full((slots, clusters_pad - clusters), -1, jnp.int32)], axis=1
        )
    return jnp.concatenate([rows[at : at + 1, :] for at in range(slots)], axis=1)


def cluster_row(clusters, head):
    return clusters[head, pl.ds(here(SECTION), 1), :]


def rank_kernel(heads, cl_pad, lengths, tops, clusters, own_pick, hubs, members_t):
    rows = own_pick.shape[1]
    high_rows = hubs.shape[0]
    named = None
    for h in range(heads):
        position = named_rows(tops, h, cl_pad)
        entries = position.shape[1]
        high_hot = (iota((high_rows, entries), 0) == position // LANES).astype(f32).astype(bf16)
        low_hot = (iota((LANES, entries), 0) == position % LANES).astype(f32).astype(bf16)
        found = mt(high_hot, low_hot)
        named = found if named is None else named + found
    named = named > 0.5
    mask = named.astype(f32).astype(bf16)
    upper = (iota((LANES, LANES), 0) <= iota((LANES, LANES), 1)).astype(f32).astype(bf16)
    before = (iota((high_rows, high_rows), 1) < iota((high_rows, high_rows), 0)).astype(f32)
    rank = mm(mask, upper) + jnp.sum(mm(before.astype(bf16), mask), axis=1, keepdims=True)
    rank = jnp.where(named, rank, 0.0)
    hubs[...] = rank
    first = here(SEQ) * (rows // LANES)
    at_row = iota((high_rows, LANES), 0)
    own = jnp.concatenate(
        [
            jnp.sum(jnp.where(at_row == first + r, rank, 0.0), axis=0, keepdims=True)
            for r in range(rows // LANES)
        ],
        axis=1,
    )
    hub_row = iota((HUBS, rows), 0).astype(f32) + 1.0
    own_pick[...] = (hub_row == own).astype(f32).astype(bf16)
    live = live_row(lengths, rows)
    for h in range(heads):
        same = iota((cl_pad, rows), 0) == cluster_row(clusters, h)
        members_t[h] = (same & live).astype(f32).astype(bf16)


def list_kernel(heads, cl_pad, lengths, tops, clusters, hubs, own_pick, in_top, chosen, members):
    slots = tops.shape[2]
    rows = own_pick.shape[1]
    high_rows = hubs.shape[0]
    rank = hubs[...].astype(bf16)
    for h in range(heads):
        position = named_rows(tops, h, cl_pad)
        entries = position.shape[1]
        high_hot = (iota((high_rows, entries), 0) == position // LANES).astype(f32).astype(bf16)
        by_low = tm(rank, high_hot)
        hub_of = jnp.sum(
            jnp.where(iota((LANES, entries), 0) == position % LANES, by_low, 0.0),
            axis=0,
            keepdims=True,
        )
        hub_row = iota((HUBS, cl_pad), 0).astype(f32) + 1.0
        in_list = jnp.zeros((HUBS, cl_pad), f32)
        for at in range(slots):
            row = hub_of[:, at * cl_pad : (at + 1) * cl_pad]
            in_list = jnp.where(hub_row == row, 1.0, in_list)
        in_list = in_list.astype(bf16)
        in_top[h] = tm(in_list, own_pick[...]).astype(bf16)
        same = (iota((cl_pad, rows), 0) == cluster_row(clusters, h)).astype(f32)
        table = same.T.astype(bf16)
        members[h] = table
        chosen[:, h * HUBS : (h + 1) * HUBS] = mt(table, in_list).astype(bf16)


def project_kernel(layer, heads, size, cl_rows, lengths, *refs):
    if layer == 0:
        source, gain_mine, gain_other, members_t, own_pick, w_mine, w_other = refs[:7]
        n1r, q, k, v, pay, w_qkv, sems = refs[7:]
    else:
        source, *four = refs[:5]
        gain_mine, gain_other, members_t, own_pick, w_mine, w_other = refs[5:11]
        y, n1r, q, k, v, pay, w_qkv, sems = refs[11:]
    weights = Choice(layer, [(w_mine, w_other)], [w_qkv], [sems.at[0]])
    if layer == 0:
        x = source[here(SECTION)].astype(f32)
    else:
        x = source[...] + summed(four)
        y[...] = x
    hat, _ = layer_stats(x)
    n1 = (hat * gain_row(gain_mine, gain_other, layer, 0)).astype(bf16)
    weights.wait(0)
    qv = mt(n1, w_qkv[0]).astype(bf16)
    kv = mt(n1, w_qkv[1]).astype(bf16)
    vv = mt(n1, w_qkv[2]).astype(bf16)
    q[...] = qv
    k[...] = kv
    v[...] = vv
    sums, counts = [], []
    for h in range(heads):
        members = members_t[h]
        sums.append(mm(members, qv[:, h * size : (h + 1) * size]))
        counts.append(jnp.sum(members.astype(f32), axis=1, keepdims=True))
    width = heads * size
    spare = round_up(width + 1, LANES) - width
    cl_pad = members_t.shape[1]
    block = jnp.concatenate(sums + [columns(spare, counts, cl_pad)], axis=1).astype(bf16)
    put_blocks(pay, 0, block, cl_rows)
    both = jnp.concatenate([mm(own_pick[...], kv), mm(own_pick[...], vv)], axis=1).astype(bf16)
    put_blocks(pay, cl_rows * (block.shape[1] // LANES), both, HUBS)
    n1r[...] = n1


def put_blocks(ref, start, block, rows):
    for at in range(block.shape[1] // LANES):
        ref[start + at * rows : start + (at + 1) * rows, :] = block[
            :rows, at * LANES : (at + 1) * LANES
        ]


def get_blocks(values, start, rows, count):
    return jnp.concatenate(
        [values[start + at * rows : start + (at + 1) * rows] for at in range(count)], axis=1
    )


def total_of(refs, start, rows, count):
    total = None
    for ref in refs:
        piece = ref[start : start + rows * count, :].astype(f32)
        total = piece if total is None else total + piece
    return get_blocks(total, 0, rows, count)


def pad_rows(values, rows):
    extra = rows - values.shape[0]
    if extra == 0:
        return values
    return jnp.concatenate([values, jnp.zeros((extra, values.shape[1]), values.dtype)], axis=0)


def centroid_kernel(count, heads, size, cl_rows, lengths, *refs):
    pays = refs[:count]
    k, v, in_tops, centre_ref, cnt_ref, pay = refs[count:]
    width = heads * size
    cl_pad = in_tops.shape[1]
    blocks = round_up(width + 1, LANES) // LANES
    total = pad_rows(total_of(pays, 0, cl_rows, blocks), cl_pad)
    cnt_ref[...] = total[:, (blocks - 1) * LANES :]
    rows = k.shape[0]
    live = live_row(lengths, rows)
    inv_root = size ** (-0.5)
    carried, extras = [], []
    for h in range(heads):
        cnt = total[:, width + h : width + h + 1]
        centre = jnp.where(
            cnt > 0, total[:, h * size : (h + 1) * size] / jnp.maximum(cnt, 1.0), 0.0
        ).astype(bf16)
        centre_ref[h] = centre
        scores = mt(centre, k[:, h * size : (h + 1) * size]) * inv_root
        peak = jnp.max(jnp.where(live, scores, negative), axis=1, keepdims=True)
        weighted = jnp.where(live, jnp.exp(jnp.where(live, scores - peak, 0.0)), 0.0)
        in_top = in_tops[h].astype(f32)
        mass = jnp.sum(weighted, axis=1, keepdims=True)
        top_mass = jnp.sum(weighted * in_top, axis=1, keepdims=True)
        rest = (weighted * (1.0 - in_top)).astype(bf16)
        carried.append(mm(rest, v[:, h * size : (h + 1) * size]))
        for value in (peak, mass, top_mass):
            extras.extend(parts3(value))
    spare = blocks * LANES - width
    block = jnp.concatenate(carried + [columns(spare, extras, cl_pad)], axis=1).astype(bf16)
    put_blocks(pay, 0, block, cl_rows)


def member_kernel(count, heads, size, cl_rows, lengths, *refs):
    pays = refs[:count]
    q, chosen_ref, hub_ref, prob_ref, top_ref = refs[count:]
    width = heads * size
    blocks = round_up(width + 1, LANES) // LANES
    hub = total_of(pays, blocks * cl_rows, HUBS, 2 * width // LANES).astype(bf16)
    hub_ref[...] = hub
    inv_root = size ** (-0.5)
    probs, outs = [], []
    for h in range(heads):
        keys = hub[:, h * size : (h + 1) * size]
        values = hub[:, width + h * size : width + (h + 1) * size]
        logits = mt(q[:, h * size : (h + 1) * size], keys) * inv_root
        chosen = chosen_ref[:, h * HUBS : (h + 1) * HUBS].astype(f32) > 0.5
        logits = jnp.where(chosen, logits, negative)
        exponent = jnp.where(
            chosen, jnp.exp(logits - jnp.max(logits, axis=1, keepdims=True)), 0.0
        )
        prob = exponent / jnp.sum(exponent, axis=1, keepdims=True)
        probs.append(prob)
        outs.append(mm(prob.astype(bf16), values))
    prob_ref[...] = jnp.concatenate(probs, axis=1)
    top_ref[...] = jnp.concatenate(outs, axis=1)


def combine_kernel(layer, count, heads, size, cl_rows, lengths, *refs):
    pays = refs[:count]
    top_out, members, mine, other, att_ref, top, low, stat_ref, w_out, sems = refs[count:]
    weights = Choice(layer, [(mine, other)], [w_out], [sems.at[0]])
    width = heads * size
    cl_pad = members.shape[2]
    blocks = round_up(width + 1, LANES) // LANES
    tables = [
        pad_rows(get_blocks(ref[...].astype(f32), 0, cl_rows, blocks), cl_pad) for ref in pays
    ]
    rows = top_out.shape[0]
    live = live_col(lengths, rows)
    pieces = []
    for h in range(heads):

        def value(one, which):
            at = width + 9 * h + 3 * which
            return one[:, at : at + 1] + one[:, at + 1 : at + 2] + one[:, at + 2 : at + 3]

        peaks = [value(one, 0) for one in tables]
        peak = functools.reduce(jnp.maximum, peaks)
        mass = top_mass = carried = 0.0
        for one, mine in zip(tables, peaks):
            scale = jnp.exp(mine - peak)
            mass = mass + value(one, 1) * scale
            top_mass = top_mass + value(one, 2) * scale
            carried = carried + one[:, h * size : (h + 1) * size] * scale
        safe = jnp.where(mass > 0, mass, 1.0)
        remote = carried / safe
        share = top_mass / safe
        lanes = LANES - size
        stat_ref[h] = jnp.concatenate(
            [carried, columns(lanes, (peak, safe, top_mass, share), cl_pad)], axis=1
        )
        looked = pick_rows(
            members[h], jnp.concatenate([remote, columns(lanes, (share,), cl_pad)], axis=1)
        )
        att = looked[:, size : size + 1] * top_out[:, h * size : (h + 1) * size] + looked[:, :size]
        pieces.append(jnp.where(live, att, 0.0))
    joined = jnp.concatenate(pieces, axis=1).astype(bf16)
    att_ref[...] = joined
    weights.wait(0)
    halves(mm(joined, w_out[...]), top, low)


def feed_kernel(layer, with_back, lengths, *refs):
    source, *four = refs[:5]
    gain_mine, gain_other, in_mine, in_other, back_mine, back_other = refs[5:11]
    if with_back:
        x1_ref, n2r, active_ref, slope_ref, top, low, w_in, w_back, sems = refs[11:]
        pairs = [(in_mine, in_other), (back_mine, back_other)]
        weights = Choice(layer, pairs, [w_in, w_back], [sems.at[0], sems.at[1]])
    else:
        x1_ref, n2r, active_ref, slope_ref, w_in, sems = refs[11:]
        weights = Choice(layer, [(in_mine, in_other)], [w_in], [sems.at[0]])
    x1 = source[here(SECTION)].astype(f32) if layer == 0 else source[...]
    x1 = x1 + summed(four)
    x1_ref[...] = x1
    hat, _ = layer_stats(x1)
    n2 = (hat * gain_row(gain_mine, gain_other, layer, 1)).astype(bf16)
    weights.wait(0)
    hidden = mm(n2, w_in[...])
    root = (2.0 / 3.141592653589793) ** 0.5
    square = hidden * hidden
    bent = jnp.tanh(root * hidden * (1.0 + 0.044715 * square))
    active = (0.5 * hidden * (1.0 + bent)).astype(bf16)
    active_ref[...] = active
    slope_ref[...] = 0.5 * (1.0 + bent) + 0.5 * hidden * (1.0 - bent * bent) * root * (
        1.0 + 3 * 0.044715 * square
    )
    if with_back:
        weights.wait(1)
        halves(mm(active, w_back[...]), top, low)
    n2r[...] = n2


def late_feed_kernel(layer, lengths, active, mine, other, top, low, w_back, sems):
    weights = Choice(layer, [(mine, other)], [w_back], [sems.at[0]])
    weights.wait(0)
    halves(mm(active[...], w_back[...]), top, low)


def pass_kernel(lengths, one, two, one_on, two_on):
    one_on[...] = one[...]
    two_on[...] = two[...]


def feed_back_kernel(layer, lengths, *refs):
    if layer == 1:
        cot, slope = refs[:2]
        refs = refs[2:]
    else:
        grad_middle, source, *four = refs[:6]
        gain = gain_row(*refs[6:8], layer + 1, 0)
        slope = refs[8]
        refs = refs[9:]
    weights = Choice(
        layer, [refs[:2], refs[2:4]], refs[-3:-1], [refs[-1].at[0], refs[-1].at[1]]
    )
    w_back, w_in = refs[-3:-1]
    dybr, dz_ref, top, low = refs[-7:-3]
    if layer == 1:
        dyb = cot[here(SECTION)]
    else:
        dy_ref, gain_ref = refs[4:6]
        dy = input_grad(grad_middle, source[...], four, gain, gain_ref)
        dy_ref[...] = dy
        dyb = dy.astype(bf16)
    weights.wait(0)
    dz = (mt(dyb, w_back[...]) * slope[...]).astype(bf16)
    dz_ref[...] = dz
    weights.wait(1)
    halves(mt(dz, w_in[...]), top, low)
    dybr[...] = dyb


def input_grad(grad_middle, source, four, gain, gain_ref):
    grad_normed = summed(four)
    hat, inverse = layer_stats(source)
    if gain_ref is not None:
        gain_ref[...] = jnp.sum(grad_normed * hat, axis=0, keepdims=True)
    return grad_middle[...] + norm_back(grad_normed * gain, hat, inverse)


def input_grad_kernel(lengths, *refs):
    grad_middle, source, *four = refs[:6]
    *gains, gain_two, last_one, last_two, sent, keep, gain_one = refs[6:]
    source = source[here(SECTION)].astype(f32)
    rows = source.shape[0]
    sent[:rows, :] = input_grad(grad_middle, source, four, gain_row(*gains, 0, 0), gain_one)
    first = jnp.concatenate([gain_one[...], gain_two[...]], axis=0)
    last = jnp.concatenate([last_one[...], last_two[...]], axis=0)
    keep[...] = jnp.where(here(SECTION) == 0, first, last)
    give = jnp.where(here(SECTION) == 0, last, first)
    sent[rows:, :] = jnp.concatenate([give, jnp.zeros((6, give.shape[1]), f32)], axis=0)


def middle_back_kernel(layer, heads, size, cl_rows, lengths, *refs):
    four = refs[:4]
    middle, grad_out, gain_mine, gain_other, top_out, members_t = refs[4:10]
    mine, other, dx1_ref, dx1r, dtop_ref, gain_ref, pay, w_out, sems = refs[10:]
    weights = Choice(layer, [(mine, other)], [w_out], [sems.at[0]])
    grad_normed = summed(four)
    hat, inverse = layer_stats(middle[...])
    gain_ref[...] = jnp.sum(grad_normed * hat, axis=0, keepdims=True)
    grad = grad_out[here(SECTION)].astype(f32) if layer == 1 else grad_out[...]
    dx1 = grad + norm_back(
        grad_normed * gain_row(gain_mine, gain_other, layer, 1), hat, inverse
    )
    dx1_ref[...] = dx1
    dx1b = dx1.astype(bf16)
    rows = dx1.shape[0]
    weights.wait(0)
    datt = mt(dx1b, w_out[...])
    dtop = jnp.where(live_col(lengths, rows), datt, 0.0).astype(bf16)
    dtop_ref[...] = dtop
    sums, shares = [], []
    for h in range(heads):
        members = members_t[h]
        own = dtop[:, h * size : (h + 1) * size]
        sums.append(mm(members, own))
        product = own.astype(f32) * top_out[:, h * size : (h + 1) * size]
        both = mm(members, jnp.concatenate(parts2(product), axis=1))
        shares.extend(parts3(jnp.sum(both, axis=1, keepdims=True)))
    width = heads * size
    spare = round_up(width + 1, LANES) - width
    cl_pad = members_t.shape[1]
    block = jnp.concatenate(sums + [columns(spare, shares, cl_pad)], axis=1).astype(bf16)
    put_blocks(pay, 0, block, cl_rows)
    dx1r[...] = dx1b


def member_back_kernel(heads, size, lengths, *refs):
    q, hub_ref, prob_ref, dtop, stat, members, dq_ref, pay = refs
    width = heads * size
    inv_root = size ** (-0.5)
    hub = hub_ref[...]
    dqs, dks, dvs = [], [], []
    for h in range(heads):
        keys = hub[:, h * size : (h + 1) * size]
        values = hub[:, width + h * size : width + (h + 1) * size]
        prob = prob_ref[:, h * HUBS : (h + 1) * HUBS]
        own = dtop[:, h * size : (h + 1) * size]
        share = pick_rows(members[h], stat[h])[:, size + 3 : size + 4]
        da = mt(own, values) * share
        dg = (prob * (da - jnp.sum(prob * da, axis=1, keepdims=True))).astype(bf16)
        dqs.append(mm(dg, keys) * inv_root)
        dks.append(tm(dg, q[:, h * size : (h + 1) * size]) * inv_root)
        scaled = own.astype(f32) * share
        dvs.append(tm(prob.astype(bf16), scaled.astype(bf16)))
    dq_ref[...] = jnp.concatenate(dqs, axis=1)
    put_blocks(pay, 0, jnp.concatenate(dks + dvs, axis=1).astype(bf16), HUBS)


def centroid_back_kernel(count, heads, size, cl_rows, lengths, *refs):
    pays = refs[:count]
    centre_ref, stat, k, v, in_tops, hub_pay, pay, dk_ref, dv_ref = refs[count:]
    width = heads * size
    cl_pad = in_tops.shape[1]
    blocks = round_up(width + 1, LANES) // LANES
    total = pad_rows(total_of(pays, 0, cl_rows, blocks), cl_pad)
    rows = k.shape[0]
    live = live_row(lengths, rows)
    inv_root = size ** (-0.5)
    dcs, dks, dvs = [], [], []
    for h in range(heads):
        keys = k[:, h * size : (h + 1) * size]
        values = v[:, h * size : (h + 1) * size]
        centre = centre_ref[h]
        grad_remote = total[:, h * size : (h + 1) * size]
        at = width + 3 * h
        grad_share = total[:, at : at + 1] + total[:, at + 1 : at + 2] + total[:, at + 2 : at + 3]
        carried = stat[h][:, :size]
        peak = stat[h][:, size : size + 1]
        mass = stat[h][:, size + 1 : size + 2]
        top_mass = stat[h][:, size + 2 : size + 3]
        grad_carried = (grad_remote / mass).astype(bf16)
        grad_top = grad_share / mass
        grad_mass = -(
            jnp.sum(grad_remote * carried, axis=1, keepdims=True) + grad_share * top_mass
        ) / (mass * mass)
        scores = mt(centre, keys) * inv_root
        weighted = jnp.where(live, jnp.exp(jnp.where(live, scores - peak, 0.0)), 0.0)
        in_top = in_tops[h].astype(f32)
        rest = (weighted * (1.0 - in_top)).astype(bf16)
        grad_weighted = (
            (1.0 - in_top) * mt(grad_carried, values) + in_top * grad_top + grad_mass
        )
        grad_scores = (grad_weighted * weighted).astype(bf16)
        dcs.append(mm(grad_scores, keys) * inv_root)
        dks.append(tm(grad_scores, centre) * inv_root)
        dvs.append(tm(rest, grad_carried))
    spare = blocks * LANES - width
    block = jnp.concatenate(dcs + [jnp.zeros((cl_pad, spare), f32)], axis=1).astype(bf16)
    put_blocks(pay, 0, block, cl_rows)
    pay[blocks * cl_rows :, :] = hub_pay[...]
    dk_ref[...] = jnp.concatenate(dks, axis=1)
    dv_ref[...] = jnp.concatenate(dvs, axis=1)


def project_back_kernel(layer, count, heads, size, cl_rows, lengths, *refs):
    pays = refs[:count]
    dq_top, dk_c, dv_c, cnt_ref, members, own_pick, mine, other = refs[count : count + 8]
    dqkv_ref, top, low, w_qkv, sems = refs[count + 8 :]
    weights = Choice(layer, [(mine, other)], [w_qkv], [sems.at[0]])
    width = heads * size
    cl_pad = members.shape[2]
    blocks = round_up(width + 1, LANES) // LANES
    total = pad_rows(total_of(pays, 0, cl_rows, blocks), cl_pad)
    hub = total_of(pays, blocks * cl_rows, HUBS, 2 * width // LANES)
    high, low_part = parts2(hub)
    spread = tm(own_pick[...], high) + tm(own_pick[...], low_part)
    rows = dq_top.shape[0]
    live = live_col(lengths, rows)
    base = round_up(width + 1, LANES) - LANES
    dqs = []
    for h in range(heads):
        at = width - base + h
        cnt = jnp.maximum(cnt_ref[:, at : at + 1], 1.0)
        from_centre = pick_rows(members[h], total[:, h * size : (h + 1) * size] / cnt)
        dqs.append(jnp.where(live, from_centre, 0.0))
    dq = (dq_top[...] + jnp.concatenate(dqs, axis=1)).astype(bf16)
    dk = (dk_c[...] + spread[:, :width]).astype(bf16)
    dv = (dv_c[...] + spread[:, width:]).astype(bf16)
    dqkv_ref[...] = jnp.concatenate([dq, dk, dv], axis=1)
    weights.wait(0)
    halves(mm(dq, w_qkv[0]) + mm(dk, w_qkv[1]) + mm(dv, w_qkv[2]), top, low)


def feed_grads_kernel(lengths, dyb, active, n2, dz, keep, give):
    back = tm(dyb[...], active[...]).astype(bf16)
    into = tm(n2[...], dz[...]).astype(bf16)

    @pl.when(here(SECTION) == 0)
    def _():
        keep[...] = back
        give[...] = into

    @pl.when(here(SECTION) == 1)
    def _():
        keep[...] = into
        give[...] = back


def attention_grads_kernel(count, lengths, n1, dqkv, dx1b, att, keep, give):
    part = n1.shape[1] // count
    half = part // 2
    both = jnp.concatenate([tm(n1[...], dqkv[...]), tm(dx1b[...], att[...])], axis=1).astype(bf16)

    def put(ref, first):
        for at in range(count):
            ref[at] = both[at * part + first : at * part + first + half]

    @pl.when(here(SECTION) == 0)
    def _():
        put(keep, 0)
        put(give, half)

    @pl.when(here(SECTION) == 1)
    def _():
        put(keep, half)
        put(give, 0)


def chip_sum_kernel(lengths, mine, far, keep, give):
    me = here(SEQ)
    for at in range(keep.shape[0]):
        stay, go = 2 * at + me % 2, 2 * at + 1 - me % 2
        keep[at] = (mine[stay].astype(f32) + far[stay].astype(f32)).astype(bf16)
        give[at] = (mine[go].astype(f32) + far[go].astype(f32)).astype(bf16)


def pair_sum_kernel(lengths, mine, far, keep, give):
    stay = here(SEQ) // 2
    go = 1 - stay
    keep[...] = (mine[stay].astype(f32) + far[stay].astype(f32)).astype(bf16)
    give[...] = (mine[go].astype(f32) + far[go].astype(f32)).astype(bf16)


def sorted_sum_kernel(lengths, mine, far, *outs):
    for k, out in enumerate(outs):
        at = lax.rem(here(SEQ) + k, len(outs))
        out[...] = (mine[at].astype(f32) + far[at].astype(f32)).astype(bf16)


def seq_sum_kernel(lengths, *refs):
    total = refs[0][...].astype(f32)
    for ref in refs[1:-1]:
        total = total + ref[...].astype(f32)
    refs[-1][...] = total


def ship_kernel(sums, lengths, *refs):
    row = 0
    out = refs[-1]
    for at in range(sums):
        mine, far = refs[2 * at : 2 * at + 2]
        out[row : row + mine.shape[0], :] = mine[...].astype(f32) + far[...].astype(f32)
        row += mine.shape[0]
    grad, source, *four = refs[2 * sums : -1]
    out[row : row + grad.shape[0], :] = grad[...]
    row += grad.shape[0]
    out[row:, :] = source[...] + summed(four)


def feed_owner_kernel(lengths, first, first_far, shipped, shipped_far, back, into, token):
    rows = first.shape[0]
    token[...] = jnp.zeros_like(token)

    @pl.when(here(SECTION) == 0)
    def _():
        back[...] = first[...]
        into[...] = first_far[...]

    @pl.when(here(SECTION) == 1)
    def _():
        into[...] = shipped[:rows, :]
        back[...] = shipped_far[:rows, :]


def attention_owner_kernel(width, start, lengths, first, first_far, shipped, shipped_far, grad_qkv, grad_out):
    rows = first.shape[0]

    def put(low_half, high_half):
        both = jnp.concatenate([low_half, high_half], axis=0)
        for at in range(3):
            grad_qkv[at] = both[:, at * width : (at + 1) * width]
        grad_out[...] = both[:, 3 * width :].T

    @pl.when(here(SECTION) == 0)
    def _():
        put(first[...], first_far[...])

    @pl.when(here(SECTION) == 1)
    def _():
        put(shipped_far[start : start + rows, :], shipped[start : start + rows, :])


def place_kernel(start, lengths, own_first, far_first, shipped, shipped_far, out, token):
    rows = out.shape[1]
    token[...] = jnp.zeros_like(token)

    @pl.when(here(SECTION) == 0)
    def _():
        out[0] = own_first[:rows, :]
        out[1] = far_first[:rows, :]

    @pl.when(here(SECTION) == 1)
    def _():
        out[0] = shipped_far[start : start + rows, :]
        out[1] = shipped[start : start + rows, :]


def gain_kernel(lengths, keep, sent_far, out):
    rows = sent_far.shape[0] - 8
    out[...] = keep[...] + sent_far[rows : rows + 2, :]


def moved(block, axis, target):
    devices = range(lax.axis_size(axis))
    return lax.ppermute(block, axis, [(i, target(i)) for i in devices])


def swap(block):
    return moved(block, SECTION, lambda i: i ^ 1)


def every_seq(block):
    count = lax.axis_size(SEQ)
    if count > DIRECT:
        gathered = lax.all_gather(block, SEQ)
        return [gathered[at] for at in range(count)]
    return [block] + [
        moved(block, SEQ, lambda i, k=k: (i + k) % count) for k in range(1, count)
    ]


def every_head(block):
    return [block] + [
        moved(block, HEAD, lambda i, k=k: i ^ k) for k in range(1, lax.axis_size(HEAD))
    ]


def every_head_in_turn(block):
    pieces = [block]
    distance = 1
    while distance < lax.axis_size(HEAD):
        pieces += [moved(piece, HEAD, lambda i: i ^ distance) for piece in pieces]
        distance *= 2
    return pieces


def fold_kernel(lengths, top_a, top_b, low_a, low_b, top, low):
    top[...] = (top_a[...].astype(f32) + top_b[...].astype(f32)).astype(bf16)
    low[...] = (low_a[...].astype(f32) + low_b[...].astype(f32)).astype(bf16)


def head_sum(top, low, run, before_fold=None):
    distances = [1 << at for at in range(lax.axis_size(HEAD).bit_length() - 1)]
    for step in range(len(distances)):
        one = distances[step]
        other = distances[len(distances) - 1 - step]
        far_top = moved(top, HEAD, lambda i: i ^ one)
        far_low = moved(low, HEAD, lambda i: i ^ other)
        if step < len(distances) - 1:
            ties = before_fold() if before_fold and step == 0 else []
            shape = [shaped(top.shape, bf16)] * 2
            top, low = run(
                fold_kernel, shape, [top, far_top, low, far_low], ties=ties
            )
    return (top, far_top, low, far_low)


def to_core(block, layer):
    return lax.ppermute(block, SECTION, [(1 - layer, layer)])


def seq_xor(block, distance):
    return moved(block, SEQ, lambda i: i ^ distance)


def pair_step(keep, far, run, ties=()):
    half = shaped((keep.shape[0] // 2,) + keep.shape[1:], bf16)
    keep, give = run(chip_sum_kernel, [half] * 2, [keep, far], ties=ties)
    return keep, seq_xor(give, 1)


def far_step(keep, far, run, ties=()):
    keep, give = run(
        pair_sum_kernel, [shaped(keep.shape[1:], bf16)] * 2, [keep, far], ties=ties
    )
    return keep, seq_xor(give, 2)


def shards(tokens, cotangent, lengths, clusters, top_index, w_qkv, w_out, w_in, w_back, gains):
    section = lax.axis_index(SECTION)
    me = lax.axis_index(SEQ)
    count = lax.axis_size(SEQ)
    head_devices = lax.axis_size(HEAD)
    micro, rows, dim = tokens.shape
    _, heads, cluster_count, slots = top_index.shape
    size = w_qkv.shape[3] // heads
    width = heads * size
    hidden = w_in.shape[2]
    total_rows = rows * count
    cl_pad = round_up(cluster_count, LANES)
    cl_rows = round_up(cluster_count, 16)
    high_rows = round_up(max(total_rows // LANES, 1), 16)
    blocks = round_up(width + 1, LANES) // LANES
    hub_blocks = 2 * width // LANES
    sizes = (heads, size, cl_rows)
    run = lambda kernel, outs, args, **kw: call(kernel, outs, lengths, args, **kw)
    part = functools.partial
    fours = [shaped((rows // 2, dim), bf16)] * 2
    pay_shape = shaped((blocks * cl_rows, LANES), bf16)
    table_shape = shaped((heads, cl_pad, rows), bf16)
    square = shaped((dim, hidden), bf16)
    qkv_buf = shaped((3, width, dim), bf16)

    qkv_t = w_qkv[0].transpose(0, 2, 1)
    qkv_pair = (qkv_t, swap(qkv_t))
    gain_pair = (gains[0], swap(gains[0]))
    tops = top_index.transpose(0, 1, 3, 2)
    clusters = clusters.transpose(1, 0, 2)
    out_pair = (w_out[0], swap(w_out[0]))
    in_pair = (w_in[0], swap(w_in[0]))
    back_pair = (w_back[0], swap(w_back[0]))
    own_pick, hubs, members_t = run(
        part(rank_kernel, heads, cl_pad),
        [shaped((HUBS, rows), bf16), shaped((high_rows, LANES)), table_shape],
        [tops, clusters],
    )

    source, lists = tokens, None
    kept, acts = [], []
    for layer in range(2):
        outs = [
            shaped((rows, dim), bf16),
            shaped((rows, width), bf16),
            shaped((rows, width), bf16),
            shaped((rows, width), bf16),
            shaped((blocks * cl_rows + hub_blocks * HUBS, LANES), bf16),
        ]
        if layer:
            outs = [shaped((rows, dim))] + outs
        found = run(
            part(project_kernel, layer, *sizes),
            outs,
            ([tokens] if layer == 0 else [x1, *four])
            + [*gain_pair, members_t, own_pick],
            anys=qkv_pair,
            bufs=[qkv_buf],
        )
        if layer:
            source, *found = found
            acts.append(source)
            acts_far = to_core(source, 0)
        n1r, q, k, v, pay = found
        pays = every_seq(pay)
        if lists is None:
            in_tops, chosen, members = lists = run(
                part(list_kernel, heads, cl_pad),
                [
                    table_shape,
                    shaped((rows, heads * HUBS), bf16),
                    shaped((heads, rows, cl_pad), bf16),
                ],
                [tops, clusters, hubs, own_pick],
            )
        centre, cnt, pay = run(
            part(centroid_kernel, len(pays), *sizes),
            [shaped((heads, cl_pad, size), bf16), shaped((cl_pad, LANES)), pay_shape],
            [*pays, k, v, in_tops],
        )
        stats = every_seq(pay)
        hub, prob, top_out = run(
            part(member_kernel, len(pays), *sizes),
            [
                shaped((HUBS, 2 * width), bf16),
                shaped((rows, heads * HUBS)),
                shaped((rows, width)),
            ],
            [*pays, q, chosen],
            ties=[in_pair[1]] if layer == 0 else [acts_far],
        )
        att, top, low, stat = run(
            part(combine_kernel, layer, len(stats), *sizes),
            [shaped((rows, width), bf16)] + fours + [shaped((heads, cl_pad, LANES))],
            [*stats, top_out, members],
            anys=out_pair,
            bufs=[shaped((width, dim), bf16)],
        )
        four = head_sum(top, low, run)
        with_back = layer == 0
        found = run(
            part(feed_kernel, layer, with_back),
            [
                shaped((rows, dim)),
                shaped((rows, dim), bf16),
                shaped((rows, hidden), bf16),
                shaped((rows, hidden)),
            ]
            + fours * with_back,
            [source, *four, *gain_pair],
            anys=[*in_pair, *back_pair],
            bufs=[square] + [square] * with_back,
        )
        x1, n2r, active, slope = found[:4]
        if with_back:
            four = head_sum(*found[4:], run)
        kept.append(
            (source, n1r, q, k, v, centre, cnt, hub, prob, top_out, att, stat, x1, n2r, active, slope)
        )

    direct = count == DIRECT
    seq_part = dim // count
    half = seq_part // 2
    extra = 16
    if not direct:
        seq_part = half = None

    def plain_sum(grad, layer):
        total = grad.astype(f32) + to_core(grad.astype(bf16), layer).astype(f32)
        return lax.psum_scatter(
            total.astype(bf16), SEQ, scatter_dimension=0, tiled=True
        ).astype(f32)

    def feed_grads(layer, dyb, dz, ties=()):
        active, n2 = kept[layer][14], kept[layer][13]
        if not direct:
            return plain_sum(tm(dyb, active), layer), plain_sum(tm(n2, dz), layer)
        return run(
            feed_grads_kernel, [square] * 2, [dyb, active, n2, dz], ties=ties
        )

    def attention_grads(layer, dqkv, dx1b):
        n1, att = kept[layer][1], kept[layer][10]
        if not direct:
            return plain_sum(jnp.concatenate([tm(n1, dqkv), tm(dx1b, att)], axis=1), layer)
        return run(
            part(attention_grads_kernel, count),
            [shaped((count, half, 4 * width), bf16)] * 2,
            [n1, dqkv, dx1b, att],
        )

    def swapped(made):
        far = swap(made[1])
        shape = (count, -1, made[0].shape[-1])
        return made[0].reshape(shape), far.reshape(shape)

    def middle_back(layer, four, dy, ties):
        top_out, x1 = kept[layer][9], kept[layer][12]
        return run(
            part(middle_back_kernel, layer, *sizes),
            [
                shaped((rows, dim)),
                shaped((rows, dim), bf16),
                shaped((rows, width), bf16),
                shaped((1, dim)),
                pay_shape,
            ],
            [*four, x1, dy, *gain_pair, top_out, members_t],
            anys=out_pair,
            bufs=[shaped((width, dim), bf16)],
            ties=ties,
        )

    def member_back(layer, dtop, ties=()):
        _, _, q, _, _, _, _, hub, prob, _, _, stat = kept[layer][:12]
        return run(
            part(member_back_kernel, heads, size),
            [shaped((rows, width)), shaped((hub_blocks * HUBS, LANES), bf16)],
            [q, hub, prob, dtop, stat, members],
            ties=ties,
        )

    def centroid_back(layer, pays, hub_pay, ties):
        _, _, _, k, v, centre, _, _, _, _, _, stat = kept[layer][:12]
        return run(
            part(centroid_back_kernel, len(pays), *sizes),
            [
                shaped((blocks * cl_rows + hub_blocks * HUBS, LANES), bf16),
                shaped((rows, width)),
                shaped((rows, width)),
            ],
            [*pays, centre, stat, k, v, in_tops, hub_pay],
            ties=ties,
        )

    def project_back(layer, pays, dq_top, dk, dv, ties):
        cnt = kept[layer][6]
        return run(
            part(project_back_kernel, layer, len(pays), *sizes),
            [shaped((rows, 3 * width), bf16)] + fours,
            [*pays, dq_top, dk, dv, cnt, members, own_pick],
            anys=qkv_pair,
            bufs=[qkv_buf],
            ties=ties,
        )

    def shared(pay):
        return every_seq(pay)

    def step(parts, axis, one, other):
        return [parts[0], moved(parts[0], axis, lambda i: i ^ one),
                    parts[1], moved(parts[1], axis, lambda i: i ^ other)]

    def fold(four, ties):
        return run(fold_kernel, fours, four, ties=ties)

    def ended(group, layer, ties):
        (total,) = run(seq_sum_kernel, [shaped(group[0].shape)], group, ties=ties)
        return [total, to_core(total, layer)]

    near, away = 1, head_devices // 2
    assert head_devices == 4
    only = lambda items: list(items) if direct else []

    backs = [shaped((rows, dim), bf16), shaped((rows, hidden), bf16)] + fours
    dyb, dz, *parts = run(
        part(feed_back_kernel, 1),
        backs,
        [cotangent, kept[1][15]],
        anys=[*back_pair, *in_pair],
        bufs=[square, square],
    )
    four = step(parts, HEAD, near, away)
    parts = fold(four, [])
    four = step(parts, HEAD, away, near)
    dx1, dx1b, dtop, gain_two, pay = middle_back(1, four, cotangent, [])
    feed_last = feed_grads(1, dyb, dz, [dtop])
    pays = shared(pay)
    dq_top, hub_pay = member_back(1, dtop)
    pay, dk, dv = centroid_back(1, pays, hub_pay, only(feed_last))
    if direct:
        feed_last = swapped(feed_last)
    late_parts = run(
        part(late_feed_kernel, 1),
        fours,
        [kept[1][14]],
        anys=back_pair,
        bufs=[square],
        ties=pays[1:] + [hub_pay],
    )
    late = step(late_parts, HEAD, near, away)
    pays = shared(pay)
    if direct:
        feed_last = pair_step(*feed_last, run, pays[1:])
    dqkv, *parts = project_back(
        1, pays, dq_top, dk, dv, [late[1], late[3]] + only(feed_last[:1])
    )
    four = step(parts, HEAD, near, away)
    parts = fold(four, [])
    four = step(parts, HEAD, away, near)
    attention_last = attention_grads(1, dqkv, dx1b)
    if direct:
        feed_last = far_step(*feed_last, run)
        attention_last = swapped(attention_last)
        attention_last = pair_step(*attention_last, run)
    dy, gain_one, dyb, dz, *parts = run(
        part(feed_back_kernel, 0),
        [shaped((rows, dim)), shaped((1, dim))] + backs,
        [dx1, kept[1][0], *four, *gain_pair, kept[0][15]],
        anys=[*back_pair, *in_pair],
        bufs=[square, square],
        ties=only([feed_last[0], attention_last[0]]),
    )
    last_grad, last_gains = dy, [gain_one, gain_two]
    four = step(parts, HEAD, near, away)
    parts = fold(four, only([attention_last[1], feed_last[1]]))
    if direct:
        attention_last = far_step(*attention_last, run, parts)
    four = step(parts, HEAD, away, near)
    feed_first = feed_grads(0, dyb, dz, parts)
    dx1, dx1b, dtop, gain_two, pay = middle_back(
        0, four, dy, only(feed_first)
    )
    pays = shared(pay)
    dq_top, hub_pay = member_back(0, dtop)
    if direct:
        feed_first = swapped(feed_first)
    pay, dk, dv = centroid_back(
        0, pays, hub_pay, only([feed_first[1], attention_last[1]])
    )
    late_parts = fold(late, [dk])
    late = step(late_parts, HEAD, away, near)
    pays = shared(pay)
    if direct:
        feed_first = pair_step(*feed_first, run, pays[1:])
    dqkv, *parts = project_back(
        0, pays, dq_top, dk, dv, [late[1], late[3]] + only(feed_first[:1])
    )
    four = step(parts, HEAD, near, away)
    attention_first = attention_grads(0, dqkv, dx1b)
    before = []
    if direct:
        attention_first = swapped(attention_first)
        attention_first = pair_step(*attention_first, run)
        feed_first = far_step(*feed_first, run)
        before = [attention_first[0], feed_first[0]]
    parts = fold(four, before)
    four = step(parts, HEAD, away, near)
    sums = [*feed_last, *attention_last] if direct else []
    sum_rows = (seq_part + half) if direct else 0
    (shipped,) = run(
        part(ship_kernel, len(sums) // 2),
        [shaped((sum_rows + 2 * rows, dim))],
        [*sums, last_grad, kept[1][12], *late],
        ties=parts,
    )
    shipped = [shipped, to_core(shipped, 1)]
    if direct:
        attention_first = far_step(*attention_first, run, parts)
    sent, own_gains, _ = run(
        input_grad_kernel,
        [shaped((rows + 8, dim)), shaped((2, dim)), shaped((1, dim))],
        [dx1, tokens, *four, *gain_pair, gain_two, *last_gains],
        ties=only(attention_first[:1]) + shipped,
    )
    sent_far = swap(sent)
    token = shaped((8, LANES))
    (placed_acts, acts_token), (placed_grads, grads_token) = (
        run(part(place_kernel, start), [shaped((2, rows, dim)), token], [*first, *shipped])
        for start, first in (
            (sum_rows + rows, (acts[0], acts_far)),
            (sum_rows, (sent, sent_far)),
        )
    )
    (gain_sum,) = run(gain_kernel, [shaped((2, dim))], [own_gains, sent_far])
    if direct:
        gain_sum = gain_sum + seq_xor(gain_sum, 1)
        gain_far = seq_xor(gain_sum, 2)
        gain_sum = gain_sum + gain_far
        gain_sum = lax.dynamic_slice_in_dim(gain_sum, me * seq_part, seq_part, 1)
        feed_first = ended(feed_first, 0, [acts_token])
        back, into, feed_token = run(
            feed_owner_kernel, [shaped((seq_part, hidden))] * 2 + [token], [*feed_first, *shipped]
        )
        attention_first = ended(
            attention_first, 0, [feed_token, grads_token, gain_far]
        )
        grad_qkv, grad_out = run(
            part(attention_owner_kernel, width, seq_part),
            [shaped((3, seq_part, width)), shaped((width, seq_part))],
            [*attention_first, *shipped],
        )
    else:
        pick = lambda one, two: jnp.where(section == 0, one, two)
        gain_sum = lax.psum_scatter(gain_sum, SEQ, scatter_dimension=1, tiled=True)
        back, into = (pick(feed_first[at], feed_last[at]) for at in range(2))
        both = pick(attention_first, attention_last)
        grad_qkv = both[:, : 3 * width].reshape(-1, 3, width).transpose(1, 0, 2)
        grad_out = both[:, 3 * width :].T
    return (
        placed_acts[None],
        placed_grads[None],
        grad_qkv[None],
        grad_out[None],
        into[None],
        back.T[None],
        gain_sum[None],
    )


def solution(mesh):
    placed = (
        P(None, SEQ, None),
        P(None, SEQ, None),
        P(),
        P(None, HEAD, SEQ),
        P(None, HEAD, None, None),
        P(SECTION, None, None, HEAD),
        P(SECTION, HEAD, None),
        P(SECTION, None, HEAD),
        P(SECTION, HEAD, None),
        P(SECTION, None, None),
    )
    return jax.shard_map(
        shards,
        mesh=mesh,
        in_specs=placed,
        out_specs=(
            P(SECTION, None, SEQ, None),
            P(SECTION, None, SEQ, None),
            P(SECTION, None, SEQ, HEAD),
            P(SECTION, HEAD, SEQ),
            P(SECTION, SEQ, HEAD),
            P(SECTION, HEAD, SEQ),
            P(SECTION, None, SEQ),
        ),
        check_vma=False,
    )
```

```python
import functools

import jax
import jax.numpy as jnp
from jax import lax
from jax.experimental import pallas as pl
from jax.experimental.pallas import tpu as pltpu
from jax.sharding import PartitionSpec as P

SECTION, SEQ, HEAD = "section", "seq", "head"
epsilon = 1e-05
negative = -1e30
f32 = jnp.float32
bf16 = jnp.bfloat16
LANES = 128
HUBS = 64
VMEM_LIMIT = 32 * 1024 * 1024
DIRECT = 4


def round_up(value, step):
    return -(-value // step) * step


def iota(shape, dim):
    return lax.broadcasted_iota(jnp.int32, shape, dim)


def mm(a, b):
    return lax.dot_general(a, b, (((1,), (0,)), ((), ())), preferred_element_type=f32)


def mt(a, b):
    return lax.dot_general(a, b, (((1,), (1,)), ((), ())), preferred_element_type=f32)


def tm(a, b):
    return lax.dot_general(a, b, (((0,), (0,)), ((), ())), preferred_element_type=f32)


def parts2(v):
    high = v.astype(bf16)
    return high, (v - high.astype(f32)).astype(bf16)


def parts3(v):
    high = v.astype(bf16)
    rest = v - high.astype(f32)
    mid = rest.astype(bf16)
    return high.astype(f32), mid.astype(f32), rest - mid.astype(f32)


def pick_rows(one_hot, table):
    high, low = parts2(table)
    return mm(one_hot, high) + mm(one_hot, low)


def layer_stats(values):
    centred = values - jnp.mean(values, axis=-1, keepdims=True)
    inverse = lax.rsqrt(jnp.mean(centred * centred, axis=-1, keepdims=True) + epsilon)
    return centred * inverse, inverse


def norm_back(grad_hat, normed, inverse):
    return inverse * (
        grad_hat
        - jnp.mean(grad_hat, axis=-1, keepdims=True)
        - normed * jnp.mean(grad_hat * normed, axis=-1, keepdims=True)
    )


def columns(base_width, cols, rows):
    lane = iota((rows, base_width), 1)
    out = jnp.zeros((rows, base_width), f32)
    for at, col in enumerate(cols):
        out = jnp.where(lane == at, col, out)
    return out


def here(name):
    return lax.axis_index(name)


def live_row(lengths, rows):
    return (here(SEQ) * rows + iota((1, rows), 1)) < lengths[here(SECTION)]


def live_col(lengths, rows):
    return (here(SEQ) * rows + iota((rows, 1), 0)) < lengths[here(SECTION)]


def gain_row(mine, other, layer, row):
    return jnp.where(
        here(SECTION) == layer,
        mine[row : row + 1, :].astype(f32),
        other[row : row + 1, :].astype(f32),
    )


class Choice:
    def __init__(self, layer, pairs, bufs, sems):
        self.copies = [
            (pltpu.make_async_copy(mine, buf, sem), pltpu.make_async_copy(other, buf, sem))
            for (mine, other), buf, sem in zip(pairs, bufs, sems)
        ]
        mine_here = here(SECTION) == layer

        @pl.when(mine_here)
        def _():
            for mine, _other in self.copies:
                mine.start()

        @pl.when(jnp.logical_not(mine_here))
        def _():
            for _mine, other in self.copies:
                other.start()

    def wait(self, at):
        self.copies[at][0].wait()


def summed(four):
    top_a, top_b, low_a, low_b = four
    return jnp.concatenate(
        [
            top_a[...].astype(f32) + top_b[...].astype(f32),
            low_a[...].astype(f32) + low_b[...].astype(f32),
        ],
        axis=0,
    )


def halves(values, top, low):
    half = values.shape[0] // 2
    top[...] = values[:half].astype(bf16)
    low[...] = values[half:].astype(bf16)


def call(kernel, outs, lengths, args, anys=(), bufs=(), ties=(), sems=None, outs_any=False):
    vmem = pl.BlockSpec(memory_space=pltpu.VMEM)
    anywhere = pl.BlockSpec(memory_space=pl.ANY)
    args, anys, ties = list(args), list(anys), list(ties)
    moved_bytes = sum(a.size * a.dtype.itemsize for a in args + list(outs) + list(bufs))
    first, last = 1 + len(args) + len(anys), 1 + len(args) + len(anys) + len(ties)

    def body(*refs):
        kernel(*refs[:first], *refs[last:])

    scratch = [pltpu.VMEM(b.shape, b.dtype) for b in bufs]
    if bufs or sems:
        scratch.append(pltpu.SemaphoreType.DMA((sems or len(bufs),)))
    whole = kernel.func if isinstance(kernel, functools.partial) else kernel
    with jax.named_scope(whole.__name__):
        return pl.pallas_call(
            body,
            out_shape=outs,
            in_specs=[pl.BlockSpec(memory_space=pltpu.SMEM)]
            + [vmem] * len(args)
            + [anywhere] * (len(anys) + len(ties)),
            out_specs=[anywhere if outs_any else vmem] * len(outs),
            scratch_shapes=scratch,
            compiler_params=pltpu.CompilerParams(vmem_limit_bytes=VMEM_LIMIT),
            cost_estimate=pl.CostEstimate(
                flops=0, bytes_accessed=moved_bytes, transcendentals=0
            ),
        )(lengths, *args, *anys, *ties)


def shaped(shape, dtype=f32):
    return jax.ShapeDtypeStruct(tuple(shape), dtype)


def named_rows(tops, head, clusters_pad):
    section = here(SECTION)
    slots, clusters = tops.shape[2:]
    rows = tops[section, head]
    if clusters < clusters_pad:
        rows = jnp.concatenate(
            [rows, jnp.full((slots, clusters_pad - clusters), -1, jnp.int32)], axis=1
        )
    return jnp.concatenate([rows[at : at + 1, :] for at in range(slots)], axis=1)


def cluster_row(clusters, head):
    return clusters[head, pl.ds(here(SECTION), 1), :]


def rank_kernel(heads, cl_pad, lengths, tops, clusters, own_pick, hubs, members_t):
    rows = own_pick.shape[1]
    high_rows = hubs.shape[0]
    named = None
    for h in range(heads):
        position = named_rows(tops, h, cl_pad)
        entries = position.shape[1]
        high_hot = (iota((high_rows, entries), 0) == position // LANES).astype(f32).astype(bf16)
        low_hot = (iota((LANES, entries), 0) == position % LANES).astype(f32).astype(bf16)
        found = mt(high_hot, low_hot)
        named = found if named is None else named + found
    named = named > 0.5
    mask = named.astype(f32).astype(bf16)
    upper = (iota((LANES, LANES), 0) <= iota((LANES, LANES), 1)).astype(f32).astype(bf16)
    before = (iota((high_rows, high_rows), 1) < iota((high_rows, high_rows), 0)).astype(f32)
    rank = mm(mask, upper) + jnp.sum(mm(before.astype(bf16), mask), axis=1, keepdims=True)
    rank = jnp.where(named, rank, 0.0)
    hubs[...] = rank
    first = here(SEQ) * (rows // LANES)
    at_row = iota((high_rows, LANES), 0)
    own = jnp.concatenate(
        [
            jnp.sum(jnp.where(at_row == first + r, rank, 0.0), axis=0, keepdims=True)
            for r in range(rows // LANES)
        ],
        axis=1,
    )
    hub_row = iota((HUBS, rows), 0).astype(f32) + 1.0
    own_pick[...] = (hub_row == own).astype(f32).astype(bf16)
    live = live_row(lengths, rows)
    for h in range(heads):
        same = iota((cl_pad, rows), 0) == cluster_row(clusters, h)
        members_t[h] = (same & live).astype(f32).astype(bf16)


def list_kernel(heads, cl_pad, lengths, tops, clusters, hubs, own_pick, in_top, chosen, members):
    slots = tops.shape[2]
    rows = own_pick.shape[1]
    high_rows = hubs.shape[0]
    rank = hubs[...].astype(bf16)
    for h in range(heads):
        position = named_rows(tops, h, cl_pad)
        entries = position.shape[1]
        high_hot = (iota((high_rows, entries), 0) == position // LANES).astype(f32).astype(bf16)
        by_low = tm(rank, high_hot)
        hub_of = jnp.sum(
            jnp.where(iota((LANES, entries), 0) == position % LANES, by_low, 0.0),
            axis=0,
            keepdims=True,
        )
        hub_row = iota((HUBS, cl_pad), 0).astype(f32) + 1.0
        in_list = jnp.zeros((HUBS, cl_pad), f32)
        for at in range(slots):
            row = hub_of[:, at * cl_pad : (at + 1) * cl_pad]
            in_list = jnp.where(hub_row == row, 1.0, in_list)
        in_list = in_list.astype(bf16)
        in_top[h] = tm(in_list, own_pick[...]).astype(bf16)
        same = (iota((cl_pad, rows), 0) == cluster_row(clusters, h)).astype(f32)
        table = same.T.astype(bf16)
        members[h] = table
        chosen[:, h * HUBS : (h + 1) * HUBS] = mt(table, in_list).astype(bf16)


def project_kernel(layer, heads, size, cl_rows, lengths, *refs):
    if layer == 0:
        source, gain_mine, gain_other, members_t, own_pick, w_mine, w_other = refs[:7]
        n1r, q, k, v, pay, w_qkv, sems = refs[7:]
    else:
        source, *four = refs[:5]
        gain_mine, gain_other, members_t, own_pick, w_mine, w_other = refs[5:11]
        y, n1r, q, k, v, pay, w_qkv, sems = refs[11:]
    weights = Choice(layer, [(w_mine, w_other)], [w_qkv], [sems.at[0]])
    if layer == 0:
        x = source[here(SECTION)].astype(f32)
    else:
        x = source[...] + summed(four)
        y[...] = x
    hat, _ = layer_stats(x)
    n1 = (hat * gain_row(gain_mine, gain_other, layer, 0)).astype(bf16)
    weights.wait(0)
    qv = mt(n1, w_qkv[0]).astype(bf16)
    kv = mt(n1, w_qkv[1]).astype(bf16)
    vv = mt(n1, w_qkv[2]).astype(bf16)
    q[...] = qv
    k[...] = kv
    v[...] = vv
    sums, counts = [], []
    for h in range(heads):
        members = members_t[h]
        sums.append(mm(members, qv[:, h * size : (h + 1) * size]))
        counts.append(jnp.sum(members.astype(f32), axis=1, keepdims=True))
    width = heads * size
    spare = round_up(width + 1, LANES) - width
    cl_pad = members_t.shape[1]
    block = jnp.concatenate(sums + [columns(spare, counts, cl_pad)], axis=1).astype(bf16)
    put_blocks(pay, 0, block, cl_rows)
    both = jnp.concatenate([mm(own_pick[...], kv), mm(own_pick[...], vv)], axis=1).astype(bf16)
    put_blocks(pay, cl_rows * (block.shape[1] // LANES), both, HUBS)
    n1r[...] = n1


def put_blocks(ref, start, block, rows):
    for at in range(block.shape[1] // LANES):
        ref[start + at * rows : start + (at + 1) * rows, :] = block[
            :rows, at * LANES : (at + 1) * LANES
        ]


def get_blocks(values, start, rows, count):
    return jnp.concatenate(
        [values[start + at * rows : start + (at + 1) * rows] for at in range(count)], axis=1
    )


def total_of(refs, start, rows, count):
    total = None
    for ref in refs:
        piece = ref[start : start + rows * count, :].astype(f32)
        total = piece if total is None else total + piece
    return get_blocks(total, 0, rows, count)


def pad_rows(values, rows):
    extra = rows - values.shape[0]
    if extra == 0:
        return values
    return jnp.concatenate([values, jnp.zeros((extra, values.shape[1]), values.dtype)], axis=0)


def centroid_kernel(count, heads, size, cl_rows, lengths, *refs):
    pays = refs[:count]
    k, v, in_tops, centre_ref, cnt_ref, pay = refs[count:]
    width = heads * size
    cl_pad = in_tops.shape[1]
    blocks = round_up(width + 1, LANES) // LANES
    total = pad_rows(total_of(pays, 0, cl_rows, blocks), cl_pad)
    cnt_ref[...] = total[:, (blocks - 1) * LANES :]
    rows = k.shape[0]
    live = live_row(lengths, rows)
    inv_root = size ** (-0.5)
    carried, extras = [], []
    for h in range(heads):
        cnt = total[:, width + h : width + h + 1]
        centre = jnp.where(
            cnt > 0, total[:, h * size : (h + 1) * size] / jnp.maximum(cnt, 1.0), 0.0
        ).astype(bf16)
        centre_ref[h] = centre
        scores = mt(centre, k[:, h * size : (h + 1) * size]) * inv_root
        peak = jnp.max(jnp.where(live, scores, negative), axis=1, keepdims=True)
        weighted = jnp.where(live, jnp.exp(jnp.where(live, scores - peak, 0.0)), 0.0)
        in_top = in_tops[h].astype(f32)
        mass = jnp.sum(weighted, axis=1, keepdims=True)
        top_mass = jnp.sum(weighted * in_top, axis=1, keepdims=True)
        rest = (weighted * (1.0 - in_top)).astype(bf16)
        carried.append(mm(rest, v[:, h * size : (h + 1) * size]))
        for value in (peak, mass, top_mass):
            extras.extend(parts3(value))
    spare = blocks * LANES - width
    block = jnp.concatenate(carried + [columns(spare, extras, cl_pad)], axis=1).astype(bf16)
    put_blocks(pay, 0, block, cl_rows)


def member_kernel(count, heads, size, cl_rows, lengths, *refs):
    pays = refs[:count]
    q, chosen_ref, hub_ref, prob_ref, top_ref = refs[count:]
    width = heads * size
    blocks = round_up(width + 1, LANES) // LANES
    hub = total_of(pays, blocks * cl_rows, HUBS, 2 * width // LANES).astype(bf16)
    hub_ref[...] = hub
    inv_root = size ** (-0.5)
    probs, outs = [], []
    for h in range(heads):
        keys = hub[:, h * size : (h + 1) * size]
        values = hub[:, width + h * size : width + (h + 1) * size]
        logits = mt(q[:, h * size : (h + 1) * size], keys) * inv_root
        chosen = chosen_ref[:, h * HUBS : (h + 1) * HUBS].astype(f32) > 0.5
        logits = jnp.where(chosen, logits, negative)
        exponent = jnp.where(
            chosen, jnp.exp(logits - jnp.max(logits, axis=1, keepdims=True)), 0.0
        )
        prob = exponent / jnp.sum(exponent, axis=1, keepdims=True)
        probs.append(prob)
        outs.append(mm(prob.astype(bf16), values))
    prob_ref[...] = jnp.concatenate(probs, axis=1)
    top_ref[...] = jnp.concatenate(outs, axis=1)


def combine_kernel(layer, count, heads, size, cl_rows, lengths, *refs):
    pays = refs[:count]
    top_out, members, mine, other, att_ref, top, low, stat_ref, w_out, sems = refs[count:]
    weights = Choice(layer, [(mine, other)], [w_out], [sems.at[0]])
    width = heads * size
    cl_pad = members.shape[2]
    blocks = round_up(width + 1, LANES) // LANES
    tables = [
        pad_rows(get_blocks(ref[...].astype(f32), 0, cl_rows, blocks), cl_pad) for ref in pays
    ]
    base = width - (blocks - 1) * LANES
    shift = lambda block, by: pltpu.roll(block, by % LANES, 1)
    stats = []
    for one in tables:
        block = one[:, (blocks - 1) * LANES :]
        stats.append(block + shift(block, -1) + shift(block, -2))
    peaks = functools.reduce(jnp.maximum, stats)
    scales = [jnp.exp(mine - peaks) for mine in stats]
    masses = sum(mine * shift(scale, 3) for mine, scale in zip(stats, scales))
    top_masses = sum(mine * shift(scale, 6) for mine, scale in zip(stats, scales))
    rows = top_out.shape[0]
    live = live_col(lengths, rows)
    pieces = []
    for h in range(heads):
        at = base + 9 * h
        peak, mass, top_mass = (
            every[:, at + 3 * which : at + 3 * which + 1]
            for which, every in enumerate((peaks, masses, top_masses))
        )
        carried = 0.0
        for one, scale in zip(tables, scales):
            carried = carried + one[:, h * size : (h + 1) * size] * scale[:, at : at + 1]
        safe = jnp.where(mass > 0, mass, 1.0)
        remote = carried / safe
        share = top_mass / safe
        lanes = LANES - size
        stat_ref[h] = jnp.concatenate(
            [carried, columns(lanes, (peak, safe, top_mass, share), cl_pad)], axis=1
        )
        looked = pick_rows(
            members[h], jnp.concatenate([remote, columns(lanes, (share,), cl_pad)], axis=1)
        )
        att = looked[:, size : size + 1] * top_out[:, h * size : (h + 1) * size] + looked[:, :size]
        pieces.append(jnp.where(live, att, 0.0))
    joined = jnp.concatenate(pieces, axis=1).astype(bf16)
    att_ref[...] = joined
    weights.wait(0)
    halves(mm(joined, w_out[...]), top, low)


def gelu_slope(hidden):
    root = (2.0 / 3.141592653589793) ** 0.5
    square = hidden * hidden
    bent = jnp.tanh(root * hidden * (1.0 + 0.044715 * square))
    slope = 0.5 * (1.0 + bent) + 0.5 * hidden * (1.0 - bent * bent) * root * (
        1.0 + 3 * 0.044715 * square
    )
    return (0.5 * hidden * (1.0 + bent)).astype(bf16), slope


def feed_kernel(lengths, *refs):
    source, *four = refs[:5]
    gain_mine, gain_other, in_mine, in_other, back_mine, back_other = refs[5:11]
    x1_ref, n2r, active_ref, slope_ref, top, low, w_in, w_back, sems = refs[11:]
    pairs = [(in_mine, in_other), (back_mine, back_other)]
    weights = Choice(0, pairs, [w_in, w_back], [sems.at[0], sems.at[1]])
    x1 = source[here(SECTION)].astype(f32) + summed(four)
    x1_ref[...] = x1
    hat, _ = layer_stats(x1)
    n2 = (hat * gain_row(gain_mine, gain_other, 0, 1)).astype(bf16)
    weights.wait(0)
    active, slope = gelu_slope(mm(n2, w_in[...]))
    active_ref[...] = active
    slope_ref[...] = slope
    weights.wait(1)
    halves(mm(active, w_back[...]), top, low)
    n2r[...] = n2


def turn_kernel(lengths, *refs):
    source, *four = refs[:5]
    gain_mine, gain_other, cot, in_mine, in_other, back_mine, back_other = refs[5:12]
    x1_ref, n2r, active_ref, dyb_ref, dz_ref, top, low, w_in, w_back, sems = refs[12:]
    pairs = [(in_mine, in_other), (back_mine, back_other)]
    weights = Choice(1, pairs, [w_in, w_back], [sems.at[0], sems.at[1]])
    x1 = source[...] + summed(four)
    x1_ref[...] = x1
    hat, _ = layer_stats(x1)
    n2 = (hat * gain_row(gain_mine, gain_other, 1, 1)).astype(bf16)
    n2r[...] = n2
    weights.wait(0)
    active, slope = gelu_slope(mm(n2, w_in[...]))
    active_ref[...] = active
    dyb = cot[here(SECTION)]
    dyb_ref[...] = dyb
    weights.wait(1)
    dz = (mt(dyb, w_back[...]) * slope).astype(bf16)
    dz_ref[...] = dz
    halves(mt(dz, w_in[...]), top, low)


def late_feed_kernel(layer, lengths, active, mine, other, top, low, w_back, sems):
    weights = Choice(layer, [(mine, other)], [w_back], [sems.at[0]])
    weights.wait(0)
    halves(mm(active[...], w_back[...]), top, low)


def feed_back_kernel(lengths, *refs):
    grad_middle, source, *four = refs[:6]
    gain = gain_row(*refs[6:8], 1, 0)
    slope, back_mine, back_other, in_mine, in_other = refs[8:13]
    dy_ref, gain_ref, dybr, dz_ref, top, low, w_back, w_in, sems = refs[13:]
    pairs = [(back_mine, back_other), (in_mine, in_other)]
    weights = Choice(0, pairs, [w_back, w_in], [sems.at[0], sems.at[1]])
    dy = input_grad(grad_middle, source[...], four, gain, gain_ref)
    dy_ref[...] = dy
    dyb = dy.astype(bf16)
    weights.wait(0)
    dz = (mt(dyb, w_back[...]) * slope[...]).astype(bf16)
    dz_ref[...] = dz
    weights.wait(1)
    halves(mt(dz, w_in[...]), top, low)
    dybr[...] = dyb


def input_grad(grad_middle, source, four, gain, gain_ref):
    grad_normed = summed(four)
    hat, inverse = layer_stats(source)
    if gain_ref is not None:
        gain_ref[...] = jnp.sum(grad_normed * hat, axis=0, keepdims=True)
    return grad_middle[...] + norm_back(grad_normed * gain, hat, inverse)


def input_grad_kernel(lengths, *refs):
    grad_middle, source, *four = refs[:6]
    *gains, gain_two, last_one, last_two, sent, keep, gain_one = refs[6:]
    source = source[here(SECTION)].astype(f32)
    rows = source.shape[0]
    sent[:rows, :] = input_grad(grad_middle, source, four, gain_row(*gains, 0, 0), gain_one)
    first = jnp.concatenate([gain_one[...], gain_two[...]], axis=0)
    last = jnp.concatenate([last_one[...], last_two[...]], axis=0)
    keep[...] = jnp.where(here(SECTION) == 0, first, last)
    give = jnp.where(here(SECTION) == 0, last, first)
    sent[rows:, :] = jnp.concatenate([give, jnp.zeros((6, give.shape[1]), f32)], axis=0)


def middle_back_kernel(layer, heads, size, cl_rows, lengths, *refs):
    four = refs[:4]
    middle, grad_out, gain_mine, gain_other, top_out, members_t = refs[4:10]
    mine, other, dx1_ref, dx1r, dtop_ref, gain_ref, pay, w_out, sems = refs[10:]
    weights = Choice(layer, [(mine, other)], [w_out], [sems.at[0]])
    grad_normed = summed(four)
    hat, inverse = layer_stats(middle[...])
    gain_ref[...] = jnp.sum(grad_normed * hat, axis=0, keepdims=True)
    grad = grad_out[here(SECTION)].astype(f32) if layer == 1 else grad_out[...]
    dx1 = grad + norm_back(
        grad_normed * gain_row(gain_mine, gain_other, layer, 1), hat, inverse
    )
    dx1_ref[...] = dx1
    dx1b = dx1.astype(bf16)
    rows = dx1.shape[0]
    weights.wait(0)
    datt = mt(dx1b, w_out[...])
    dtop = jnp.where(live_col(lengths, rows), datt, 0.0).astype(bf16)
    dtop_ref[...] = dtop
    sums, shares = [], []
    for h in range(heads):
        members = members_t[h]
        own = dtop[:, h * size : (h + 1) * size]
        sums.append(mm(members, own))
        product = own.astype(f32) * top_out[:, h * size : (h + 1) * size]
        both = mm(members, jnp.concatenate(parts2(product), axis=1))
        shares.extend(parts3(jnp.sum(both, axis=1, keepdims=True)))
    width = heads * size
    spare = round_up(width + 1, LANES) - width
    cl_pad = members_t.shape[1]
    block = jnp.concatenate(sums + [columns(spare, shares, cl_pad)], axis=1).astype(bf16)
    put_blocks(pay, 0, block, cl_rows)
    dx1r[...] = dx1b


def member_back_kernel(heads, size, lengths, *refs):
    q, hub_ref, prob_ref, dtop, stat, members, dq_ref, pay = refs
    width = heads * size
    inv_root = size ** (-0.5)
    hub = hub_ref[...]
    dqs, dks, dvs = [], [], []
    for h in range(heads):
        keys = hub[:, h * size : (h + 1) * size]
        values = hub[:, width + h * size : width + (h + 1) * size]
        prob = prob_ref[:, h * HUBS : (h + 1) * HUBS]
        own = dtop[:, h * size : (h + 1) * size]
        share = pick_rows(members[h], stat[h])[:, size + 3 : size + 4]
        da = mt(own, values) * share
        dg = (prob * (da - jnp.sum(prob * da, axis=1, keepdims=True))).astype(bf16)
        dqs.append(mm(dg, keys) * inv_root)
        dks.append(tm(dg, q[:, h * size : (h + 1) * size]) * inv_root)
        scaled = own.astype(f32) * share
        dvs.append(tm(prob.astype(bf16), scaled.astype(bf16)))
    dq_ref[...] = jnp.concatenate(dqs, axis=1)
    put_blocks(pay, 0, jnp.concatenate(dks + dvs, axis=1).astype(bf16), HUBS)


def centroid_back_kernel(count, heads, size, cl_rows, lengths, *refs):
    pays = refs[:count]
    centre_ref, stat, k, v, in_tops, hub_pay, pay, dk_ref, dv_ref = refs[count:]
    width = heads * size
    cl_pad = in_tops.shape[1]
    blocks = round_up(width + 1, LANES) // LANES
    total = pad_rows(total_of(pays, 0, cl_rows, blocks), cl_pad)
    rows = k.shape[0]
    live = live_row(lengths, rows)
    inv_root = size ** (-0.5)
    dcs, dks, dvs = [], [], []
    for h in range(heads):
        keys = k[:, h * size : (h + 1) * size]
        values = v[:, h * size : (h + 1) * size]
        centre = centre_ref[h]
        grad_remote = total[:, h * size : (h + 1) * size]
        at = width + 3 * h
        grad_share = total[:, at : at + 1] + total[:, at + 1 : at + 2] + total[:, at + 2 : at + 3]
        carried = stat[h][:, :size]
        peak = stat[h][:, size : size + 1]
        mass = stat[h][:, size + 1 : size + 2]
        top_mass = stat[h][:, size + 2 : size + 3]
        grad_carried = (grad_remote / mass).astype(bf16)
        grad_top = grad_share / mass
        grad_mass = -(
            jnp.sum(grad_remote * carried, axis=1, keepdims=True) + grad_share * top_mass
        ) / (mass * mass)
        scores = mt(centre, keys) * inv_root
        weighted = jnp.where(live, jnp.exp(jnp.where(live, scores - peak, 0.0)), 0.0)
        in_top = in_tops[h].astype(f32)
        rest = (weighted * (1.0 - in_top)).astype(bf16)
        grad_weighted = (
            (1.0 - in_top) * mt(grad_carried, values) + in_top * grad_top + grad_mass
        )
        grad_scores = (grad_weighted * weighted).astype(bf16)
        dcs.append(mm(grad_scores, keys) * inv_root)
        dks.append(tm(grad_scores, centre) * inv_root)
        dvs.append(tm(rest, grad_carried))
    spare = blocks * LANES - width
    block = jnp.concatenate(dcs + [jnp.zeros((cl_pad, spare), f32)], axis=1).astype(bf16)
    put_blocks(pay, 0, block, cl_rows)
    pay[blocks * cl_rows :, :] = hub_pay[...]
    dk_ref[...] = jnp.concatenate(dks, axis=1)
    dv_ref[...] = jnp.concatenate(dvs, axis=1)


def project_back_kernel(layer, count, heads, size, cl_rows, lengths, *refs):
    pays = refs[:count]
    dq_top, dk_c, dv_c, cnt_ref, members, own_pick, mine, other = refs[count : count + 8]
    dqkv_ref, top, low, w_qkv, sems = refs[count + 8 :]
    weights = Choice(layer, [(mine, other)], [w_qkv], [sems.at[0]])
    width = heads * size
    cl_pad = members.shape[2]
    blocks = round_up(width + 1, LANES) // LANES
    total = pad_rows(total_of(pays, 0, cl_rows, blocks), cl_pad)
    hub = total_of(pays, blocks * cl_rows, HUBS, 2 * width // LANES)
    high, low_part = parts2(hub)
    spread = tm(own_pick[...], high) + tm(own_pick[...], low_part)
    rows = dq_top.shape[0]
    live = live_col(lengths, rows)
    base = round_up(width + 1, LANES) - LANES
    dqs = []
    for h in range(heads):
        at = width - base + h
        cnt = jnp.maximum(cnt_ref[:, at : at + 1], 1.0)
        from_centre = pick_rows(members[h], total[:, h * size : (h + 1) * size] / cnt)
        dqs.append(jnp.where(live, from_centre, 0.0))
    dq = (dq_top[...] + jnp.concatenate(dqs, axis=1)).astype(bf16)
    dk = (dk_c[...] + spread[:, :width]).astype(bf16)
    dv = (dv_c[...] + spread[:, width:]).astype(bf16)
    dqkv_ref[...] = jnp.concatenate([dq, dk, dv], axis=1)
    weights.wait(0)
    halves(mm(dq, w_qkv[0]) + mm(dk, w_qkv[1]) + mm(dv, w_qkv[2]), top, low)


def feed_grads_kernel(lengths, dyb, active, n2, dz, keep, give):
    back = tm(dyb[...], active[...]).astype(bf16)
    into = tm(n2[...], dz[...]).astype(bf16)

    @pl.when(here(SECTION) == 0)
    def _():
        keep[...] = back
        give[...] = into

    @pl.when(here(SECTION) == 1)
    def _():
        keep[...] = into
        give[...] = back


def attention_grads_kernel(count, lengths, n1, dqkv, dx1b, att, keep, give):
    part = n1.shape[1] // count
    half = part // 2
    both = jnp.concatenate([tm(n1[...], dqkv[...]), tm(dx1b[...], att[...])], axis=1).astype(bf16)

    def put(ref, first):
        for at in range(count):
            ref[at] = both[at * part + first : at * part + first + half]

    @pl.when(here(SECTION) == 0)
    def _():
        put(keep, 0)
        put(give, half)

    @pl.when(here(SECTION) == 1)
    def _():
        put(keep, half)
        put(give, 0)


def chip_sum_kernel(lengths, mine, far, keep, give):
    me = here(SEQ)
    for at in range(keep.shape[0]):
        stay, go = 2 * at + me % 2, 2 * at + 1 - me % 2
        keep[at] = (mine[stay].astype(f32) + far[stay].astype(f32)).astype(bf16)
        give[at] = (mine[go].astype(f32) + far[go].astype(f32)).astype(bf16)


def pair_sum_kernel(lengths, mine, far, keep, give):
    stay = here(SEQ) // 2
    go = 1 - stay
    keep[...] = (mine[stay].astype(f32) + far[stay].astype(f32)).astype(bf16)
    give[...] = (mine[go].astype(f32) + far[go].astype(f32)).astype(bf16)


def sorted_sum_kernel(lengths, mine, far, *outs):
    for k, out in enumerate(outs):
        at = lax.rem(here(SEQ) + k, len(outs))
        out[...] = (mine[at].astype(f32) + far[at].astype(f32)).astype(bf16)


def seq_sum_kernel(lengths, *refs):
    total = refs[0][...].astype(f32)
    for ref in refs[1:-1]:
        total = total + ref[...].astype(f32)
    refs[-1][...] = total


def ship_kernel(sums, lengths, *refs):
    row = 0
    out = refs[-1]
    for at in range(sums):
        mine, far = refs[2 * at : 2 * at + 2]
        out[row : row + mine.shape[0], :] = mine[...].astype(f32) + far[...].astype(f32)
        row += mine.shape[0]
    grad, source, *four = refs[2 * sums : -1]
    out[row : row + grad.shape[0], :] = grad[...]
    row += grad.shape[0]
    out[row:, :] = source[...] + summed(four)


def feed_owner_kernel(lengths, first, first_far, shipped, shipped_far, back, into, token):
    rows = first.shape[0]
    token[...] = jnp.zeros_like(token)

    @pl.when(here(SECTION) == 0)
    def _():
        back[...] = first[...]
        into[...] = first_far[...]

    @pl.when(here(SECTION) == 1)
    def _():
        into[...] = shipped[:rows, :]
        back[...] = shipped_far[:rows, :]


def attention_owner_kernel(width, start, lengths, first, first_far, shipped, shipped_far, grad_qkv, grad_out):
    rows = first.shape[0]

    def put(low_half, high_half):
        both = jnp.concatenate([low_half, high_half], axis=0)
        for at in range(3):
            grad_qkv[at] = both[:, at * width : (at + 1) * width]
        grad_out[...] = both[:, 3 * width :].T

    @pl.when(here(SECTION) == 0)
    def _():
        put(first[...], first_far[...])

    @pl.when(here(SECTION) == 1)
    def _():
        put(shipped_far[start : start + rows, :], shipped[start : start + rows, :])


def place_kernel(start, lengths, own_first, far_first, shipped, shipped_far, out, token):
    rows = out.shape[1]
    token[...] = jnp.zeros_like(token)

    @pl.when(here(SECTION) == 0)
    def _():
        out[0] = own_first[:rows, :]
        out[1] = far_first[:rows, :]

    @pl.when(here(SECTION) == 1)
    def _():
        out[0] = shipped_far[start : start + rows, :]
        out[1] = shipped[start : start + rows, :]


def gain_kernel(lengths, keep, sent_far, out):
    rows = sent_far.shape[0] - 8
    out[...] = keep[...] + sent_far[rows : rows + 2, :]


def moved(block, axis, target):
    devices = range(lax.axis_size(axis))
    return lax.ppermute(block, axis, [(i, target(i)) for i in devices])


def swap(block):
    return moved(block, SECTION, lambda i: i ^ 1)


def every_seq(block):
    count = lax.axis_size(SEQ)
    if count > DIRECT:
        gathered = lax.all_gather(block, SEQ)
        return [gathered[at] for at in range(count)]
    return [block] + [
        moved(block, SEQ, lambda i, k=k: (i + k) % count) for k in range(1, count)
    ]


def every_head(block):
    return [block] + [
        moved(block, HEAD, lambda i, k=k: i ^ k) for k in range(1, lax.axis_size(HEAD))
    ]


def every_head_in_turn(block):
    pieces = [block]
    distance = 1
    while distance < lax.axis_size(HEAD):
        pieces += [moved(piece, HEAD, lambda i: i ^ distance) for piece in pieces]
        distance *= 2
    return pieces


def fold_kernel(lengths, top_a, top_b, low_a, low_b, top, low):
    top[...] = (top_a[...].astype(f32) + top_b[...].astype(f32)).astype(bf16)
    low[...] = (low_a[...].astype(f32) + low_b[...].astype(f32)).astype(bf16)


def head_sum(top, low, run, before_fold=None):
    distances = [1 << at for at in range(lax.axis_size(HEAD).bit_length() - 1)]
    for step in range(len(distances)):
        one = distances[step]
        other = distances[len(distances) - 1 - step]
        far_top = moved(top, HEAD, lambda i: i ^ one)
        far_low = moved(low, HEAD, lambda i: i ^ other)
        if step < len(distances) - 1:
            ties = before_fold() if before_fold and step == 0 else []
            shape = [shaped(top.shape, bf16)] * 2
            top, low = run(
                fold_kernel, shape, [top, far_top, low, far_low], ties=ties
            )
    return (top, far_top, low, far_low)


def to_core(block, layer):
    return lax.ppermute(block, SECTION, [(1 - layer, layer)])


def seq_xor(block, distance):
    return moved(block, SEQ, lambda i: i ^ distance)


def pair_step(keep, far, run, ties=()):
    half = shaped((keep.shape[0] // 2,) + keep.shape[1:], bf16)
    keep, give = run(chip_sum_kernel, [half] * 2, [keep, far], ties=ties)
    return keep, seq_xor(give, 1)


def far_step(keep, far, run, ties=()):
    keep, give = run(
        pair_sum_kernel, [shaped(keep.shape[1:], bf16)] * 2, [keep, far], ties=ties
    )
    return keep, seq_xor(give, 2)


def shards(tokens, cotangent, lengths, clusters, top_index, w_qkv, w_out, w_in, w_back, gains):
    section = lax.axis_index(SECTION)
    me = lax.axis_index(SEQ)
    count = lax.axis_size(SEQ)
    head_devices = lax.axis_size(HEAD)
    micro, rows, dim = tokens.shape
    _, heads, cluster_count, slots = top_index.shape
    size = w_qkv.shape[3] // heads
    width = heads * size
    hidden = w_in.shape[2]
    total_rows = rows * count
    cl_pad = round_up(cluster_count, LANES)
    cl_rows = round_up(cluster_count, 16)
    high_rows = round_up(max(total_rows // LANES, 1), 16)
    blocks = round_up(width + 1, LANES) // LANES
    hub_blocks = 2 * width // LANES
    sizes = (heads, size, cl_rows)
    run = lambda kernel, outs, args, **kw: call(kernel, outs, lengths, args, **kw)
    part = functools.partial
    fours = [shaped((rows // 2, dim), bf16)] * 2
    pay_shape = shaped((blocks * cl_rows, LANES), bf16)
    table_shape = shaped((heads, cl_pad, rows), bf16)
    square = shaped((dim, hidden), bf16)
    qkv_buf = shaped((3, width, dim), bf16)

    qkv_t = w_qkv[0].transpose(0, 2, 1)
    qkv_pair = (qkv_t, swap(qkv_t))
    gain_pair = (gains[0], swap(gains[0]))
    tops = top_index.transpose(0, 1, 3, 2)
    clusters = clusters.transpose(1, 0, 2)
    out_pair = (w_out[0], swap(w_out[0]))
    in_pair = (w_in[0], swap(w_in[0]))
    back_pair = (w_back[0], swap(w_back[0]))
    own_pick, hubs, members_t = run(
        part(rank_kernel, heads, cl_pad),
        [shaped((HUBS, rows), bf16), shaped((high_rows, LANES)), table_shape],
        [tops, clusters],
    )

    source, lists = tokens, None
    kept, acts = [], []
    for layer in range(2):
        outs = [
            shaped((rows, dim), bf16),
            shaped((rows, width), bf16),
            shaped((rows, width), bf16),
            shaped((rows, width), bf16),
            shaped((blocks * cl_rows + hub_blocks * HUBS, LANES), bf16),
        ]
        if layer:
            outs = [shaped((rows, dim))] + outs
        found = run(
            part(project_kernel, layer, *sizes),
            outs,
            ([tokens] if layer == 0 else [x1, *four])
            + [*gain_pair, members_t, own_pick],
            anys=qkv_pair,
            bufs=[qkv_buf],
        )
        if layer:
            source, *found = found
            acts.append(source)
            acts_far = to_core(source, 0)
        n1r, q, k, v, pay = found
        pays = every_seq(pay)
        if lists is None:
            in_tops, chosen, members = lists = run(
                part(list_kernel, heads, cl_pad),
                [
                    table_shape,
                    shaped((rows, heads * HUBS), bf16),
                    shaped((heads, rows, cl_pad), bf16),
                ],
                [tops, clusters, hubs, own_pick],
            )
        centre, cnt, pay = run(
            part(centroid_kernel, len(pays), *sizes),
            [shaped((heads, cl_pad, size), bf16), shaped((cl_pad, LANES)), pay_shape],
            [*pays, k, v, in_tops],
        )
        stats = every_seq(pay)
        hub, prob, top_out = run(
            part(member_kernel, len(pays), *sizes),
            [
                shaped((HUBS, 2 * width), bf16),
                shaped((rows, heads * HUBS)),
                shaped((rows, width)),
            ],
            [*pays, q, chosen],
            ties=[in_pair[1]] if layer == 0 else [acts_far],
        )
        att, top, low, stat = run(
            part(combine_kernel, layer, len(stats), *sizes),
            [shaped((rows, width), bf16)] + fours + [shaped((heads, cl_pad, LANES))],
            [*stats, top_out, members],
            anys=out_pair,
            bufs=[shaped((width, dim), bf16)],
        )
        four = head_sum(top, low, run)
        by_token = [shaped((rows, dim)), shaped((rows, dim), bf16), shaped((rows, hidden), bf16)]
        if layer == 0:
            x1, n2r, active, slope, *parts = run(
                feed_kernel,
                by_token + [shaped((rows, hidden))] + fours,
                [source, *four, *gain_pair],
                anys=[*in_pair, *back_pair],
                bufs=[square, square],
            )
            four = head_sum(*parts, run)
        else:
            slope = None
            x1, n2r, active, dyb, dz, *parts = run(
                turn_kernel,
                by_token + [shaped((rows, dim), bf16), shaped((rows, hidden), bf16)] + fours,
                [source, *four, *gain_pair, cotangent],
                anys=[*in_pair, *back_pair],
                bufs=[square, square],
            )
        kept.append(
            (source, n1r, q, k, v, centre, cnt, hub, prob, top_out, att, stat, x1, n2r, active, slope)
        )

    direct = count == DIRECT
    seq_part = dim // count
    half = seq_part // 2
    extra = 16
    if not direct:
        seq_part = half = None

    def plain_sum(grad, layer):
        total = grad.astype(f32) + to_core(grad.astype(bf16), layer).astype(f32)
        return lax.psum_scatter(
            total.astype(bf16), SEQ, scatter_dimension=0, tiled=True
        ).astype(f32)

    def feed_grads(layer, dyb, dz, ties=()):
        active, n2 = kept[layer][14], kept[layer][13]
        if not direct:
            return plain_sum(tm(dyb, active), layer), plain_sum(tm(n2, dz), layer)
        return run(
            feed_grads_kernel, [square] * 2, [dyb, active, n2, dz], ties=ties
        )

    def attention_grads(layer, dqkv, dx1b):
        n1, att = kept[layer][1], kept[layer][10]
        if not direct:
            return plain_sum(jnp.concatenate([tm(n1, dqkv), tm(dx1b, att)], axis=1), layer)
        return run(
            part(attention_grads_kernel, count),
            [shaped((count, half, 4 * width), bf16)] * 2,
            [n1, dqkv, dx1b, att],
        )

    def swapped(made):
        far = swap(made[1])
        shape = (count, -1, made[0].shape[-1])
        return made[0].reshape(shape), far.reshape(shape)

    def middle_back(layer, four, dy, ties):
        top_out, x1 = kept[layer][9], kept[layer][12]
        return run(
            part(middle_back_kernel, layer, *sizes),
            [
                shaped((rows, dim)),
                shaped((rows, dim), bf16),
                shaped((rows, width), bf16),
                shaped((1, dim)),
                pay_shape,
            ],
            [*four, x1, dy, *gain_pair, top_out, members_t],
            anys=out_pair,
            bufs=[shaped((width, dim), bf16)],
            ties=ties,
        )

    def member_back(layer, dtop, ties=()):
        _, _, q, _, _, _, _, hub, prob, _, _, stat = kept[layer][:12]
        return run(
            part(member_back_kernel, heads, size),
            [shaped((rows, width)), shaped((hub_blocks * HUBS, LANES), bf16)],
            [q, hub, prob, dtop, stat, members],
            ties=ties,
        )

    def centroid_back(layer, pays, hub_pay, ties):
        _, _, _, k, v, centre, _, _, _, _, _, stat = kept[layer][:12]
        return run(
            part(centroid_back_kernel, len(pays), *sizes),
            [
                shaped((blocks * cl_rows + hub_blocks * HUBS, LANES), bf16),
                shaped((rows, width)),
                shaped((rows, width)),
            ],
            [*pays, centre, stat, k, v, in_tops, hub_pay],
            ties=ties,
        )

    def project_back(layer, pays, dq_top, dk, dv, ties):
        cnt = kept[layer][6]
        return run(
            part(project_back_kernel, layer, len(pays), *sizes),
            [shaped((rows, 3 * width), bf16)] + fours,
            [*pays, dq_top, dk, dv, cnt, members, own_pick],
            anys=qkv_pair,
            bufs=[qkv_buf],
            ties=ties,
        )

    def shared(pay):
        return every_seq(pay)

    def step(parts, axis, one, other):
        return [parts[0], moved(parts[0], axis, lambda i: i ^ one),
                    parts[1], moved(parts[1], axis, lambda i: i ^ other)]

    def fold(four, ties):
        return run(fold_kernel, fours, four, ties=ties)

    def ended(group, layer, ties):
        (total,) = run(seq_sum_kernel, [shaped(group[0].shape)], group, ties=ties)
        return [total, to_core(total, layer)]

    near, away = 1, head_devices // 2
    assert head_devices == 4
    only = lambda items: list(items) if direct else []

    backs = [shaped((rows, dim), bf16), shaped((rows, hidden), bf16)] + fours
    four = step(parts, HEAD, near, away)
    parts = fold(four, [])
    four = step(parts, HEAD, away, near)
    dx1, dx1b, dtop, gain_two, pay = middle_back(1, four, cotangent, [])
    feed_last = feed_grads(1, dyb, dz, parts)
    pays = shared(pay)
    dq_top, hub_pay = member_back(1, dtop)
    pay, dk, dv = centroid_back(1, pays, hub_pay, only(feed_last))
    if direct:
        feed_last = swapped(feed_last)
    late_parts = run(
        part(late_feed_kernel, 1),
        fours,
        [kept[1][14]],
        anys=back_pair,
        bufs=[square],
        ties=pays[1:] + [hub_pay],
    )
    late = step(late_parts, HEAD, near, away)
    pays = shared(pay)
    if direct:
        feed_last = pair_step(*feed_last, run, pays[1:])
    dqkv, *parts = project_back(
        1, pays, dq_top, dk, dv, [late[1], late[3]] + only(feed_last[:1])
    )
    four = step(parts, HEAD, near, away)
    parts = fold(four, [])
    four = step(parts, HEAD, away, near)
    attention_last = attention_grads(1, dqkv, dx1b)
    if direct:
        feed_last = far_step(*feed_last, run)
        attention_last = swapped(attention_last)
        attention_last = pair_step(*attention_last, run)
    dy, gain_one, dyb, dz, *parts = run(
        feed_back_kernel,
        [shaped((rows, dim)), shaped((1, dim))] + backs,
        [dx1, kept[1][0], *four, *gain_pair, kept[0][15]],
        anys=[*back_pair, *in_pair],
        bufs=[square, square],
        ties=only([feed_last[0], attention_last[0]]),
    )
    last_grad, last_gains = dy, [gain_one, gain_two]
    four = step(parts, HEAD, near, away)
    parts = fold(four, only([attention_last[1], feed_last[1]]))
    if direct:
        attention_last = far_step(*attention_last, run, parts)
    four = step(parts, HEAD, away, near)
    feed_first = feed_grads(0, dyb, dz, parts)
    dx1, dx1b, dtop, gain_two, pay = middle_back(
        0, four, dy, only(feed_first)
    )
    pays = shared(pay)
    dq_top, hub_pay = member_back(0, dtop)
    if direct:
        feed_first = swapped(feed_first)
    pay, dk, dv = centroid_back(
        0, pays, hub_pay, only([feed_first[1], attention_last[1]])
    )
    late_parts = fold(late, [dk])
    late = step(late_parts, HEAD, away, near)
    pays = shared(pay)
    if direct:
        feed_first = pair_step(*feed_first, run, pays[1:])
    dqkv, *parts = project_back(
        0, pays, dq_top, dk, dv, [late[1], late[3]] + only(feed_first[:1])
    )
    four = step(parts, HEAD, near, away)
    attention_first = attention_grads(0, dqkv, dx1b)
    before = []
    if direct:
        attention_first = swapped(attention_first)
        attention_first = pair_step(*attention_first, run)
        feed_first = far_step(*feed_first, run)
        before = [attention_first[0], feed_first[0]]
    parts = fold(four, before)
    four = step(parts, HEAD, away, near)
    sums = [*feed_last, *attention_last] if direct else []
    sum_rows = (seq_part + half) if direct else 0
    (shipped,) = run(
        part(ship_kernel, len(sums) // 2),
        [shaped((sum_rows + 2 * rows, dim))],
        [*sums, last_grad, kept[1][12], *late],
        ties=parts,
    )
    shipped = [shipped, to_core(shipped, 1)]
    if direct:
        attention_first = far_step(*attention_first, run, parts)
    sent, own_gains, _ = run(
        input_grad_kernel,
        [shaped((rows + 8, dim)), shaped((2, dim)), shaped((1, dim))],
        [dx1, tokens, *four, *gain_pair, gain_two, *last_gains],
        ties=only(attention_first[:1]) + shipped,
    )
    sent_far = swap(sent)
    token = shaped((8, LANES))
    (placed_acts, acts_token), (placed_grads, grads_token) = (
        run(part(place_kernel, start), [shaped((2, rows, dim)), token], [*first, *shipped])
        for start, first in (
            (sum_rows + rows, (acts[0], acts_far)),
            (sum_rows, (sent, sent_far)),
        )
    )
    (gain_sum,) = run(gain_kernel, [shaped((2, dim))], [own_gains, sent_far])
    if direct:
        gain_sum = gain_sum + seq_xor(gain_sum, 1)
        gain_far = seq_xor(gain_sum, 2)
        gain_sum = gain_sum + gain_far
        gain_sum = lax.dynamic_slice_in_dim(gain_sum, me * seq_part, seq_part, 1)
        feed_first = ended(feed_first, 0, [acts_token])
        back, into, feed_token = run(
            feed_owner_kernel, [shaped((seq_part, hidden))] * 2 + [token], [*feed_first, *shipped]
        )
        attention_first = ended(
            attention_first, 0, [feed_token, grads_token, gain_far]
        )
        grad_qkv, grad_out = run(
            part(attention_owner_kernel, width, seq_part),
            [shaped((3, seq_part, width)), shaped((width, seq_part))],
            [*attention_first, *shipped],
        )
    else:
        pick = lambda one, two: jnp.where(section == 0, one, two)
        gain_sum = lax.psum_scatter(gain_sum, SEQ, scatter_dimension=1, tiled=True)
        back, into = (pick(feed_first[at], feed_last[at]) for at in range(2))
        both = pick(attention_first, attention_last)
        grad_qkv = both[:, : 3 * width].reshape(-1, 3, width).transpose(1, 0, 2)
        grad_out = both[:, 3 * width :].T
    return (
        placed_acts[None],
        placed_grads[None],
        grad_qkv[None],
        grad_out[None],
        into[None],
        back.T[None],
        gain_sum[None],
    )


def solution(mesh):
    placed = (
        P(None, SEQ, None),
        P(None, SEQ, None),
        P(),
        P(None, HEAD, SEQ),
        P(None, HEAD, None, None),
        P(SECTION, None, None, HEAD),
        P(SECTION, HEAD, None),
        P(SECTION, None, HEAD),
        P(SECTION, HEAD, None),
        P(SECTION, None, None),
    )
    return jax.shard_map(
        shards,
        mesh=mesh,
        in_specs=placed,
        out_specs=(
            P(SECTION, None, SEQ, None),
            P(SECTION, None, SEQ, None),
            P(SECTION, None, SEQ, HEAD),
            P(SECTION, HEAD, SEQ),
            P(SECTION, SEQ, HEAD),
            P(SECTION, HEAD, SEQ),
            P(SECTION, None, SEQ),
        ),
        check_vma=False,
    )
```

```python
import functools

import jax
import jax.numpy as jnp
from jax import lax
from jax.experimental import pallas as pl
from jax.experimental.pallas import tpu as pltpu
from jax.sharding import PartitionSpec as P

SECTION, SEQ, HEAD = "section", "seq", "head"
epsilon = 1e-05
negative = -1e30
f32 = jnp.float32
bf16 = jnp.bfloat16
LANES = 128
HUBS = 64
VMEM_LIMIT = 32 * 1024 * 1024
DIRECT = 4


def round_up(value, step):
    return -(-value // step) * step


def iota(shape, dim):
    return lax.broadcasted_iota(jnp.int32, shape, dim)


def mm(a, b):
    return lax.dot_general(a, b, (((1,), (0,)), ((), ())), preferred_element_type=f32)


def mt(a, b):
    return lax.dot_general(a, b, (((1,), (1,)), ((), ())), preferred_element_type=f32)


def tm(a, b):
    return lax.dot_general(a, b, (((0,), (0,)), ((), ())), preferred_element_type=f32)


def parts2(v):
    high = v.astype(bf16)
    return high, (v - high.astype(f32)).astype(bf16)


def parts3(v):
    high = v.astype(bf16)
    rest = v - high.astype(f32)
    mid = rest.astype(bf16)
    return high.astype(f32), mid.astype(f32), rest - mid.astype(f32)


def pick_rows(one_hot, table):
    high, low = parts2(table)
    return mm(one_hot, high) + mm(one_hot, low)


def layer_stats(values):
    centred = values - jnp.mean(values, axis=-1, keepdims=True)
    inverse = lax.rsqrt(jnp.mean(centred * centred, axis=-1, keepdims=True) + epsilon)
    return centred * inverse, inverse


def norm_back(grad_hat, normed, inverse):
    return inverse * (
        grad_hat
        - jnp.mean(grad_hat, axis=-1, keepdims=True)
        - normed * jnp.mean(grad_hat * normed, axis=-1, keepdims=True)
    )


def columns(base_width, cols, rows):
    lane = iota((rows, base_width), 1)
    out = jnp.zeros((rows, base_width), f32)
    for at, col in enumerate(cols):
        out = jnp.where(lane == at, col, out)
    return out


def here(name):
    return lax.axis_index(name)


def live_row(lengths, rows):
    return (here(SEQ) * rows + iota((1, rows), 1)) < lengths[here(SECTION)]


def live_col(lengths, rows):
    return (here(SEQ) * rows + iota((rows, 1), 0)) < lengths[here(SECTION)]


def gain_row(mine, other, layer, row):
    return jnp.where(
        here(SECTION) == layer,
        mine[row : row + 1, :].astype(f32),
        other[row : row + 1, :].astype(f32),
    )


class Choice:
    def __init__(self, layer, pairs, bufs, sems):
        self.copies = [
            (pltpu.make_async_copy(mine, buf, sem), pltpu.make_async_copy(other, buf, sem))
            for (mine, other), buf, sem in zip(pairs, bufs, sems)
        ]
        mine_here = here(SECTION) == layer

        @pl.when(mine_here)
        def _():
            for mine, _other in self.copies:
                mine.start()

        @pl.when(jnp.logical_not(mine_here))
        def _():
            for _mine, other in self.copies:
                other.start()

    def wait(self, at):
        self.copies[at][0].wait()


def summed(four):
    top_a, top_b, low_a, low_b = four
    return jnp.concatenate(
        [
            top_a[...].astype(f32) + top_b[...].astype(f32),
            low_a[...].astype(f32) + low_b[...].astype(f32),
        ],
        axis=0,
    )


def halves(values, top, low):
    half = values.shape[0] // 2
    top[...] = values[:half].astype(bf16)
    low[...] = values[half:].astype(bf16)


def call(kernel, outs, lengths, args, anys=(), bufs=(), ties=(), sems=None, outs_any=False):
    vmem = pl.BlockSpec(memory_space=pltpu.VMEM)
    anywhere = pl.BlockSpec(memory_space=pl.ANY)
    args, anys, ties = list(args), list(anys), list(ties)
    moved_bytes = sum(a.size * a.dtype.itemsize for a in args + list(outs) + list(bufs))
    first, last = 1 + len(args) + len(anys), 1 + len(args) + len(anys) + len(ties)

    def body(*refs):
        kernel(*refs[:first], *refs[last:])

    scratch = [pltpu.VMEM(b.shape, b.dtype) for b in bufs]
    if bufs or sems:
        scratch.append(pltpu.SemaphoreType.DMA((sems or len(bufs),)))
    whole = kernel.func if isinstance(kernel, functools.partial) else kernel
    with jax.named_scope(whole.__name__):
        return pl.pallas_call(
            body,
            out_shape=outs,
            in_specs=[pl.BlockSpec(memory_space=pltpu.SMEM)]
            + [vmem] * len(args)
            + [anywhere] * (len(anys) + len(ties)),
            out_specs=[anywhere if outs_any else vmem] * len(outs),
            scratch_shapes=scratch,
            compiler_params=pltpu.CompilerParams(vmem_limit_bytes=VMEM_LIMIT),
            cost_estimate=pl.CostEstimate(
                flops=0, bytes_accessed=moved_bytes, transcendentals=0
            ),
        )(lengths, *args, *anys, *ties)


def shaped(shape, dtype=f32):
    return jax.ShapeDtypeStruct(tuple(shape), dtype)


def named_rows(tops, head, clusters_pad):
    section = here(SECTION)
    slots, clusters = tops.shape[2:]
    rows = tops[section, head]
    if clusters < clusters_pad:
        rows = jnp.concatenate(
            [rows, jnp.full((slots, clusters_pad - clusters), -1, jnp.int32)], axis=1
        )
    return jnp.concatenate([rows[at : at + 1, :] for at in range(slots)], axis=1)


def cluster_row(clusters, head):
    return clusters[head, pl.ds(here(SECTION), 1), :]


def rank_kernel(heads, cl_pad, lengths, tops, clusters, own_pick, hubs, members_t):
    rows = own_pick.shape[1]
    high_rows = hubs.shape[0]
    named = None
    for h in range(heads):
        position = named_rows(tops, h, cl_pad)
        entries = position.shape[1]
        high_hot = (iota((high_rows, entries), 0) == position // LANES).astype(f32).astype(bf16)
        low_hot = (iota((LANES, entries), 0) == position % LANES).astype(f32).astype(bf16)
        found = mt(high_hot, low_hot)
        named = found if named is None else named + found
    named = named > 0.5
    mask = named.astype(f32).astype(bf16)
    upper = (iota((LANES, LANES), 0) <= iota((LANES, LANES), 1)).astype(f32).astype(bf16)
    before = (iota((high_rows, high_rows), 1) < iota((high_rows, high_rows), 0)).astype(f32)
    rank = mm(mask, upper) + jnp.sum(mm(before.astype(bf16), mask), axis=1, keepdims=True)
    rank = jnp.where(named, rank, 0.0)
    hubs[...] = rank
    first = here(SEQ) * (rows // LANES)
    at_row = iota((high_rows, LANES), 0)
    own = jnp.concatenate(
        [
            jnp.sum(jnp.where(at_row == first + r, rank, 0.0), axis=0, keepdims=True)
            for r in range(rows // LANES)
        ],
        axis=1,
    )
    hub_row = iota((HUBS, rows), 0).astype(f32) + 1.0
    own_pick[...] = (hub_row == own).astype(f32).astype(bf16)
    live = live_row(lengths, rows)
    for h in range(heads):
        same = iota((cl_pad, rows), 0) == cluster_row(clusters, h)
        members_t[h] = (same & live).astype(f32).astype(bf16)


def list_kernel(heads, cl_pad, lengths, tops, clusters, hubs, own_pick, in_top, chosen, members):
    slots = tops.shape[2]
    rows = own_pick.shape[1]
    high_rows = hubs.shape[0]
    rank = hubs[...].astype(bf16)
    for h in range(heads):
        position = named_rows(tops, h, cl_pad)
        entries = position.shape[1]
        high_hot = (iota((high_rows, entries), 0) == position // LANES).astype(f32).astype(bf16)
        by_low = tm(rank, high_hot)
        hub_of = jnp.sum(
            jnp.where(iota((LANES, entries), 0) == position % LANES, by_low, 0.0),
            axis=0,
            keepdims=True,
        )
        hub_row = iota((HUBS, cl_pad), 0).astype(f32) + 1.0
        in_list = jnp.zeros((HUBS, cl_pad), f32)
        for at in range(slots):
            row = hub_of[:, at * cl_pad : (at + 1) * cl_pad]
            in_list = jnp.where(hub_row == row, 1.0, in_list)
        in_list = in_list.astype(bf16)
        in_top[h] = tm(in_list, own_pick[...]).astype(bf16)
        same = (iota((cl_pad, rows), 0) == cluster_row(clusters, h)).astype(f32)
        table = same.T.astype(bf16)
        members[h] = table
        chosen[:, h * HUBS : (h + 1) * HUBS] = mt(table, in_list).astype(bf16)


def project_kernel(layer, heads, size, cl_rows, lengths, *refs):
    if layer == 0:
        source, gain_mine, gain_other, members_t, own_pick, w_mine, w_other = refs[:7]
        n1r, q, k, v, pay, w_qkv, sems = refs[7:]
    else:
        source, *four = refs[:5]
        gain_mine, gain_other, members_t, own_pick, w_mine, w_other = refs[5:11]
        y, n1r, q, k, v, pay, w_qkv, sems = refs[11:]
    weights = Choice(layer, [(w_mine, w_other)], [w_qkv], [sems.at[0]])
    if layer == 0:
        x = source[here(SECTION)].astype(f32)
    else:
        x = source[...] + summed(four)
        y[...] = x
    hat, _ = layer_stats(x)
    n1 = (hat * gain_row(gain_mine, gain_other, layer, 0)).astype(bf16)
    weights.wait(0)
    qv = mt(n1, w_qkv[0]).astype(bf16)
    kv = mt(n1, w_qkv[1]).astype(bf16)
    vv = mt(n1, w_qkv[2]).astype(bf16)
    q[...] = qv
    k[...] = kv
    v[...] = vv
    sums = [mm(members_t[h], qv[:, h * size : (h + 1) * size]) for h in range(heads)]
    width = heads * size
    spare = round_up(width + 1, LANES) - width
    cl_pad = members_t.shape[1]
    if layer == 0:
        counts = [jnp.sum(members_t[h].astype(f32), axis=1, keepdims=True) for h in range(heads)]
        block = jnp.concatenate(sums + [columns(spare, counts, cl_pad)], axis=1).astype(bf16)
        put_blocks(pay, 0, block, cl_rows)
        start = cl_rows * (block.shape[1] // LANES)
    else:
        put_table(pay, jnp.concatenate(sums, axis=1).astype(bf16), cl_rows)
        start = cl_rows + cl_pad // 2
    both = jnp.concatenate([mm(own_pick[...], kv), mm(own_pick[...], vv)], axis=1).astype(bf16)
    put_blocks(pay, start, both, HUBS)
    n1r[...] = n1


def put_blocks(ref, start, block, rows):
    for at in range(block.shape[1] // LANES):
        ref[start + at * rows : start + (at + 1) * rows, :] = block[
            :rows, at * LANES : (at + 1) * LANES
        ]


def get_blocks(values, start, rows, count):
    return jnp.concatenate(
        [values[start + at * rows : start + (at + 1) * rows] for at in range(count)], axis=1
    )


def total_of(refs, start, rows, count):
    total = None
    for ref in refs:
        piece = ref[start : start + rows * count, :].astype(f32)
        total = piece if total is None else total + piece
    return get_blocks(total, 0, rows, count)


def put_table(ref, block, rows):
    half = block.shape[0] // 2
    ref[:rows, :] = block[:rows, :LANES]
    odd = block[:, LANES:]
    ref[rows : rows + half, :] = jnp.concatenate([odd[:half], odd[half:]], axis=1)


def table_of(refs, rows, clusters_pad):
    total = None
    end = rows + clusters_pad // 2
    for ref in refs:
        piece = ref[:end, :].astype(f32)
        total = piece if total is None else total + piece
    odd = total[rows:]
    half = odd.shape[1] // 2
    return jnp.concatenate(
        [
            pad_rows(total[:rows], clusters_pad),
            jnp.concatenate([odd[:, :half], odd[:, half:]], axis=0),
        ],
        axis=1,
    )


def pad_rows(values, rows):
    extra = rows - values.shape[0]
    if extra == 0:
        return values
    return jnp.concatenate([values, jnp.zeros((extra, values.shape[1]), values.dtype)], axis=0)


def centroid_kernel(layer, count, heads, size, cl_rows, lengths, *refs):
    pays = refs[:count]
    k, v, in_tops, *more = refs[count:]
    width = heads * size
    cl_pad = in_tops.shape[1]
    blocks = round_up(width + 1, LANES) // LANES
    if layer == 0:
        centre_ref, cnt_ref, pay = more
        total = pad_rows(total_of(pays, 0, cl_rows, blocks), cl_pad)
        counts = total[:, (blocks - 1) * LANES :]
        cnt_ref[...] = counts
    else:
        cnt_ref, centre_ref, pay = more
        total = table_of(pays, cl_rows, cl_pad)
        counts = cnt_ref[...]
    base = width - (blocks - 1) * LANES
    rows = k.shape[0]
    live = live_row(lengths, rows)
    inv_root = size ** (-0.5)
    carried, extras = [], []
    for h in range(heads):
        cnt = counts[:, base + h : base + h + 1]
        centre = jnp.where(
            cnt > 0, total[:, h * size : (h + 1) * size] / jnp.maximum(cnt, 1.0), 0.0
        ).astype(bf16)
        centre_ref[h] = centre
        scores = mt(centre, k[:, h * size : (h + 1) * size]) * inv_root
        peak = jnp.max(jnp.where(live, scores, negative), axis=1, keepdims=True)
        weighted = jnp.where(live, jnp.exp(jnp.where(live, scores - peak, 0.0)), 0.0)
        in_top = in_tops[h].astype(f32)
        mass = jnp.sum(weighted, axis=1, keepdims=True)
        top_mass = jnp.sum(weighted * in_top, axis=1, keepdims=True)
        rest = (weighted * (1.0 - in_top)).astype(bf16)
        carried.append(mm(rest, v[:, h * size : (h + 1) * size]))
        for value in (peak, mass, top_mass):
            extras.extend(parts3(value))
    spare = blocks * LANES - width
    block = jnp.concatenate(carried + [columns(spare, extras, cl_pad)], axis=1).astype(bf16)
    put_blocks(pay, 0, block, cl_rows)


def member_kernel(start, count, heads, size, lengths, *refs):
    pays = refs[:count]
    q, chosen_ref, hub_ref, prob_ref, top_ref = refs[count:]
    width = heads * size
    hub = total_of(pays, start, HUBS, 2 * width // LANES).astype(bf16)
    hub_ref[...] = hub
    inv_root = size ** (-0.5)
    probs, outs = [], []
    for h in range(heads):
        keys = hub[:, h * size : (h + 1) * size]
        values = hub[:, width + h * size : width + (h + 1) * size]
        logits = mt(q[:, h * size : (h + 1) * size], keys) * inv_root
        chosen = chosen_ref[:, h * HUBS : (h + 1) * HUBS].astype(f32) > 0.5
        logits = jnp.where(chosen, logits, negative)
        exponent = jnp.where(
            chosen, jnp.exp(logits - jnp.max(logits, axis=1, keepdims=True)), 0.0
        )
        prob = exponent / jnp.sum(exponent, axis=1, keepdims=True)
        probs.append(prob)
        outs.append(mm(prob.astype(bf16), values))
    prob_ref[...] = jnp.concatenate(probs, axis=1)
    top_ref[...] = jnp.concatenate(outs, axis=1)


def combine_kernel(layer, count, heads, size, cl_rows, lengths, *refs):
    pays = refs[:count]
    top_out, members, mine, other, att_ref, top, low, stat_ref, w_out, sems = refs[count:]
    weights = Choice(layer, [(mine, other)], [w_out], [sems.at[0]])
    width = heads * size
    cl_pad = members.shape[2]
    blocks = round_up(width + 1, LANES) // LANES
    tables = [
        pad_rows(get_blocks(ref[...].astype(f32), 0, cl_rows, blocks), cl_pad) for ref in pays
    ]
    base = width - (blocks - 1) * LANES
    shift = lambda block, by: pltpu.roll(block, by % LANES, 1)
    stats = []
    for one in tables:
        block = one[:, (blocks - 1) * LANES :]
        stats.append(block + shift(block, -1) + shift(block, -2))
    peaks = functools.reduce(jnp.maximum, stats)
    scales = [jnp.exp(mine - peaks) for mine in stats]
    masses = sum(mine * shift(scale, 3) for mine, scale in zip(stats, scales))
    top_masses = sum(mine * shift(scale, 6) for mine, scale in zip(stats, scales))
    rows = top_out.shape[0]
    live = live_col(lengths, rows)
    pieces = []
    for h in range(heads):
        at = base + 9 * h
        peak, mass, top_mass = (
            every[:, at + 3 * which : at + 3 * which + 1]
            for which, every in enumerate((peaks, masses, top_masses))
        )
        carried = 0.0
        for one, scale in zip(tables, scales):
            carried = carried + one[:, h * size : (h + 1) * size] * scale[:, at : at + 1]
        safe = jnp.where(mass > 0, mass, 1.0)
        remote = carried / safe
        share = top_mass / safe
        lanes = LANES - size
        stat_ref[h] = jnp.concatenate(
            [carried, columns(lanes, (peak, safe, top_mass, share), cl_pad)], axis=1
        )
        looked = pick_rows(
            members[h], jnp.concatenate([remote, columns(lanes, (share,), cl_pad)], axis=1)
        )
        att = looked[:, size : size + 1] * top_out[:, h * size : (h + 1) * size] + looked[:, :size]
        pieces.append(jnp.where(live, att, 0.0))
    joined = jnp.concatenate(pieces, axis=1).astype(bf16)
    att_ref[...] = joined
    weights.wait(0)
    halves(mm(joined, w_out[...]), top, low)


def gelu_slope(hidden):
    root = (2.0 / 3.141592653589793) ** 0.5
    square = hidden * hidden
    bent = jnp.tanh(root * hidden * (1.0 + 0.044715 * square))
    slope = 0.5 * (1.0 + bent) + 0.5 * hidden * (1.0 - bent * bent) * root * (
        1.0 + 3 * 0.044715 * square
    )
    return (0.5 * hidden * (1.0 + bent)).astype(bf16), slope


def feed_kernel(lengths, *refs):
    source, *four = refs[:5]
    gain_mine, gain_other, in_mine, in_other, back_mine, back_other = refs[5:11]
    x1_ref, n2r, active_ref, slope_ref, top, low, w_in, w_back, sems = refs[11:]
    pairs = [(in_mine, in_other), (back_mine, back_other)]
    weights = Choice(0, pairs, [w_in, w_back], [sems.at[0], sems.at[1]])
    x1 = source[here(SECTION)].astype(f32) + summed(four)
    x1_ref[...] = x1
    hat, _ = layer_stats(x1)
    n2 = (hat * gain_row(gain_mine, gain_other, 0, 1)).astype(bf16)
    weights.wait(0)
    active, slope = gelu_slope(mm(n2, w_in[...]))
    active_ref[...] = active
    slope_ref[...] = slope
    weights.wait(1)
    halves(mm(active, w_back[...]), top, low)
    n2r[...] = n2


def turn_kernel(lengths, *refs):
    source, *four = refs[:5]
    gain_mine, gain_other, cot, in_mine, in_other, back_mine, back_other = refs[5:12]
    x1_ref, n2r, active_ref, dyb_ref, dz_ref, top, low, w_in, w_back, sems = refs[12:]
    pairs = [(in_mine, in_other), (back_mine, back_other)]
    weights = Choice(1, pairs, [w_in, w_back], [sems.at[0], sems.at[1]])
    x1 = source[...] + summed(four)
    x1_ref[...] = x1
    hat, _ = layer_stats(x1)
    n2 = (hat * gain_row(gain_mine, gain_other, 1, 1)).astype(bf16)
    n2r[...] = n2
    weights.wait(0)
    active, slope = gelu_slope(mm(n2, w_in[...]))
    active_ref[...] = active
    dyb = cot[here(SECTION)]
    dyb_ref[...] = dyb
    weights.wait(1)
    dz = (mt(dyb, w_back[...]) * slope).astype(bf16)
    dz_ref[...] = dz
    halves(mt(dz, w_in[...]), top, low)


def late_feed_kernel(layer, lengths, active, mine, other, top, low, w_back, sems):
    weights = Choice(layer, [(mine, other)], [w_back], [sems.at[0]])
    weights.wait(0)
    halves(mm(active[...], w_back[...]), top, low)


def feed_back_kernel(lengths, *refs):
    grad_middle, source, *four = refs[:6]
    gain = gain_row(*refs[6:8], 1, 0)
    slope, back_mine, back_other, in_mine, in_other = refs[8:13]
    dy_ref, gain_ref, dybr, dz_ref, top, low, w_back, w_in, sems = refs[13:]
    pairs = [(back_mine, back_other), (in_mine, in_other)]
    weights = Choice(0, pairs, [w_back, w_in], [sems.at[0], sems.at[1]])
    dy = input_grad(grad_middle, source[...], four, gain, gain_ref)
    dy_ref[...] = dy
    dyb = dy.astype(bf16)
    weights.wait(0)
    dz = (mt(dyb, w_back[...]) * slope[...]).astype(bf16)
    dz_ref[...] = dz
    weights.wait(1)
    halves(mt(dz, w_in[...]), top, low)
    dybr[...] = dyb


def input_grad(grad_middle, source, four, gain, gain_ref):
    grad_normed = summed(four)
    hat, inverse = layer_stats(source)
    if gain_ref is not None:
        gain_ref[...] = jnp.sum(grad_normed * hat, axis=0, keepdims=True)
    return grad_middle[...] + norm_back(grad_normed * gain, hat, inverse)


def input_grad_kernel(lengths, *refs):
    grad_middle, source, *four = refs[:6]
    *gains, gain_two, last_one, last_two, sent, keep, gain_one = refs[6:]
    source = source[here(SECTION)].astype(f32)
    rows = source.shape[0]
    sent[:rows, :] = input_grad(grad_middle, source, four, gain_row(*gains, 0, 0), gain_one)
    first = jnp.concatenate([gain_one[...], gain_two[...]], axis=0)
    last = jnp.concatenate([last_one[...], last_two[...]], axis=0)
    keep[...] = jnp.where(here(SECTION) == 0, first, last)
    give = jnp.where(here(SECTION) == 0, last, first)
    sent[rows:, :] = jnp.concatenate([give, jnp.zeros((6, give.shape[1]), f32)], axis=0)


def middle_back_kernel(layer, heads, size, cl_rows, lengths, *refs):
    four = refs[:4]
    middle, grad_out, gain_mine, gain_other, top_out, members_t = refs[4:10]
    mine, other, dx1_ref, dx1r, dtop_ref, gain_ref, pay, w_out, sems = refs[10:]
    weights = Choice(layer, [(mine, other)], [w_out], [sems.at[0]])
    grad_normed = summed(four)
    hat, inverse = layer_stats(middle[...])
    gain_ref[...] = jnp.sum(grad_normed * hat, axis=0, keepdims=True)
    grad = grad_out[here(SECTION)].astype(f32) if layer == 1 else grad_out[...]
    dx1 = grad + norm_back(
        grad_normed * gain_row(gain_mine, gain_other, layer, 1), hat, inverse
    )
    dx1_ref[...] = dx1
    dx1b = dx1.astype(bf16)
    rows = dx1.shape[0]
    weights.wait(0)
    datt = mt(dx1b, w_out[...])
    dtop = jnp.where(live_col(lengths, rows), datt, 0.0).astype(bf16)
    dtop_ref[...] = dtop
    sums, shares = [], []
    for h in range(heads):
        members = members_t[h]
        own = dtop[:, h * size : (h + 1) * size]
        sums.append(mm(members, own))
        product = own.astype(f32) * top_out[:, h * size : (h + 1) * size]
        both = mm(members, jnp.concatenate(parts2(product), axis=1))
        shares.extend(parts3(jnp.sum(both, axis=1, keepdims=True)))
    width = heads * size
    spare = round_up(width + 1, LANES) - width
    cl_pad = members_t.shape[1]
    block = jnp.concatenate(sums + [columns(spare, shares, cl_pad)], axis=1).astype(bf16)
    put_blocks(pay, 0, block, cl_rows)
    dx1r[...] = dx1b


def member_back_kernel(heads, size, lengths, *refs):
    q, hub_ref, prob_ref, dtop, stat, members, dq_ref, pay = refs
    width = heads * size
    inv_root = size ** (-0.5)
    hub = hub_ref[...]
    dqs, dks, dvs = [], [], []
    for h in range(heads):
        keys = hub[:, h * size : (h + 1) * size]
        values = hub[:, width + h * size : width + (h + 1) * size]
        prob = prob_ref[:, h * HUBS : (h + 1) * HUBS]
        own = dtop[:, h * size : (h + 1) * size]
        share = pick_rows(members[h], stat[h])[:, size + 3 : size + 4]
        da = mt(own, values) * share
        dg = (prob * (da - jnp.sum(prob * da, axis=1, keepdims=True))).astype(bf16)
        dqs.append(mm(dg, keys) * inv_root)
        dks.append(tm(dg, q[:, h * size : (h + 1) * size]) * inv_root)
        scaled = own.astype(f32) * share
        dvs.append(tm(prob.astype(bf16), scaled.astype(bf16)))
    dq_ref[...] = jnp.concatenate(dqs, axis=1)
    put_blocks(pay, 0, jnp.concatenate(dks + dvs, axis=1).astype(bf16), HUBS)


def centroid_back_kernel(layer, count, heads, size, cl_rows, lengths, *refs):
    pays = refs[:count]
    centre_ref, stat, k, v, in_tops, hub_pay, pay, dk_ref, dv_ref = refs[count:]
    width = heads * size
    cl_pad = in_tops.shape[1]
    blocks = round_up(width + 1, LANES) // LANES
    total = pad_rows(total_of(pays, 0, cl_rows, blocks), cl_pad)
    rows = k.shape[0]
    live = live_row(lengths, rows)
    inv_root = size ** (-0.5)
    dcs, dks, dvs = [], [], []
    for h in range(heads):
        keys = k[:, h * size : (h + 1) * size]
        values = v[:, h * size : (h + 1) * size]
        centre = centre_ref[h]
        grad_remote = total[:, h * size : (h + 1) * size]
        at = width + 3 * h
        grad_share = total[:, at : at + 1] + total[:, at + 1 : at + 2] + total[:, at + 2 : at + 3]
        carried = stat[h][:, :size]
        peak = stat[h][:, size : size + 1]
        mass = stat[h][:, size + 1 : size + 2]
        top_mass = stat[h][:, size + 2 : size + 3]
        grad_carried = (grad_remote / mass).astype(bf16)
        grad_top = grad_share / mass
        grad_mass = -(
            jnp.sum(grad_remote * carried, axis=1, keepdims=True) + grad_share * top_mass
        ) / (mass * mass)
        scores = mt(centre, keys) * inv_root
        weighted = jnp.where(live, jnp.exp(jnp.where(live, scores - peak, 0.0)), 0.0)
        in_top = in_tops[h].astype(f32)
        rest = (weighted * (1.0 - in_top)).astype(bf16)
        grad_weighted = (
            (1.0 - in_top) * mt(grad_carried, values) + in_top * grad_top + grad_mass
        )
        grad_scores = (grad_weighted * weighted).astype(bf16)
        dcs.append(mm(grad_scores, keys) * inv_root)
        dks.append(tm(grad_scores, centre) * inv_root)
        dvs.append(tm(rest, grad_carried))
    if layer == 0:
        put_table(pay, jnp.concatenate(dcs, axis=1).astype(bf16), cl_rows)
        pay[cl_rows + cl_pad // 2 :, :] = hub_pay[...]
    else:
        spare = blocks * LANES - width
        block = jnp.concatenate(dcs + [jnp.zeros((cl_pad, spare), f32)], axis=1).astype(bf16)
        put_blocks(pay, 0, block, cl_rows)
        pay[blocks * cl_rows :, :] = hub_pay[...]
    dk_ref[...] = jnp.concatenate(dks, axis=1)
    dv_ref[...] = jnp.concatenate(dvs, axis=1)


def project_back_kernel(layer, count, heads, size, cl_rows, lengths, *refs):
    pays = refs[:count]
    dq_top, dk_c, dv_c, cnt_ref, members, own_pick, mine, other = refs[count : count + 8]
    dqkv_ref, top, low, w_qkv, sems = refs[count + 8 :]
    weights = Choice(layer, [(mine, other)], [w_qkv], [sems.at[0]])
    width = heads * size
    cl_pad = members.shape[2]
    blocks = round_up(width + 1, LANES) // LANES
    if layer == 0:
        total = table_of(pays, cl_rows, cl_pad)
        start = cl_rows + cl_pad // 2
    else:
        total = pad_rows(total_of(pays, 0, cl_rows, blocks), cl_pad)
        start = blocks * cl_rows
    hub = total_of(pays, start, HUBS, 2 * width // LANES)
    high, low_part = parts2(hub)
    spread = tm(own_pick[...], high) + tm(own_pick[...], low_part)
    rows = dq_top.shape[0]
    live = live_col(lengths, rows)
    base = round_up(width + 1, LANES) - LANES
    dqs = []
    for h in range(heads):
        at = width - base + h
        cnt = jnp.maximum(cnt_ref[:, at : at + 1], 1.0)
        from_centre = pick_rows(members[h], total[:, h * size : (h + 1) * size] / cnt)
        dqs.append(jnp.where(live, from_centre, 0.0))
    dq = (dq_top[...] + jnp.concatenate(dqs, axis=1)).astype(bf16)
    dk = (dk_c[...] + spread[:, :width]).astype(bf16)
    dv = (dv_c[...] + spread[:, width:]).astype(bf16)
    dqkv_ref[...] = jnp.concatenate([dq, dk, dv], axis=1)
    weights.wait(0)
    halves(mm(dq, w_qkv[0]) + mm(dk, w_qkv[1]) + mm(dv, w_qkv[2]), top, low)


def feed_grads_kernel(lengths, dyb, active, n2, dz, keep, give):
    back = tm(dyb[...], active[...]).astype(bf16)
    into = tm(n2[...], dz[...]).astype(bf16)

    @pl.when(here(SECTION) == 0)
    def _():
        keep[...] = back
        give[...] = into

    @pl.when(here(SECTION) == 1)
    def _():
        keep[...] = into
        give[...] = back


def attention_grads_kernel(count, lengths, n1, dqkv, dx1b, att, keep, give):
    part = n1.shape[1] // count
    half = part // 2
    both = jnp.concatenate([tm(n1[...], dqkv[...]), tm(dx1b[...], att[...])], axis=1).astype(bf16)

    def put(ref, first):
        for at in range(count):
            ref[at] = both[at * part + first : at * part + first + half]

    @pl.when(here(SECTION) == 0)
    def _():
        put(keep, 0)
        put(give, half)

    @pl.when(here(SECTION) == 1)
    def _():
        put(keep, half)
        put(give, 0)


def chip_sum_kernel(lengths, mine, far, keep, give):
    me = here(SEQ)
    for at in range(keep.shape[0]):
        stay, go = 2 * at + me % 2, 2 * at + 1 - me % 2
        keep[at] = (mine[stay].astype(f32) + far[stay].astype(f32)).astype(bf16)
        give[at] = (mine[go].astype(f32) + far[go].astype(f32)).astype(bf16)


def pair_sum_kernel(lengths, mine, far, keep, give):
    stay = here(SEQ) // 2
    go = 1 - stay
    keep[...] = (mine[stay].astype(f32) + far[stay].astype(f32)).astype(bf16)
    give[...] = (mine[go].astype(f32) + far[go].astype(f32)).astype(bf16)


def sorted_sum_kernel(lengths, mine, far, *outs):
    for k, out in enumerate(outs):
        at = lax.rem(here(SEQ) + k, len(outs))
        out[...] = (mine[at].astype(f32) + far[at].astype(f32)).astype(bf16)


def seq_sum_kernel(lengths, *refs):
    total = refs[0][...].astype(f32)
    for ref in refs[1:-1]:
        total = total + ref[...].astype(f32)
    refs[-1][...] = total


def ship_kernel(sums, lengths, *refs):
    row = 0
    out = refs[-1]
    for at in range(sums):
        mine, far = refs[2 * at : 2 * at + 2]
        out[row : row + mine.shape[0], :] = mine[...].astype(f32) + far[...].astype(f32)
        row += mine.shape[0]
    grad, source, *four = refs[2 * sums : -1]
    out[row : row + grad.shape[0], :] = grad[...]
    row += grad.shape[0]
    out[row:, :] = source[...] + summed(four)


def feed_owner_kernel(lengths, first, first_far, shipped, shipped_far, back, into, own, far):
    rows = first.shape[0]
    own[...] = shipped[rows : rows + own.shape[0], :]
    far[...] = shipped_far[rows : rows + far.shape[0], :]

    @pl.when(here(SECTION) == 0)
    def _():
        back[...] = first[...]
        into[...] = first_far[...]

    @pl.when(here(SECTION) == 1)
    def _():
        into[...] = shipped[:rows, :]
        back[...] = shipped_far[:rows, :]


def attention_owner_kernel(width, lengths, first, first_far, last, last_far, grad_qkv, grad_out):
    def put(low_half, high_half):
        both = jnp.concatenate([low_half, high_half], axis=0)
        for at in range(3):
            grad_qkv[at] = both[:, at * width : (at + 1) * width]
        grad_out[...] = both[:, 3 * width :].T

    @pl.when(here(SECTION) == 0)
    def _():
        put(first[...], first_far[...])

    @pl.when(here(SECTION) == 1)
    def _():
        put(last_far[...], last[...])


def place_kernel(start, lengths, own_first, far_first, shipped, shipped_far, out, token):
    rows = out.shape[1]
    token[...] = jnp.zeros_like(token)

    @pl.when(here(SECTION) == 0)
    def _():
        out[0] = own_first[:rows, :]
        out[1] = far_first[:rows, :]

    @pl.when(here(SECTION) == 1)
    def _():
        out[0] = shipped_far[start : start + rows, :]
        out[1] = shipped[start : start + rows, :]


def gain_kernel(lengths, keep, sent_far, out):
    rows = sent_far.shape[0] - 8
    out[...] = keep[...] + sent_far[rows : rows + 2, :]


def moved(block, axis, target):
    devices = range(lax.axis_size(axis))
    return lax.ppermute(block, axis, [(i, target(i)) for i in devices])


def swap(block):
    return moved(block, SECTION, lambda i: i ^ 1)


def every_seq(block):
    count = lax.axis_size(SEQ)
    if count > DIRECT:
        gathered = lax.all_gather(block, SEQ)
        return [gathered[at] for at in range(count)]
    return [block] + [
        moved(block, SEQ, lambda i, k=k: (i + k) % count) for k in range(1, count)
    ]


def every_head(block):
    return [block] + [
        moved(block, HEAD, lambda i, k=k: i ^ k) for k in range(1, lax.axis_size(HEAD))
    ]


def every_head_in_turn(block):
    pieces = [block]
    distance = 1
    while distance < lax.axis_size(HEAD):
        pieces += [moved(piece, HEAD, lambda i: i ^ distance) for piece in pieces]
        distance *= 2
    return pieces


def fold_kernel(lengths, top_a, top_b, low_a, low_b, top, low):
    top[...] = (top_a[...].astype(f32) + top_b[...].astype(f32)).astype(bf16)
    low[...] = (low_a[...].astype(f32) + low_b[...].astype(f32)).astype(bf16)


def head_sum(top, low, run, before_fold=None):
    distances = [1 << at for at in range(lax.axis_size(HEAD).bit_length() - 1)]
    for step in range(len(distances)):
        one = distances[step]
        other = distances[len(distances) - 1 - step]
        far_top = moved(top, HEAD, lambda i: i ^ one)
        far_low = moved(low, HEAD, lambda i: i ^ other)
        if step < len(distances) - 1:
            ties = before_fold() if before_fold and step == 0 else []
            shape = [shaped(top.shape, bf16)] * 2
            top, low = run(
                fold_kernel, shape, [top, far_top, low, far_low], ties=ties
            )
    return (top, far_top, low, far_low)


def to_core(block, layer):
    return lax.ppermute(block, SECTION, [(1 - layer, layer)])


def seq_xor(block, distance):
    return moved(block, SEQ, lambda i: i ^ distance)


def pair_step(keep, far, run, ties=()):
    half = shaped((keep.shape[0] // 2,) + keep.shape[1:], bf16)
    keep, give = run(chip_sum_kernel, [half] * 2, [keep, far], ties=ties)
    return keep, seq_xor(give, 1)


def far_step(keep, far, run, ties=()):
    keep, give = run(
        pair_sum_kernel, [shaped(keep.shape[1:], bf16)] * 2, [keep, far], ties=ties
    )
    return keep, seq_xor(give, 2)


def shards(tokens, cotangent, lengths, clusters, top_index, w_qkv, w_out, w_in, w_back, gains):
    section = lax.axis_index(SECTION)
    me = lax.axis_index(SEQ)
    count = lax.axis_size(SEQ)
    head_devices = lax.axis_size(HEAD)
    micro, rows, dim = tokens.shape
    _, heads, cluster_count, slots = top_index.shape
    size = w_qkv.shape[3] // heads
    width = heads * size
    hidden = w_in.shape[2]
    total_rows = rows * count
    cl_pad = round_up(cluster_count, LANES)
    cl_rows = round_up(cluster_count, 16)
    high_rows = round_up(max(total_rows // LANES, 1), 16)
    blocks = round_up(width + 1, LANES) // LANES
    hub_blocks = 2 * width // LANES
    sizes = (heads, size, cl_rows)
    run = lambda kernel, outs, args, **kw: call(kernel, outs, lengths, args, **kw)
    part = functools.partial
    fours = [shaped((rows // 2, dim), bf16)] * 2
    assert width == LANES + LANES // 2
    packed_shape = shaped((cl_rows + cl_pad // 2 + hub_blocks * HUBS, LANES), bf16)
    pay_shape = shaped((blocks * cl_rows, LANES), bf16)
    table_shape = shaped((heads, cl_pad, rows), bf16)
    square = shaped((dim, hidden), bf16)
    qkv_buf = shaped((3, width, dim), bf16)

    qkv_t = w_qkv[0].transpose(0, 2, 1)
    qkv_pair = (qkv_t, swap(qkv_t))
    gain_pair = (gains[0], swap(gains[0]))
    tops = top_index.transpose(0, 1, 3, 2)
    clusters = clusters.transpose(1, 0, 2)
    out_pair = (w_out[0], swap(w_out[0]))
    in_pair = (w_in[0], swap(w_in[0]))
    back_pair = (w_back[0], swap(w_back[0]))
    own_pick, hubs, members_t = run(
        part(rank_kernel, heads, cl_pad),
        [shaped((HUBS, rows), bf16), shaped((high_rows, LANES)), table_shape],
        [tops, clusters],
    )

    source, lists = tokens, None
    kept, acts = [], []
    for layer in range(2):
        outs = [
            shaped((rows, dim), bf16),
            shaped((rows, width), bf16),
            shaped((rows, width), bf16),
            shaped((rows, width), bf16),
            packed_shape if layer else shaped((blocks * cl_rows + hub_blocks * HUBS, LANES), bf16),
        ]
        if layer:
            outs = [shaped((rows, dim))] + outs
        found = run(
            part(project_kernel, layer, *sizes),
            outs,
            ([tokens] if layer == 0 else [x1, *four])
            + [*gain_pair, members_t, own_pick],
            anys=qkv_pair,
            bufs=[qkv_buf],
        )
        if layer:
            source, *found = found
            acts.append(source)
            acts_far = to_core(source, 0)
        n1r, q, k, v, pay = found
        pays = every_seq(pay)
        if lists is None:
            in_tops, chosen, members = lists = run(
                part(list_kernel, heads, cl_pad),
                [
                    table_shape,
                    shaped((rows, heads * HUBS), bf16),
                    shaped((heads, rows, cl_pad), bf16),
                ],
                [tops, clusters, hubs, own_pick],
            )
        centre_shape, cnt_shape = shaped((heads, cl_pad, size), bf16), shaped((cl_pad, LANES))
        centroid = part(centroid_kernel, layer, len(pays), *sizes)
        if layer == 0:
            centre, cnt, pay = run(
                centroid, [centre_shape, cnt_shape, pay_shape], [*pays, k, v, in_tops]
            )
        else:
            centre, pay = run(centroid, [centre_shape, pay_shape], [*pays, k, v, in_tops, cnt])
        stats = every_seq(pay)
        hub, prob, top_out = run(
            part(
                member_kernel,
                cl_rows + cl_pad // 2 if layer else blocks * cl_rows,
                len(pays),
                heads,
                size,
            ),
            [
                shaped((HUBS, 2 * width), bf16),
                shaped((rows, heads * HUBS)),
                shaped((rows, width)),
            ],
            [*pays, q, chosen],
            ties=[in_pair[1]] if layer == 0 else [],
        )
        att, top, low, stat = run(
            part(combine_kernel, layer, len(stats), *sizes),
            [shaped((rows, width), bf16)] + fours + [shaped((heads, cl_pad, LANES))],
            [*stats, top_out, members],
            anys=out_pair,
            bufs=[shaped((width, dim), bf16)],
        )
        four = head_sum(top, low, run)
        by_token = [shaped((rows, dim)), shaped((rows, dim), bf16), shaped((rows, hidden), bf16)]
        if layer == 0:
            x1, n2r, active, slope, *parts = run(
                feed_kernel,
                by_token + [shaped((rows, hidden))] + fours,
                [source, *four, *gain_pair],
                anys=[*in_pair, *back_pair],
                bufs=[square, square],
            )
            four = head_sum(*parts, run)
        else:
            slope = None
            x1, n2r, active, dyb, dz, *parts = run(
                turn_kernel,
                by_token + [shaped((rows, dim), bf16), shaped((rows, hidden), bf16)] + fours,
                [source, *four, *gain_pair, cotangent],
                ties=[acts_far],
                anys=[*in_pair, *back_pair],
                bufs=[square, square],
            )
        kept.append(
            (source, n1r, q, k, v, centre, cnt, hub, prob, top_out, att, stat, x1, n2r, active, slope)
        )

    direct = count == DIRECT
    seq_part = dim // count
    half = seq_part // 2
    extra = 16
    if not direct:
        seq_part = half = None

    def plain_sum(grad, layer):
        total = grad.astype(f32) + to_core(grad.astype(bf16), layer).astype(f32)
        return lax.psum_scatter(
            total.astype(bf16), SEQ, scatter_dimension=0, tiled=True
        ).astype(f32)

    def feed_grads(layer, dyb, dz, ties=()):
        active, n2 = kept[layer][14], kept[layer][13]
        if not direct:
            return plain_sum(tm(dyb, active), layer), plain_sum(tm(n2, dz), layer)
        return run(
            feed_grads_kernel, [square] * 2, [dyb, active, n2, dz], ties=ties
        )

    def attention_grads(layer, dqkv, dx1b):
        n1, att = kept[layer][1], kept[layer][10]
        if not direct:
            return plain_sum(jnp.concatenate([tm(n1, dqkv), tm(dx1b, att)], axis=1), layer)
        return run(
            part(attention_grads_kernel, count),
            [shaped((count, half, 4 * width), bf16)] * 2,
            [n1, dqkv, dx1b, att],
        )

    def swapped(made):
        far = swap(made[1])
        shape = (count, -1, made[0].shape[-1])
        return made[0].reshape(shape), far.reshape(shape)

    def middle_back(layer, four, dy, ties):
        top_out, x1 = kept[layer][9], kept[layer][12]
        return run(
            part(middle_back_kernel, layer, *sizes),
            [
                shaped((rows, dim)),
                shaped((rows, dim), bf16),
                shaped((rows, width), bf16),
                shaped((1, dim)),
                pay_shape,
            ],
            [*four, x1, dy, *gain_pair, top_out, members_t],
            anys=out_pair,
            bufs=[shaped((width, dim), bf16)],
            ties=ties,
        )

    def member_back(layer, dtop, ties=()):
        _, _, q, _, _, _, _, hub, prob, _, _, stat = kept[layer][:12]
        return run(
            part(member_back_kernel, heads, size),
            [shaped((rows, width)), shaped((hub_blocks * HUBS, LANES), bf16)],
            [q, hub, prob, dtop, stat, members],
            ties=ties,
        )

    def centroid_back(layer, pays, hub_pay, ties):
        _, _, _, k, v, centre, _, _, _, _, _, stat = kept[layer][:12]
        return run(
            part(centroid_back_kernel, layer, len(pays), *sizes),
            [
                shaped((blocks * cl_rows + hub_blocks * HUBS, LANES), bf16)
                if layer
                else packed_shape,
                shaped((rows, width)),
                shaped((rows, width)),
            ],
            [*pays, centre, stat, k, v, in_tops, hub_pay],
            ties=ties,
        )

    def project_back(layer, pays, dq_top, dk, dv, ties):
        cnt = kept[layer][6]
        return run(
            part(project_back_kernel, layer, len(pays), *sizes),
            [shaped((rows, 3 * width), bf16)] + fours,
            [*pays, dq_top, dk, dv, cnt, members, own_pick],
            anys=qkv_pair,
            bufs=[qkv_buf],
            ties=ties,
        )

    def shared(pay):
        return every_seq(pay)

    def step(parts, axis, one, other):
        return [parts[0], moved(parts[0], axis, lambda i: i ^ one),
                    parts[1], moved(parts[1], axis, lambda i: i ^ other)]

    def fold(four, ties):
        return run(fold_kernel, fours, four, ties=ties)

    def ended(group, layer, ties):
        (total,) = run(seq_sum_kernel, [shaped(group[0].shape)], group, ties=ties)
        return [total, to_core(total, layer)]

    near, away = 1, head_devices // 2
    assert head_devices == 4
    only = lambda items: list(items) if direct else []

    backs = [shaped((rows, dim), bf16), shaped((rows, hidden), bf16)] + fours
    four = step(parts, HEAD, near, away)
    parts = fold(four, [])
    four = step(parts, HEAD, away, near)
    dx1, dx1b, dtop, gain_two, pay = middle_back(1, four, cotangent, [])
    feed_last = feed_grads(1, dyb, dz, parts)
    pays = shared(pay)
    dq_top, hub_pay = member_back(1, dtop)
    pay, dk, dv = centroid_back(1, pays, hub_pay, only(feed_last))
    if direct:
        feed_last = swapped(feed_last)
    late_parts = run(
        part(late_feed_kernel, 1),
        fours,
        [kept[1][14]],
        anys=back_pair,
        bufs=[square],
        ties=pays[1:] + [hub_pay],
    )
    late = step(late_parts, HEAD, near, away)
    pays = shared(pay)
    if direct:
        feed_last = pair_step(*feed_last, run, pays[1:])
    dqkv, *parts = project_back(
        1, pays, dq_top, dk, dv, [late[1], late[3]] + only(feed_last[:1])
    )
    four = step(parts, HEAD, near, away)
    parts = fold(four, [])
    four = step(parts, HEAD, away, near)
    attention_last = attention_grads(1, dqkv, dx1b)
    if direct:
        feed_last = far_step(*feed_last, run)
        attention_last = swapped(attention_last)
        attention_last = pair_step(*attention_last, run)
    dy, gain_one, dyb, dz, *parts = run(
        feed_back_kernel,
        [shaped((rows, dim)), shaped((1, dim))] + backs,
        [dx1, kept[1][0], *four, *gain_pair, kept[0][15]],
        anys=[*back_pair, *in_pair],
        bufs=[square, square],
        ties=only([feed_last[0], attention_last[0]]),
    )
    last_grad, last_gains = dy, [gain_one, gain_two]
    four = step(parts, HEAD, near, away)
    parts = fold(four, only([attention_last[1], feed_last[1]]))
    if direct:
        attention_last = far_step(*attention_last, run, parts)
    four = step(parts, HEAD, away, near)
    feed_first = feed_grads(0, dyb, dz, parts)
    dx1, dx1b, dtop, gain_two, pay = middle_back(
        0, four, dy, only(feed_first)
    )
    pays = shared(pay)
    dq_top, hub_pay = member_back(0, dtop)
    if direct:
        feed_first = swapped(feed_first)
    pay, dk, dv = centroid_back(
        0, pays, hub_pay, only([feed_first[1], attention_last[1]])
    )
    late_parts = fold(late, [dk])
    late = step(late_parts, HEAD, away, near)
    pays = shared(pay)
    if direct:
        feed_first = pair_step(*feed_first, run, pays[1:])
    dqkv, *parts = project_back(
        0, pays, dq_top, dk, dv, [late[1], late[3]] + only(feed_first[:1])
    )
    four = step(parts, HEAD, near, away)
    attention_first = attention_grads(0, dqkv, dx1b)
    before = []
    if direct:
        attention_first = swapped(attention_first)
        attention_first = pair_step(*attention_first, run)
        feed_first = far_step(*feed_first, run)
        before = [attention_first[0], feed_first[0]]
    parts = fold(four, before)
    four = step(parts, HEAD, away, near)
    sums = [*feed_last, *attention_last] if direct else []
    sum_rows = (seq_part + half) if direct else 0
    (shipped,) = run(
        part(ship_kernel, len(sums) // 2),
        [shaped((sum_rows + 2 * rows, dim))],
        [*sums, last_grad, kept[1][12], *late],
        ties=parts,
    )
    shipped = [shipped, to_core(shipped, 1)]
    if direct:
        attention_first = far_step(*attention_first, run, parts)
    sent, own_gains, _ = run(
        input_grad_kernel,
        [shaped((rows + 8, dim)), shaped((2, dim)), shaped((1, dim))],
        [dx1, tokens, *four, *gain_pair, gain_two, *last_gains],
        ties=only(attention_first[:1]) + shipped,
    )
    sent_far = swap(sent)
    token = shaped((8, LANES))
    (placed_acts, acts_token), (placed_grads, grads_token) = (
        run(part(place_kernel, start), [shaped((2, rows, dim)), token], [*first, *shipped])
        for start, first in (
            (sum_rows + rows, (acts[0], acts_far)),
            (sum_rows, (sent, sent_far)),
        )
    )
    (gain_sum,) = run(gain_kernel, [shaped((2, dim))], [own_gains, sent_far])
    if direct:
        gain_near = seq_xor(gain_sum, 1)
        gain_sum = gain_sum + gain_near
        gain_far = seq_xor(gain_sum, 2)
        gain_sum = gain_sum + gain_far
        gain_sum = lax.dynamic_slice_in_dim(gain_sum, me * seq_part, seq_part, 1)
        feed_first = ended(feed_first, 0, [acts_token])
        halves_shape = [shaped((half, 4 * width))] * 2
        back, into, *attention_last = run(
            feed_owner_kernel,
            [shaped((seq_part, hidden))] * 2 + halves_shape,
            [*feed_first, *shipped],
        )
        attention_first = ended(
            attention_first, 0, [attention_last[0], grads_token, gain_far]
        )
        grad_qkv, grad_out = run(
            part(attention_owner_kernel, width),
            [shaped((3, seq_part, width)), shaped((width, seq_part))],
            [*attention_first, *attention_last],
        )
    else:
        pick = lambda one, two: jnp.where(section == 0, one, two)
        gain_sum = lax.psum_scatter(gain_sum, SEQ, scatter_dimension=1, tiled=True)
        back, into = (pick(feed_first[at], feed_last[at]) for at in range(2))
        both = pick(attention_first, attention_last)
        grad_qkv = both[:, : 3 * width].reshape(-1, 3, width).transpose(1, 0, 2)
        grad_out = both[:, 3 * width :].T
    return (
        placed_acts[None],
        placed_grads[None],
        grad_qkv[None],
        grad_out[None],
        into[None],
        back.T[None],
        gain_sum[None],
    )


def solution(mesh):
    placed = (
        P(None, SEQ, None),
        P(None, SEQ, None),
        P(),
        P(None, HEAD, SEQ),
        P(None, HEAD, None, None),
        P(SECTION, None, None, HEAD),
        P(SECTION, HEAD, None),
        P(SECTION, None, HEAD),
        P(SECTION, HEAD, None),
        P(SECTION, None, None),
    )
    return jax.shard_map(
        shards,
        mesh=mesh,
        in_specs=placed,
        out_specs=(
            P(SECTION, None, SEQ, None),
            P(SECTION, None, SEQ, None),
            P(SECTION, None, SEQ, HEAD),
            P(SECTION, HEAD, SEQ),
            P(SECTION, SEQ, HEAD),
            P(SECTION, HEAD, SEQ),
            P(SECTION, None, SEQ),
        ),
        check_vma=False,
    )
```
